32 devices in a mesh: seq: 4 (over y, x), exp: 8 (over z, core).
Axes of the slice: x: 2, y: 2, z: 4, core: 2. Of those that a mesh axis runs over, the one named last changes fastest.
Arguments:
- residual: bfloat16 [512, 2, 3072], P(('seq', 'exp')), may hold values from -6 to 6
- queries: bfloat16 [2, 512, 4096], P(None, 'seq', 'exp'), may hold values from -6 to 6
- key_vecs: bfloat16 [2, 512, 4096], P(None, 'seq', 'exp'), may hold values from -0.52734375 to 0.52734375
- value_vecs: bfloat16 [2, 512, 4096], P(None, 'seq', 'exp'), may hold values from -6 to 6
- log_decay: float32 [2, 32, 512], P(None, 'exp', 'seq'), may hold values from -2 to 0
- head_gain: float32 [4096], P('exp'), may hold values from 0.1 to 1.9
- out_proj: bfloat16 [4096, 3072], P('exp'), may hold values from -0.09375 to 0.09375
- norm_gain: float32 [3072], replicated, may hold values from 0.1 to 1.9
- routes: int32 [512, 2, 2], replicated, may hold values from 0 to 7, all different within a row; in each aligned block of 256 rows (0 to 255, 256 to 511, ..., all dimensions but the last counted through in order) at most 128 rows name the same one
- route_weight: float32 [512, 2, 2], replicated, may hold values from 0.1 to 1
- w_gate: bfloat16 [8, 4608, 3072], P('exp', 'seq'), may hold values from -0.109375 to 0.109375
- w_up: bfloat16 [8, 4608, 3072], P('exp', 'seq'), may hold values from -0.109375 to 0.109375
Outputs:
- attn_out: float32 [512, 2, 3072], P(('seq', 'exp'))
- expert_hidden: float32 [8, 4608, 512], P('exp', 'seq')
The draws below stay inside these ranges and needn't reach their ends.
Inputs may be any that keep to these rules, and one draw needn't show every extreme that they name: Each aligned block of 256 rows of routes (positions c * 128 .. (c + 1) * 128 - 1 of both sequences) names one expert at most 128 times, a bound that some block reaches; the 2 entries of a row differ.
All inputs are finite; a program needn't handle non-finite values.
Results may differ from the reference program's by a relative error of at most 0.0052.
Values may be sent and summed in bfloat16 or wider, within the bound.
No kernel may reach another device: no remote copies, remote signals or barrier semaphores. Data moves between devices by JAX's collectives and lax.ppermute only.
A program may use at most 64 MiB of HBM per device.

```python
import math
import jax
import jax.numpy as jnp
import numpy as np
from jax import lax

D = 3072
ATTN_GROUPS = 32
HS = 128
FF = 4608
TOPK = 2
BATCH_SIZE = 2
LC = 128
TOKEN_SPAN = 512
EXPERTS = 8
RCAP = 128


def draw_log_decay(key, part):
    whole_tuple = jax.random.split(key, 7)
    head_shape = (1, ATTN_GROUPS, 1)
    fast_flag = jax.random.randint(whole_tuple[0], head_shape, 0, 2) == 0
    slow_rate = jnp.exp(jax.random.uniform(whole_tuple[1], head_shape, minval=jnp.log(0.05), maxval=jnp.log(0.4))) / TOKEN_SPAN
    fast_rate = jnp.exp(jax.random.uniform(whole_tuple[2], head_shape, minval=jnp.log(1.0 / 50.0), maxval=jnp.log(1.0 / 30.0)))
    nominal_speed = jnp.where(fast_flag, fast_rate, slow_rate)
    processor_factor = jnp.exp(jax.random.uniform(whole_tuple[3], (BATCH_SIZE, ATTN_GROUPS, TOKEN_SPAN // LC), minval=jnp.log(0.6), maxval=jnp.log(1.7)))
    processor_factor = jnp.repeat(processor_factor, LC, axis=2)
    locus_scaling = jax.random.uniform(whole_tuple[4], (BATCH_SIZE, ATTN_GROUPS, TOKEN_SPAN), minval=0.5, maxval=1.5)
    spike_location = jax.random.randint(whole_tuple[5], (BATCH_SIZE, ATTN_GROUPS, 2), 0, TOKEN_SPAN)
    spike_slowdown = jax.random.uniform(whole_tuple[6], (BATCH_SIZE, ATTN_GROUPS, 2), minval=0.2, maxval=0.5)
    location_array = jnp.arange(TOKEN_SPAN, dtype=jnp.int32)
    spike_occurrences = jnp.sum(jnp.where(location_array[None, None, None, :] == spike_location[..., None], jnp.log(1.0 - spike_slowdown)[..., None], 0.0), axis=2)
    return (-nominal_speed * processor_factor * locus_scaling + spike_occurrences).astype(jnp.float32)


def steps_of(key, shape, cuts, smallest, largest):
    gain = 1.0
    for position, shards_of in cuts:
        heights = jax.random.uniform(jax.random.fold_in(jax.random.fold_in(key, 6), position), (shards_of,), jnp.float32, smallest / len(cuts), largest / len(cuts))
        gain = gain * jnp.repeat(jnp.exp(heights), shape[position] // shards_of).reshape((-1,) + (1,) * (len(shape) - 1 - position))
    return gain


def routed_block(key, own, number, rows, number_of, top, most, slope):
    sequence = jax.random.permutation(key, number_of)
    heavy_load, ordinary = portions_of(number_of, rows * top, most, slope, True), portions_of(number_of, rows * top, most, slope, False)
    places = jnp.arange(number_of)

    def named(tallies, turn):
        used = int((tallies > 0).sum())
        fixed = max(1, used // 4)
        moved = fixed + (places - fixed + turn * (used - fixed)) % max(1, number_of - fixed)
        return jnp.zeros((number_of,), jnp.int32).at[sequence[jnp.where(places < fixed, places, moved)]].set(jnp.asarray(tallies, jnp.int32))

    tallies = jnp.where(number % 4 == 0, named(heavy_load, number // 4), named(ordinary, number - number // 4 - 1))
    mixed = jax.random.permutation(jax.random.fold_in(own, 3), number_of)
    donor, taker = mixed[0:number_of // 2 * 2:2], mixed[1:number_of // 2 * 2:2]
    margin = jnp.minimum(tallies[donor] - 1, most - tallies[taker]) // 2
    margin = jnp.where((donor == sequence[0]) | (taker == sequence[0]) | (tallies[taker] == 0), 0, jnp.maximum(margin, 0))
    moved = jax.random.randint(jax.random.fold_in(own, 4), (number_of // 2,), 0, 1 << 20) % (margin + 1)
    tallies = tallies.at[donor].add(-moved).at[taker].add(moved)
    labels = jnp.searchsorted(jnp.cumsum(tallies), jnp.arange(rows * top), side="right").astype(jnp.int32)
    listing = labels.reshape(top, rows).T
    listing = listing[jax.random.permutation(jax.random.fold_in(own, 1), rows)]
    turn = jax.random.randint(jax.random.fold_in(own, 2), (rows, 1), 0, top)
    return jnp.take_along_axis(listing, (jnp.arange(top)[None, :] + turn) % top, axis=1)


def portions_of(count, total, bound, lean, full):
    loads = [(1 << 20) // math.isqrt(rank ** lean) + 1 for rank in range(1, count + 1)]
    largest = bound if full else min(bound, max(-(-total // count), total * loads[0] // sum(loads)))
    least = 1 if total - largest >= count - 1 else 0
    holding, surplus = [largest] + [least] * (count - 1), total - largest - least * (count - 1)
    while surplus > 0:
        movable = [i for i in range(1, count) if holding[i] < largest] or [i for i in range(1, count) if holding[i] < bound]
        whole, remaining = sum([loads[i] for i in movable]), surplus
        for i in movable:
            addition = min(bound - holding[i], max(1, remaining * loads[i] // whole), surplus)
            holding[i] = holding[i] + addition
            surplus = surplus - addition
    return np.array(holding)


def noise(own_key, dims, spread, reach, cuts=(), kind=jnp.bfloat16):
    drawn = jax.random.normal(own_key, dims, jnp.float32) * spread
    if len(cuts) > 0:
        drawn = steps_of(own_key, dims, cuts, -0.22, 0.18) * drawn
    return jnp.clip(drawn, min=-reach, max=reach).astype(kind)


def setup_inputs(seed: int = 0) -> dict:
    seeds = jax.random.split(jax.random.key(seed), 13)
    residual = noise(seeds[0], (TOKEN_SPAN, BATCH_SIZE, D), 1.0, 6.0, ((0, 32),))
    queries = noise(seeds[1], (BATCH_SIZE, TOKEN_SPAN, ATTN_GROUPS * HS), 1.0, 6.0, ((1, 4), (2, 8)))
    key_vecs = noise(seeds[2], (BATCH_SIZE, TOKEN_SPAN, ATTN_GROUPS * HS), 0.088, 0.52734375, ((1, 4), (2, 8)))
    value_vecs = noise(seeds[3], (BATCH_SIZE, TOKEN_SPAN, ATTN_GROUPS * HS), 1.0, 6.0, ((1, 4), (2, 8)))
    log_decay = draw_log_decay(jax.random.fold_in(seeds[12], 71), 0)
    head_gain = jnp.clip(1.0 + 0.18 * jax.random.normal(seeds[5], (ATTN_GROUPS * HS,), jnp.float32), 0.1, 1.9)
    out_proj = noise(seeds[6], (ATTN_GROUPS * HS, D), (ATTN_GROUPS * HS) ** -0.5, 0.09375, ((0, 8),))
    norm_gain = jnp.clip(1.0 + 0.18 * jax.random.normal(seeds[7], (D,), jnp.float32), 0.1, 1.9)
    routes_keys = jax.random.split(jax.random.fold_in(seeds[8], 1), TOKEN_SPAN * BATCH_SIZE // (2 * LC))
    routes_turns = jax.random.permutation(jax.random.fold_in(seeds[8], 3), TOKEN_SPAN * BATCH_SIZE // (2 * LC))
    routes = jax.vmap(lambda own, number: routed_block(jax.random.fold_in(seeds[8], 2), own, number, 2 * LC, EXPERTS, TOPK, RCAP, 2))(routes_keys, routes_turns).reshape((TOKEN_SPAN, BATCH_SIZE, TOPK))
    route_weight = jnp.clip(jax.random.uniform(seeds[9], (TOKEN_SPAN, BATCH_SIZE, TOPK), jnp.float32, 0.1, 1.0), 0.1, 1.0)
    w_gate = noise(seeds[10], (EXPERTS, FF, D), D ** -0.5, 0.109375, ((0, 8), (1, 4)))
    w_up = noise(seeds[11], (EXPERTS, FF, D), D ** -0.5, 0.109375, ((0, 8), (1, 4)))
    return {"residual": residual, "queries": queries, "key_vecs": key_vecs, "value_vecs": value_vecs, "log_decay": log_decay, "head_gain": head_gain, "out_proj": out_proj, "norm_gain": norm_gain, "routes": routes, "route_weight": route_weight, "w_gate": w_gate, "w_up": w_up}


PRECISE = lax.Precision.HIGHEST

def row_norm(values_in, gain_vec):
    meansq = lax.optimization_barrier(jnp.mean(values_in * values_in, axis=-1, keepdims=True))
    return values_in * lax.rsqrt(meansq + 1e-06) * gain_vec

def blocks_of(array_in):
    return array_in.astype(jnp.float32).reshape(BATCH_SIZE, TOKEN_SPAN // LC, LC, ATTN_GROUPS, HS).transpose(1, 0, 3, 2, 4)

def reference(residual, queries, key_vecs, value_vecs, log_decay, head_gain, out_proj, norm_gain, routes, route_weight, w_gate, w_up):
    query_b = blocks_of(queries)
    key_b = blocks_of(key_vecs)
    value_b = blocks_of(value_vecs)
    decay_b = log_decay.reshape(BATCH_SIZE, ATTN_GROUPS, TOKEN_SPAN // LC, LC).transpose(2, 0, 1, 3)
    causal_mask = jnp.tril(jnp.ones((LC, LC), dtype=bool))

    def advance(state_now, block_data):
        query_t, key_t, value_t, decay_t = block_data
        running = jnp.cumsum(decay_t, axis=-1)
        spread_log = running[..., :, None] - running[..., None, :]
        decay_mat = jnp.where(causal_mask, jnp.exp(jnp.where(causal_mask, spread_log, 0.0)), 0.0)
        scores = jnp.einsum('bhtc,bhjc->bhtj', query_t, key_t, precision=PRECISE) * decay_mat
        inner_part = jnp.einsum('bhtj,bhjd->bhtd', scores, value_t, precision=PRECISE)
        outer_part = jnp.exp(running)[..., None] * jnp.einsum('bhtc,bhcd->bhtd', query_t, state_now, precision=PRECISE)
        tail_decay = jnp.exp(running[..., -1:] - running)
        fresh_state = jnp.einsum('bhjc,bhjd->bhcd', key_t * tail_decay[..., None], value_t, precision=PRECISE)
        state_now = jnp.exp(running[..., -1])[..., None, None] * state_now + fresh_state
        return (state_now, inner_part + outer_part)
    start_state = jnp.zeros((BATCH_SIZE, ATTN_GROUPS, HS, HS), jnp.float32)
    final_state, outputs = lax.scan(advance, start_state, (query_b, key_b, value_b, decay_b))
    normed_heads = row_norm(outputs, head_gain.reshape(ATTN_GROUPS, HS)[None, None, :, None, :])
    attention = normed_heads.transpose(0, 3, 1, 2, 4).reshape(TOKEN_SPAN, BATCH_SIZE, ATTN_GROUPS * HS).astype(jnp.bfloat16)
    projected = jnp.dot(attention.reshape(TOKEN_SPAN * BATCH_SIZE, ATTN_GROUPS * HS), out_proj, preferred_element_type=jnp.float32).reshape(TOKEN_SPAN, BATCH_SIZE, D)
    mixed_rows = residual.astype(jnp.float32) + projected
    attn_out = mixed_rows
    normed = row_norm(mixed_rows, norm_gain).astype(jnp.bfloat16)
    row_count = 2 * LC
    groups = normed.astype(jnp.float32).reshape(TOKEN_SPAN // LC, row_count, D)
    route_blocks = routes.reshape(TOKEN_SPAN // LC, row_count, TOPK)
    weight_blocks = route_weight.reshape(TOKEN_SPAN // LC, row_count, TOPK)
    slot_ids = jnp.arange(RCAP, dtype=jnp.int32)

    def per_expert(expert_id):
        route_hits = route_blocks == expert_id
        chosen = jnp.any(route_hits, axis=-1)
        token_weight = lax.optimization_barrier(jnp.sum(jnp.where(route_hits, weight_blocks, 0.0), axis=-1))
        slot_rank = jnp.cumsum(chosen.astype(jnp.int32), axis=1) - 1
        pick_table = ((slot_rank[:, None, :] == slot_ids[None, :, None]) & chosen[:, None, :]).astype(jnp.float32)
        slot_weight = jnp.einsum('csj,cj->cs', pick_table, token_weight, precision=PRECISE).reshape(-1)
        slot_rows = jnp.einsum('csj,cjd->csd', pick_table, groups, precision=PRECISE).astype(jnp.bfloat16).reshape(-1, D)
        gate_val = lax.dot_general(w_gate[expert_id], slot_rows, (((1,), (1,)), ((), ())), preferred_element_type=jnp.float32)
        up_val = lax.dot_general(w_up[expert_id], slot_rows, (((1,), (1,)), ((), ())), preferred_element_type=jnp.float32)
        return slot_weight[None, :] * jax.nn.silu(gate_val) * up_val
    expert_hidden = lax.map(per_expert, jnp.arange(EXPERTS, dtype=jnp.int32))
    return (attn_out, expert_hidden)
```

```python
import functools

import jax
import jax.numpy as jnp
from jax import lax
from jax.experimental import pallas as pl
from jax.experimental.pallas import tpu as pltpu
from jax.sharding import PartitionSpec as P

BF, F32 = jnp.bfloat16, jnp.float32
PRECISE = lax.Precision.HIGHEST
VMEM_BYTES = 48 * 1024 * 1024
NT = (((1,), (1,)), ((), ()))
TN = (((0,), (0,)), ((), ()))


def swap(block, axis, distance, forward_only=False):
    devices = range(lax.axis_size(axis))
    route = [(i, i ^ distance) for i in devices if not forward_only or i < i ^ distance]
    return lax.ppermute(block, axis, route)


def mm(a, b, dims=(((1,), (0,)), ((), ()))):
    return lax.dot_general(a, b, dims, preferred_element_type=F32)


def halves(x):
    high = x.astype(BF)
    return high, (x - high.astype(F32)).astype(BF)


def thirds(x):
    high, rest = x.astype(BF), None
    rest = x - high.astype(F32)
    middle = rest.astype(BF)
    return high, middle, (rest - middle.astype(F32)).astype(BF)


def lower_triangle(size):
    return (
        lax.broadcasted_iota(jnp.int32, (size, size), 0) >= lax.broadcasted_iota(jnp.int32, (size, size), 1)
    )


def running_columns(log_decay):
    tri = lower_triangle(log_decay.shape[1]).astype(F32)
    return lax.dot_general(tri, log_decay, NT, precision=PRECISE, preferred_element_type=F32)


def running_rows(log_decay):
    tri = lower_triangle(log_decay.shape[1]).astype(F32)
    return lax.dot_general(log_decay, tri, NT, precision=PRECISE, preferred_element_type=F32)


def state_kernel(k_ref, v_ref, decay_ref, out_ref):
    seqs, heads, size = decay_ref.shape
    width = k_ref.shape[2] // heads
    totals = []
    for b in range(seqs):
        columns = running_columns(decay_ref[b])
        tail = jnp.exp(columns[size - 1 : size, :] - columns)
        totals.append(jnp.broadcast_to(running_rows(decay_ref[b])[:, size - 1 : size], (heads, width)))
        for h in range(heads):
            part = slice(h * width, (h + 1) * width)
            value = v_ref[b, :, part]
            high, low = halves(k_ref[b, :, part].astype(F32) * tail[:, h : h + 1])
            at = (b * heads + h) * width
            out_ref[at : at + width, :] = (mm(high, value, TN) + mm(low, value, TN)).astype(BF)
    total = jnp.concatenate(totals, axis=0)
    pieces = [piece.astype(F32) for piece in thirds(total)]
    pieces.append(jnp.zeros_like(total))
    out_ref[seqs * heads * width :, :] = jnp.concatenate(pieces, axis=0).astype(BF)


def inner_kernel(q_ref, k_ref, v_ref, decay_ref, out_ref):
    seqs, heads, size = decay_ref.shape
    width = k_ref.shape[2] // heads
    causal = lower_triangle(size)
    for b in range(seqs):
        columns = running_columns(decay_ref[b])
        rows = running_rows(decay_ref[b])
        for h in range(heads):
            part = slice(h * width, (h + 1) * width)
            spread = columns[:, h : h + 1] - rows[h : h + 1, :]
            decay = jnp.where(causal, jnp.exp(jnp.where(causal, spread, 0.0)), 0.0)
            scores = mm(q_ref[b, :, part], k_ref[b, :, part], NT) * decay
            high, low = halves(scores)
            value = v_ref[b, :, part]
            out_ref[b, :, part] = mm(high, value) + mm(low, value)


def project_kernel(count, line, *refs):
    q_ref, inner_ref, decay_ref, gain_ref = refs[:4]
    states = refs[4 : 3 + count]
    proj_ref, own_ref, partner_ref, att_ref = refs[3 + count :]
    seqs, heads, size = decay_ref.shape
    width = q_ref.shape[2] // heads

    @pl.when(pl.program_id(0) == 0)
    def _():
        me = lax.axis_index("seq")
        index = lax.axis_index("exp")
        base = seqs * heads * width
        each = seqs * heads
        totals = []
        for state in states:
            three = state[base : base + 4 * each, :].astype(F32)
            totals.append(three[:each] + three[each : 2 * each] + three[2 * each : 3 * each])
        factors = []
        for first in range(1, count):
            later = jnp.zeros_like(totals[0])
            for second in range(1, count):
                between = ((me ^ first) < (me ^ second)) & ((me ^ second) < me)
                later = later + jnp.where(between, totals[second - 1], 0.0)
            factors.append(jnp.where((me ^ first) < me, jnp.exp(later), 0.0))
        rows = []
        for b in range(seqs):
            grown = jnp.exp(running_columns(decay_ref[b]))
            parts = []
            for h in range(heads):
                part = slice(h * width, (h + 1) * width)
                n = b * heads + h
                incoming = jnp.zeros((width, width), F32)
                for state, factor in zip(states, factors):
                    incoming = incoming + factor[n : n + 1, :] * state[n * width : (n + 1) * width, :].astype(F32)
                high, low = halves(incoming)
                query = q_ref[b, :, part]
                raw = inner_ref[b, :, part] + grown[:, h : h + 1] * (mm(query, high) + mm(query, low))
                meansq = jnp.mean(raw * raw, axis=-1, keepdims=True)
                parts.append((raw * lax.rsqrt(meansq + 1e-06) * gain_ref[:, part]).astype(BF))
            rows.append(jnp.concatenate(parts, axis=1))
        attention = jnp.concatenate(rows, axis=0)
        total = seqs * size
        own = size // (2 * line)
        to = lax.broadcasted_iota(jnp.int32, (total, total), 0)
        source = source_position(to // (total // 2), (to // (seqs * own)) % line, to % own, index, own)
        source = source + size * ((to // own) % seqs)
        pick = (source == lax.broadcasted_iota(jnp.int32, (total, total), 1)).astype(BF)
        att_ref[...] = mm(pick, attention).astype(BF)

    half = att_ref.shape[0] // 2
    own_ref[...] = mm(att_ref[:half, :], proj_ref[...])
    partner_ref[...] = mm(att_ref[half:, :], proj_ref[...]).astype(BF)


def source_position(flip, distance, place, index, own):
    return own * (2 * ((index // 2) ^ distance) + ((index % 2) ^ flip)) + place


def pair_sum_kernel(own_ref, got_ref, first_ref, *send_refs):
    rows = first_ref.shape[0]
    first_ref[...] = own_ref[:rows, :] + got_ref[:rows, :].astype(F32)
    for d, send_ref in enumerate(send_refs, start=1):
        part = slice(d * rows, (d + 1) * rows)
        send_ref[...] = (own_ref[part, :] + got_ref[part, :].astype(F32)).astype(BF)


def mix_kernel(first_ref, residual_ref, gain_ref, *refs):
    mixed_ref, normed_ref = refs[-2:]
    mixed = residual_ref[...].astype(F32) + first_ref[...]
    for got_ref in refs[:-2]:
        mixed = mixed + got_ref[...].astype(F32)
    mixed_ref[...] = mixed
    meansq = jnp.mean(mixed * mixed, axis=-1, keepdims=True)
    normed_ref[...] = (mixed * lax.rsqrt(meansq + 1e-06) * gain_ref[...]).astype(BF)


def route_kernel(capacity, own, seqs, first_ref, second_ref, first_weight, second_weight, slot_ref, weight_ref, a_ref, b_ref):
    count, total = first_ref.shape
    me = lax.axis_index("seq")
    index = lax.axis_index("exp")
    line = total // (2 * own * seqs)
    hit_a, hit_b = first_ref[...] == index, second_ref[...] == index
    chosen = jnp.where(hit_a | hit_b, 1.0, 0.0).astype(BF)
    weight = jnp.where(hit_a, first_weight[...], 0.0) + jnp.where(hit_b, second_weight[...], 0.0)
    to = lax.broadcasted_iota(jnp.int32, (total, total), 1)
    piece = total // 4
    distance = (to // (2 * piece)) * (line // 2) + (to // (seqs * own)) % (line // 2)
    row = source_position((to // piece) % 2, distance, to % own, index, own) * seqs + (to // own) % seqs
    origin = lax.broadcasted_iota(jnp.int32, (total, total), 0)
    rank = mm(chosen, (origin <= row).astype(BF)) - 1.0
    same = (origin == row).astype(BF)
    picked = mm(chosen, same) > 0.5
    block = lax.broadcasted_iota(jnp.int32, (count, total), 0) % (count // 2)
    a_ref[...] = jnp.where(picked, rank.astype(jnp.int32) + block * capacity, -1)
    high, middle, low = thirds(weight)
    b_ref[...] = mm(high, same) + mm(middle, same) + mm(low, same)
    for d in range(count):
        slot_ref[d : d + 1, :] = a_ref[pl.ds(me ^ d, 1), :]
        weight_ref[d : d + 1, :] = b_ref[pl.ds(me ^ d, 1), :]


def expert_kernel(pieces, side_ref, slot_ref, weight_ref, gate_ref, up_ref, *refs):
    refs = list(refs)
    piece_refs, out_ref, rows_ref, scale_ref = refs[:pieces], *refs[-3:]

    @pl.when(pl.program_id(0) == 0)
    def _():
        blocks, total = slot_ref.shape
        slots = rows_ref.shape[0]
        each = pieces // blocks
        gathered, scale = None, None
        for n in range(blocks):
            pick = (
                slot_ref[n : n + 1, :] == lax.broadcasted_iota(jnp.int32, (slots, total), 0)
            ).astype(BF)
            rows = jnp.concatenate([ref[...] for ref in piece_refs[n * each : (n + 1) * each]], axis=0)
            part = mm(pick, rows)
            gathered = part if n == 0 else gathered + part
            share = sum(mm(jnp.broadcast_to(w, (8, total)), pick, NT) for w in thirds(weight_ref[n : n + 1, :]))
            scale = share if n == 0 else scale + share
        rows_ref[...] = gathered.astype(BF)
        scale_ref[...] = scale

    gate = mm(gate_ref[0], rows_ref[...], NT)
    up = mm(up_ref[0], rows_ref[...], NT)
    out_ref[0] = scale_ref[0:1, :] * (gate / (1.0 + jnp.exp(-gate))) * up


def params():
    return pltpu.CompilerParams(vmem_limit_bytes=VMEM_BYTES)


def cost(flops, bytes_accessed, transcendentals=0):
    return pl.CostEstimate(flops=int(flops), bytes_accessed=int(bytes_accessed), transcendentals=int(transcendentals))


def whole(shape):
    return pl.BlockSpec(shape, lambda *_: (0,) * len(shape))


def expert_half(side, slot, weight, w_gate, w_up, pieces, previous):
    units, width = w_gate.shape[1:]
    tile = max(size for size in range(16, 385, 16) if units % size == 0)
    rows = [piece for block in pieces for piece in block]
    slots = previous[1]
    total = slot.shape[1]
    aliases = {} if previous[0] is None else {5 + len(rows): 0}
    carried = [] if previous[0] is None else [previous[0]]
    weights_spec = pl.BlockSpec((1, tile, width), lambda i, side: (0, i, 0))
    grid_spec = pltpu.PrefetchScalarGridSpec(
        num_scalar_prefetch=1,
        grid=(units // tile,),
        in_specs=[
            whole(slot.shape),
            whole(weight.shape),
            weights_spec,
            weights_spec,
        ]
        + [whole(piece.shape) for piece in rows]
        + [pl.BlockSpec(memory_space=pl.ANY) for _ in carried],
        out_specs=pl.BlockSpec((1, tile, slots), lambda i, side: (0, i, side[0])),
        scratch_shapes=[pltpu.VMEM((slots, width), BF), pltpu.VMEM((8, slots), F32)],
    )
    return pl.pallas_call(
        functools.partial(expert_kernel, len(rows)),
        grid_spec=grid_spec,
        out_shape=jax.ShapeDtypeStruct((1, units, 2 * slots), F32),
        input_output_aliases=aliases,
        compiler_params=params(),
        cost_estimate=cost(4 * units * width * slots + 2 * slots * total * width * len(pieces), 4 * units * width),
        name="expert_half",
    )(side, slot, weight, w_gate, w_up, *rows, *carried)


def per_device(
    residual,
    queries,
    key_vecs,
    value_vecs,
    log_decay,
    head_gain,
    out_proj,
    norm_gain,
    routes,
    route_weight,
    w_gate,
    w_up,
):
    count, owners = lax.axis_size("seq"), lax.axis_size("exp")
    line = owners // 2
    me = lax.axis_index("seq")
    seqs, size, feat = queries.shape
    heads = log_decay.shape[1]
    width = feat // heads
    own, _, model = residual.shape
    unit = own * seqs
    total = size * seqs
    capacity = 8 * size // owners

    states = pl.pallas_call(
        state_kernel,
        out_shape=jax.ShapeDtypeStruct((seqs * heads * (width + 4), width), BF),
        compiler_params=params(),
        cost_estimate=cost(4 * total * feat * width, 6 * total * feat),
        name="states",
    )(key_vecs, value_vecs, log_decay)
    arrived = [swap(states, "seq", d, forward_only=True) for d in range(1, count)]
    inner = pl.pallas_call(
        inner_kernel,
        out_shape=jax.ShapeDtypeStruct((seqs, size, feat), F32),
        compiler_params=params(),
        cost_estimate=cost(6 * total * feat * size, 10 * total * feat),
        name="inner",
    )(queries, key_vecs, value_vecs, log_decay)

    tile = next(t for t in (1024, 512, 256, 128) if model % t == 0)
    own_sum, partner_sum = pl.pallas_call(
        functools.partial(project_kernel, count, line),
        grid=(model // tile,),
        in_specs=[whole(queries.shape), whole(inner.shape), whole(log_decay.shape), whole((1, feat))]
        + [whole(states.shape)] * (count - 1)
        + [pl.BlockSpec((feat, tile), lambda i: (0, i))],
        out_specs=[pl.BlockSpec((total // 2, tile), lambda i: (0, i))] * 2,
        out_shape=[
            jax.ShapeDtypeStruct((total // 2, model), F32),
            jax.ShapeDtypeStruct((total // 2, model), BF),
        ],
        scratch_shapes=[pltpu.VMEM((total, feat), BF)],
        compiler_params=params(),
        cost_estimate=cost(2 * total * feat * model, 2 * feat * model + 3 * total * model),
        name="project",
    )(queries, inner, log_decay, head_gain.reshape(1, feat), *arrived, out_proj)

    from_partner = swap(partner_sum, "exp", 1)
    tiles = model // tile
    first, *sends = pl.pallas_call(
        pair_sum_kernel,
        grid=(tiles,),
        in_specs=[pl.BlockSpec((total // 2, tile), lambda i: (0, i))] * 2,
        out_specs=[pl.BlockSpec((unit, tile), lambda i: (0, i))] * line,
        out_shape=[jax.ShapeDtypeStruct((unit, model), F32)] + [jax.ShapeDtypeStruct((unit, model), BF)] * (line - 1),
        compiler_params=params(),
        cost_estimate=cost(total * model, 4 * total * model),
        name="pair_sum",
    )(own_sum, from_partner)
    got = [swap(send, "exp", 2 * d) for d, send in enumerate(sends, start=1)]

    residual_rows = jnp.transpose(residual, (1, 0, 2)).reshape(unit, model)
    mixed, normed = pl.pallas_call(
        mix_kernel,
        out_shape=[jax.ShapeDtypeStruct((unit, model), F32), jax.ShapeDtypeStruct((unit, model), BF)],
        compiler_params=params(),
        cost_estimate=cost(10 * unit * model, 16 * unit * model),
        name="mix",
    )(first, residual_rows, norm_gain.reshape(1, model), *got)
    mixed_rows = jnp.transpose(mixed.reshape(seqs, own, model), (1, 0, 2))

    block_routes = routes.reshape(count, total, routes.shape[-1])
    block_weights = route_weight.reshape(count, total, routes.shape[-1])
    slot, weight = pl.pallas_call(
        functools.partial(route_kernel, capacity, own, seqs),
        out_shape=[jax.ShapeDtypeStruct((count, total), jnp.int32), jax.ShapeDtypeStruct((count, total), F32)],
        scratch_shapes=[pltpu.VMEM((count, total), jnp.int32), pltpu.VMEM((count, total), F32)],
        compiler_params=params(),
        cost_estimate=cost(10 * count * total * total, 16 * count * total),
        name="route",
    )(block_routes[..., 0], block_routes[..., 1], block_weights[..., 0], block_weights[..., 1])

    along = [normed] + [swap(normed, "exp", 2 * d) for d in range(1, line)]
    parts = [jnp.concatenate(along[: line // 2], axis=0), jnp.concatenate(along[line // 2 :], axis=0)]
    blocks = []
    for d in range(count):
        pieces = []
        for part in parts:
            here = part if d == 0 else swap(part, "seq", d)
            pieces += [here, swap(here, "exp", 1)]
        blocks.append(pieces)
    half = count // 2
    slots = half * capacity
    side = (me // half).astype(jnp.int32).reshape(1)
    hidden = expert_half(side, slot[:half], weight[:half], w_gate, w_up, blocks[:half], (None, slots))
    hidden = expert_half(1 - side, slot[half:], weight[half:], w_gate, w_up, blocks[half:], (hidden, slots))
    return (mixed_rows, hidden)


def solution(mesh):
    placed = (
        P(("seq", "exp"), None, None),
        P(None, "seq", "exp"),
        P(None, "seq", "exp"),
        P(None, "seq", "exp"),
        P(None, "exp", "seq"),
        P("exp"),
        P("exp", None),
        P(),
        P(),
        P(),
        P("exp", "seq", None),
        P("exp", "seq", None),
    )
    return jax.shard_map(
        per_device,
        mesh=mesh,
        in_specs=placed,
        out_specs=(P(("seq", "exp"), None, None), P("exp", "seq", None)),
        check_vma=False,
    )
```

```python
import functools

import jax
import jax.numpy as jnp
from jax import lax
from jax.experimental import pallas as pl
from jax.experimental.pallas import tpu as pltpu
from jax.sharding import PartitionSpec as P

BF, F32 = jnp.bfloat16, jnp.float32
PRECISE = lax.Precision.HIGHEST
VMEM_BYTES = 16 * 1024 * 1024
NT = (((1,), (1,)), ((), ()))
TN = (((0,), (0,)), ((), ()))


def in_hbm(*arrays):
    return [pltpu.with_memory_space_constraint(array, pltpu.HBM) for array in arrays]


def in_vmem(*arrays):
    return [pltpu.with_memory_space_constraint(array, pltpu.VMEM) for array in arrays]


def swap(block, axis, distance, forward_only=False):
    devices = range(lax.axis_size(axis))
    route = [(i, i ^ distance) for i in devices if not forward_only or i < i ^ distance]
    return lax.ppermute(block, axis, route)


def mm(a, b, dims=(((1,), (0,)), ((), ()))):
    return lax.dot_general(a, b, dims, preferred_element_type=F32)


def halves(x):
    high = x.astype(BF)
    return high, (x - high.astype(F32)).astype(BF)


def thirds(x):
    high, rest = x.astype(BF), None
    rest = x - high.astype(F32)
    middle = rest.astype(BF)
    return high, middle, (rest - middle.astype(F32)).astype(BF)


def lower_triangle(size):
    return (
        lax.broadcasted_iota(jnp.int32, (size, size), 0) >= lax.broadcasted_iota(jnp.int32, (size, size), 1)
    )


def running_columns(log_decay):
    tri = lower_triangle(log_decay.shape[1]).astype(F32)
    return lax.dot_general(tri, log_decay, NT, precision=PRECISE, preferred_element_type=F32)


def running_rows(log_decay):
    tri = lower_triangle(log_decay.shape[1]).astype(F32)
    return lax.dot_general(log_decay, tri, NT, precision=PRECISE, preferred_element_type=F32)


def state_kernel(k_hbm, v_hbm, decay_hbm, *refs):
    out_refs, (k_ref, v_ref, decay_ref, sems) = refs[:-4], refs[-4:]
    copies = [
        pltpu.make_async_copy(source, to, sems.at[n])
        for n, (source, to) in enumerate(((decay_hbm, decay_ref), (k_hbm, k_ref), (v_hbm, v_ref)))
    ]
    for copy in copies:
        copy.start()
    for copy in copies:
        copy.wait()
    seqs, heads, size = decay_ref.shape
    width = k_ref.shape[2] // heads
    group = seqs // len(out_refs)
    for g, out_ref in enumerate(out_refs):
        totals = []
        for b in range(group):
            log_decay = decay_ref[g * group + b]
            columns = running_columns(log_decay)
            tail = jnp.exp(columns[size - 1 : size, :] - columns)
            totals.append(jnp.broadcast_to(running_rows(log_decay)[:, size - 1 : size], (heads, width)))
            for h in range(heads):
                part = slice(h * width, (h + 1) * width)
                value = v_ref[g * group + b, :, part]
                high, low = halves(k_ref[g * group + b, :, part].astype(F32) * tail[:, h : h + 1])
                at = (b * heads + h) * width
                out_ref[at : at + width, :] = (mm(high, value, TN) + mm(low, value, TN)).astype(BF)
        total = jnp.concatenate(totals, axis=0)
        pieces = [piece.astype(F32) for piece in thirds(total)]
        pieces.append(jnp.zeros_like(total))
        out_ref[group * heads * width :, :] = jnp.concatenate(pieces, axis=0).astype(BF)


def inner_kernel(q_hbm, k_hbm, v_hbm, decay_hbm, proj_hbm, residual_hbm, out_ref, q_ref, proj_ref, rows_ref, *scratch):
    k_ref, v_ref, decay_ref, residual_ref, sems = scratch
    pairs = (
        (decay_hbm, decay_ref),
        (q_hbm, q_ref),
        (k_hbm, k_ref),
        (v_hbm, v_ref),
        (residual_hbm, residual_ref),
        (proj_hbm, proj_ref),
    )
    copies = [pltpu.make_async_copy(source, to, sems.at[n]) for n, (source, to) in enumerate(pairs)]
    for copy in copies:
        copy.start()
    for copy in copies[:-1]:
        copy.wait()
    own, seqs, _ = residual_ref.shape
    for b in range(seqs):
        rows_ref[b * own : (b + 1) * own, :] = residual_ref[:, b, :].astype(F32)
    _, heads, size = decay_ref.shape
    width = k_ref.shape[2] // heads
    causal = lower_triangle(size)
    for b in range(seqs):
        columns = running_columns(decay_ref[b])
        rows = running_rows(decay_ref[b])
        for h in range(heads):
            part = slice(h * width, (h + 1) * width)
            spread = columns[:, h : h + 1] - rows[h : h + 1, :]
            decay = jnp.where(causal, jnp.exp(jnp.where(causal, spread, 0.0)), 0.0)
            scores = mm(q_ref[b, :, part], k_ref[b, :, part], NT) * decay
            high, low = halves(scores)
            value = v_ref[b, :, part]
            out_ref[b, :, part] = mm(high, value) + mm(low, value)
    copies[-1].wait()


def project_kernel(count, line, *refs):
    q_ref, inner_ref, decay_ref, gain_ref = refs[:4]
    states = refs[4 : 3 + count]
    proj_ref, own_ref, partner_ref = refs[3 + count :]
    seqs, size, feat = q_ref.shape
    heads = decay_ref.shape[1]
    width = feat // heads
    me = lax.axis_index("seq")
    index = lax.axis_index("exp")
    each = seqs * heads
    base = each * width
    totals = []
    for state in states:
        three = state[base : base + 4 * each, :].astype(F32)
        totals.append(three[:each] + three[each : 2 * each] + three[2 * each : 3 * each])
    factors = []
    for first in range(1, count):
        later = jnp.zeros_like(totals[0])
        for second in range(1, count):
            between = ((me ^ first) < (me ^ second)) & ((me ^ second) < me)
            later = later + jnp.where(between, totals[second - 1], 0.0)
        factors.append(jnp.where((me ^ first) < me, jnp.exp(later), 0.0))
    rows = []
    for b in range(seqs):
        grown = jnp.exp(running_columns(decay_ref[b]))
        parts = []
        for h in range(heads):
            part = slice(h * width, (h + 1) * width)
            n = b * heads + h
            incoming = jnp.zeros((width, width), F32)
            for state, factor in zip(states, factors):
                incoming = incoming + factor[n : n + 1, :] * state[n * width : (n + 1) * width, :].astype(F32)
            high, low = halves(incoming)
            query = q_ref[b, :, part]
            raw = inner_ref[b, :, part] + grown[:, h : h + 1] * (mm(query, high) + mm(query, low))
            meansq = jnp.mean(raw * raw, axis=-1, keepdims=True)
            parts.append((raw * lax.rsqrt(meansq + 1e-06) * gain_ref[:, part]).astype(BF))
        rows.append(jnp.concatenate(parts, axis=1))
    attention = jnp.concatenate(rows, axis=0)
    total = seqs * size
    own = size // (2 * line)
    to = lax.broadcasted_iota(jnp.int32, (total, total), 0)
    source = source_position(to // (total // 2), (to // (seqs * own)) % line, to % own, index, own)
    source = source + size * ((to // own) % seqs)
    pick = (source == lax.broadcasted_iota(jnp.int32, (total, total), 1)).astype(BF)
    attention = mm(pick, attention).astype(BF)
    model = proj_ref.shape[1]
    tile = column_tile(model)
    for n in range(model // tile):
        columns = slice(n * tile, (n + 1) * tile)
        product = mm(attention, proj_ref[:, columns])
        own_ref[:, columns] = product[: total // 2, :]
        partner_ref[:, columns] = product[total // 2 :, :].astype(BF)


def column_tile(model):
    return max(t for t in range(128, 1025, 128) if model % t == 0)


def source_position(flip, distance, place, index, own):
    return own * (2 * ((index // 2) ^ distance) + ((index % 2) ^ flip)) + place


def fold_kernel(kept_ref, got_ref, keep_ref, *send_refs):
    rows = keep_ref.shape[0]
    keep_ref[...] = kept_ref[:rows, :] + got_ref[:rows, :].astype(F32)
    for d, send_ref in enumerate(send_refs, start=1):
        part = slice(d * rows, (d + 1) * rows)
        send_ref[...] = (kept_ref[part, :] + got_ref[part, :].astype(F32)).astype(BF)


def mix_kernel(kept_ref, residual_ref, gain_ref, *refs):
    mixed_ref, normed_ref = refs[-2:]
    mixed = residual_ref[...] + kept_ref[...]
    for got_ref in refs[:-2]:
        mixed = mixed + got_ref[...].astype(F32)
    mixed_ref[...] = mixed
    meansq = jnp.mean(mixed * mixed, axis=-1, keepdims=True)
    normed_ref[...] = (mixed * lax.rsqrt(meansq + 1e-06) * gain_ref[...]).astype(BF)


def place_kernel(mixed_ref, out_ref):
    own, seqs, _ = out_ref.shape
    for b in range(seqs):
        out_ref[:, b, :] = mixed_ref[b * own : (b + 1) * own, :]


def load_kernel(gate_hbm, up_hbm, after, gate_ref, up_ref, sems):
    parts = sems.shape[1]
    rows = gate_ref.shape[1] // parts
    copies = []
    for m, (source, to) in enumerate(((gate_hbm, gate_ref), (up_hbm, up_ref))):
        for n in range(parts):
            part = pl.ds(n * rows, rows)
            copies.append(pltpu.make_async_copy(source.at[0, part], to.at[0, part], sems.at[m, n]))
            copies[-1].start()
    for copy in copies:
        copy.wait()


def gather_kernel(first, second, *refs):
    for to, sources in zip(refs[-2:], (refs[:first], refs[first : first + second])):
        at = 0
        for source in sources:
            to[at : at + source.shape[0], :] = source[...]
            at += source.shape[0]


def halves_kernel(one_ref, two_ref, after, low_ref, high_ref):
    half = low_ref.shape[0]
    low_ref[...] = one_ref[:half, :]
    high_ref[...] = two_ref[half:, :]


def exchanged(block, count, after):
    if count != 4 or block.shape[0] % 32 != 0:
        return [[swap(block, "seq", d)] for d in range(1, count)]
    half = block.shape[0] // 2
    one, two = swap(block, "seq", 1), swap(block, "seq", 2)
    vmem, anywhere = pl.BlockSpec(memory_space=pltpu.VMEM), pl.BlockSpec(memory_space=pl.ANY)
    low, high = pl.pallas_call(
        halves_kernel,
        in_specs=[vmem] * 2 + [anywhere],
        out_specs=[vmem] * 2,
        out_shape=[jax.ShapeDtypeStruct((half, block.shape[1]), block.dtype)] * 2,
        compiler_params=params(VMEM_BYTES // 8),
        cost_estimate=cost(1, 4 * block.size),
        name="halves",
    )(one, two, after)
    one, two, low, high = lax.optimization_barrier((one, two, low, high))
    return [[one], [two], [swap(low, "seq", 2), swap(high, "seq", 1)]]


def route_kernel(capacity, own, routes_ref, weights_ref, slot_ref, weight_ref, a_ref, b_ref):
    seqs, tops, _ = routes_ref.shape
    count, total = slot_ref.shape
    size = total // seqs
    me = lax.axis_index("seq")
    index = lax.axis_index("exp")
    line = size // (2 * own)
    lines, shares = [], []
    for c in range(count):
        part = slice(c * size, (c + 1) * size)
        hit, share = [], []
        for b in range(seqs):
            hits = [routes_ref[b, k : k + 1, part] == index for k in range(tops)]
            hit.append(sum(jnp.where(one, 1.0, 0.0) for one in hits))
            share.append(sum(jnp.where(one, weights_ref[b, k : k + 1, part], 0.0) for k, one in enumerate(hits)))
        lines.append(jnp.concatenate(hit, axis=1))
        shares.append(jnp.concatenate(share, axis=1))
    chosen = jnp.concatenate(lines, axis=0).astype(BF)
    weight = jnp.concatenate(shares, axis=0)
    to = lax.broadcasted_iota(jnp.int32, (total, total), 1)
    row = source_position(to // (total // 2), (to // (seqs * own)) % line, to % own, index, own) * seqs
    row = row + (to // own) % seqs
    origin = lax.broadcasted_iota(jnp.int32, (total, total), 0)
    origin = (origin % size) * seqs + origin // size
    rank = mm(chosen, (origin <= row).astype(BF)) - 1.0
    same = (origin == row).astype(BF)
    picked = mm(chosen, same) > 0.5
    block = lax.broadcasted_iota(jnp.int32, (count, total), 0) % (count // 2)
    a_ref[...] = jnp.where(picked, rank.astype(jnp.int32) + block * capacity, -1)
    high, middle, low = thirds(weight)
    b_ref[...] = mm(high, same) + mm(middle, same) + mm(low, same)
    for d in range(count):
        slot_ref[d : d + 1, :] = a_ref[pl.ds(me ^ d, 1), :]
        weight_ref[d : d + 1, :] = b_ref[pl.ds(me ^ d, 1), :]


def expert_kernel(plan, arrays, later, slot_ref, weight_ref, gate_ref, up_ref, *refs):
    array_refs, (out_hbm, rows_ref, out_ref, sems) = refs[:arrays], refs[-4:]
    count, total = slot_ref.shape
    blocks = count // 2
    first_block = later * blocks
    slots, width = rows_ref.shape
    tile = out_ref.shape[1]
    numbers = lax.broadcasted_iota(jnp.int32, (slots, total), 0)
    lines = range(first_block, first_block + blocks)
    pick = jnp.concatenate([(slot_ref[n : n + 1, :] == numbers).astype(BF) for n in lines], axis=1)
    weight = jnp.concatenate([weight_ref[n : n + 1, :] for n in lines], axis=1)
    parts = [part.astype(F32) for part in thirds(weight)] + [jnp.zeros((5, blocks * total), F32)]
    scale = jnp.sum(mm(jnp.concatenate(parts, axis=0).astype(BF), pick, NT), axis=0, keepdims=True)

    step = column_tile(width)
    for n in range(width // step):
        part = slice(n * step, (n + 1) * step)
        rows = [array_refs[number][first : first + height, part] for number, first, height in plan]
        rows_ref[:, part] = mm(pick, jnp.concatenate(rows, axis=0)).astype(BF)
    side = (lax.axis_index("seq") // blocks) ^ later
    columns = pl.ds(pl.multiple_of(side * slots, slots), slots)
    copies = []
    for step in range(out_ref.shape[0]):
        part = slice(step * tile, (step + 1) * tile)
        gate = mm(gate_ref[0, part, :], rows_ref[...], NT)
        up = mm(up_ref[0, part, :], rows_ref[...], NT)
        out_ref[step] = scale * (gate / (1.0 + jnp.exp(-gate))) * up
        copies.append(pltpu.make_async_copy(out_ref.at[step], out_hbm.at[0, part, columns], sems.at[step]))
        copies[-1].start()
    for copy in copies:
        copy.wait()


def params(vmem=VMEM_BYTES):
    return pltpu.CompilerParams(vmem_limit_bytes=vmem)


def cost(flops, bytes_accessed, transcendentals=0):
    return pl.CostEstimate(flops=int(flops), bytes_accessed=int(bytes_accessed), transcendentals=int(transcendentals))


def whole(shape):
    return pl.BlockSpec(shape, lambda *_: (0,) * len(shape))


def expert_half(later, slot, weight, w_gate, w_up, plan, arrays, previous, slots):
    units, width = w_gate.shape[1:]
    tile = max(size for size in range(16, 385, 16) if units % size == 0)
    steps = units // tile
    carried = [] if previous is None else [previous]
    vmem, hbm = pl.BlockSpec(memory_space=pltpu.VMEM), pl.BlockSpec(memory_space=pltpu.HBM)
    return pl.pallas_call(
        functools.partial(expert_kernel, plan, len(arrays), later),
        in_specs=[vmem] * (4 + len(arrays)) + [hbm] * len(carried),
        out_specs=hbm,
        out_shape=jax.ShapeDtypeStruct((1, units, 2 * slots), F32),
        scratch_shapes=[
            pltpu.VMEM((slots, width), BF),
            pltpu.VMEM((steps, tile, slots), F32),
            pltpu.SemaphoreType.DMA((steps,)),
        ],
        input_output_aliases={4 + len(arrays): 0} if carried else {},
        compiler_params=params(),
        cost_estimate=cost(4 * units * width * slots, 2 * slots * width),
        name="experts",
    )(slot, weight, *in_vmem(w_gate, w_up), *arrays, *carried)


def per_device(
    residual,
    queries,
    key_vecs,
    value_vecs,
    log_decay,
    head_gain,
    out_proj,
    norm_gain,
    routes,
    route_weight,
    w_gate,
    w_up,
):
    count, owners = lax.axis_size("seq"), lax.axis_size("exp")
    line = owners // 2
    me = lax.axis_index("seq")
    seqs, size, feat = queries.shape
    heads = log_decay.shape[1]
    width = feat // heads
    own, _, model = residual.shape
    unit = own * seqs
    total = size * seqs
    capacity = 8 * size // owners

    vmem, hbm, anywhere = (pl.BlockSpec(memory_space=space) for space in (pltpu.VMEM, pltpu.HBM, pl.ANY))

    states = pl.pallas_call(
        state_kernel,
        in_specs=[hbm] * 3,
        out_shape=jax.ShapeDtypeStruct((seqs * heads * (width + 4), width), BF),
        scratch_shapes=[
            pltpu.VMEM(key_vecs.shape, BF),
            pltpu.VMEM(value_vecs.shape, BF),
            pltpu.VMEM(log_decay.shape, F32),
            pltpu.SemaphoreType.DMA((3,)),
        ],
        compiler_params=params(),
        cost_estimate=cost(4 * total * feat * width, 6 * total * feat),
        name="states",
    )(*in_hbm(key_vecs, value_vecs, log_decay))
    arrived = [swap(states, "seq", d, forward_only=True) for d in range(1, count)]

    inner, query, proj, residual_rows = pl.pallas_call(
        inner_kernel,
        in_specs=[hbm] * 6,
        out_specs=[vmem] * 4,
        out_shape=[
            pltpu.VMEM((seqs, size, feat), F32),
            pltpu.VMEM(queries.shape, BF),
            pltpu.VMEM(out_proj.shape, BF),
            pltpu.VMEM((unit, model), F32),
        ],
        scratch_shapes=[
            pltpu.VMEM(key_vecs.shape, BF),
            pltpu.VMEM(value_vecs.shape, BF),
            pltpu.VMEM(log_decay.shape, F32),
            pltpu.VMEM(residual.shape, BF),
            pltpu.SemaphoreType.DMA((6,)),
        ],
        compiler_params=params(),
        cost_estimate=cost(6 * total * feat * size, 10 * total * feat),
        name="inner",
    )(*in_hbm(queries, key_vecs, value_vecs, log_decay, out_proj, residual))

    own_sum, partner_sum = pl.pallas_call(
        functools.partial(project_kernel, count, line),
        in_specs=[vmem] * (5 + count - 1),
        out_specs=[vmem] * 2,
        out_shape=[jax.ShapeDtypeStruct((total // 2, model), F32), jax.ShapeDtypeStruct((total // 2, model), BF)],
        compiler_params=params(),
        cost_estimate=cost(2 * total * feat * model, 2 * feat * model + 3 * total * model),
        name="project",
    )(*in_vmem(query, inner), log_decay, head_gain.reshape(1, feat), *arrived, *in_vmem(proj))

    tile = column_tile(model)

    def column_blocks(count):
        return pl.BlockSpec((count, tile), lambda i: (0, i))

    keep, *sends = pl.pallas_call(
        fold_kernel,
        grid=(model // tile,),
        in_specs=[column_blocks(total // 2)] * 2,
        out_specs=[column_blocks(unit)] * line,
        out_shape=[jax.ShapeDtypeStruct((unit, model), F32)]
        + [jax.ShapeDtypeStruct((unit, model), BF)] * (line - 1),
        compiler_params=params(),
        cost_estimate=cost(total * model, 4 * total * model),
        name="fold",
    )(own_sum, swap(partner_sum, "exp", 1))
    got = [swap(send, "exp", 2 * d) for d, send in enumerate(sends, start=1)]

    routes, route_weight, keep = lax.optimization_barrier((routes, route_weight, keep))
    slot, weight = pl.pallas_call(
        functools.partial(route_kernel, capacity, own),
        out_shape=[jax.ShapeDtypeStruct((count, total), jnp.int32), jax.ShapeDtypeStruct((count, total), F32)],
        scratch_shapes=[pltpu.VMEM((count, total), jnp.int32), pltpu.VMEM((count, total), F32)],
        compiler_params=params(),
        cost_estimate=cost(10 * count * total * total, 16 * count * total),
        name="route",
    )(jnp.transpose(routes, (1, 2, 0)), jnp.transpose(route_weight, (1, 2, 0)))

    keep, slot, weight = lax.optimization_barrier((keep, slot, weight))
    mixed, normed = pl.pallas_call(
        mix_kernel,
        out_shape=[jax.ShapeDtypeStruct((unit, model), F32), jax.ShapeDtypeStruct((unit, model), BF)],
        compiler_params=params(),
        cost_estimate=cost(10 * unit * model, 16 * unit * model),
        name="mix",
    )(keep, residual_rows, norm_gain.reshape(1, model), *got)
    attn_out = pl.pallas_call(
        place_kernel,
        out_shape=jax.ShapeDtypeStruct((own, seqs, model), F32),
        compiler_params=params(VMEM_BYTES // 8),
        cost_estimate=cost(1, 8 * unit * model),
        name="place",
    )(mixed)

    along = [swap(normed, "exp", 2 * d) for d in range(1, line)]
    across = [normed] + [swap(normed, "seq", d) for d in range(1, count)]
    rows = [len(arrays) * unit for arrays in (across, along)]
    near, rest = pl.pallas_call(
        functools.partial(gather_kernel, count, line - 1),
        in_specs=[vmem] * (count + line - 1) + [anywhere],
        out_specs=[vmem] * 2,
        out_shape=[jax.ShapeDtypeStruct((n, model), BF) for n in rows],
        compiler_params=params(VMEM_BYTES // 8),
        cost_estimate=cost(1, 4 * sum(rows) * model),
        name="gather",
    )(*across, *along, *in_hbm(attn_out))
    gate, up = pl.pallas_call(
        load_kernel,
        in_specs=[hbm, hbm, anywhere],
        out_specs=[vmem] * 2,
        out_shape=[pltpu.VMEM(w_gate.shape, BF), pltpu.VMEM(w_up.shape, BF)],
        scratch_shapes=[pltpu.SemaphoreType.DMA((2, 4))],
        compiler_params=params(VMEM_BYTES // 8),
        cost_estimate=cost(1, 4 * w_gate.size),
        name="load",
    )(*in_hbm(w_gate, w_up), rest)
    rests = [[rest]] + exchanged(rest, count, *in_vmem(gate))
    half = count // 2
    slots = half * capacity

    def planned(first, parts):
        plan, arrays = [], [near, near_partner]
        for n, pieces in enumerate(parts):
            partners = [swap(piece, "exp", 1) for piece in pieces]
            for k, share in enumerate((pieces, partners)):
                plan.append((k, (first + n) * unit, unit))
                for piece in share:
                    plan.append((len(arrays), 0, piece.shape[0]))
                    arrays.append(piece)
        return plan, arrays

    near_partner = swap(near, "exp", 1)
    plan, arrays = planned(0, rests[:half])
    hidden = expert_half(0, slot, weight, gate, up, plan, arrays, None, slots)
    late = [len(pieces) for pieces in rests[half:]]
    *pieces, hidden = lax.optimization_barrier((*(piece for part in rests[half:] for piece in part), hidden))
    pieces = iter(pieces)
    plan, arrays = planned(half, [[next(pieces) for _ in range(n)] for n in late])
    hidden = expert_half(1, slot, weight, gate, up, plan, arrays, hidden, slots)
    return (attn_out, hidden)


def solution(mesh):
    placed = (
        P(("seq", "exp"), None, None),
        P(None, "seq", "exp"),
        P(None, "seq", "exp"),
        P(None, "seq", "exp"),
        P(None, "exp", "seq"),
        P("exp"),
        P("exp", None),
        P(),
        P(),
        P(),
        P("exp", "seq", None),
        P("exp", "seq", None),
    )
    return jax.shard_map(
        per_device,
        mesh=mesh,
        in_specs=placed,
        out_specs=(P(("seq", "exp"), None, None), P("exp", "seq", None)),
        check_vma=False,
    )
```

```python
import functools

import jax
import jax.numpy as jnp
from jax import lax
from jax.experimental import pallas as pl
from jax.experimental.pallas import tpu as pltpu
from jax.sharding import PartitionSpec as P

BF, F32 = jnp.bfloat16, jnp.float32
PRECISE = lax.Precision.HIGHEST
VMEM_BYTES = 16 * 1024 * 1024
NT = (((1,), (1,)), ((), ()))
TN = (((0,), (0,)), ((), ()))


def in_hbm(*arrays):
    return [pltpu.with_memory_space_constraint(array, pltpu.HBM) for array in arrays]


def in_vmem(*arrays):
    return [pltpu.with_memory_space_constraint(array, pltpu.VMEM) for array in arrays]


def swap(block, axis, distance, forward_only=False):
    devices = range(lax.axis_size(axis))
    route = [(i, i ^ distance) for i in devices if not forward_only or i < i ^ distance]
    return lax.ppermute(block, axis, route)


def mm(a, b, dims=(((1,), (0,)), ((), ()))):
    return lax.dot_general(a, b, dims, preferred_element_type=F32)


def halves(x):
    high = x.astype(BF)
    return high, (x - high.astype(F32)).astype(BF)


def thirds(x):
    high, rest = x.astype(BF), None
    rest = x - high.astype(F32)
    middle = rest.astype(BF)
    return high, middle, (rest - middle.astype(F32)).astype(BF)


def lower_triangle(size):
    return (
        lax.broadcasted_iota(jnp.int32, (size, size), 0) >= lax.broadcasted_iota(jnp.int32, (size, size), 1)
    )


def running_columns(log_decay):
    tri = lower_triangle(log_decay.shape[1]).astype(F32)
    return lax.dot_general(tri, log_decay, NT, precision=PRECISE, preferred_element_type=F32)


def running_rows(log_decay):
    tri = lower_triangle(log_decay.shape[1]).astype(F32)
    return lax.dot_general(log_decay, tri, NT, precision=PRECISE, preferred_element_type=F32)


def state_kernel(k_hbm, v_hbm, decay_hbm, proj_hbm, out_ref, proj_ref, k_ref, v_ref, decay_ref, sems):
    pairs = ((decay_hbm, decay_ref), (k_hbm, k_ref), (v_hbm, v_ref), (proj_hbm, proj_ref))
    copies = [pltpu.make_async_copy(source, to, sems.at[n]) for n, (source, to) in enumerate(pairs)]
    for copy in copies:
        copy.start()
    for copy in copies[:-1]:
        copy.wait()
    seqs, heads, size = decay_ref.shape
    width = k_ref.shape[2] // heads
    totals = []
    for b in range(seqs):
        columns = running_columns(decay_ref[b])
        tail = jnp.exp(columns[size - 1 : size, :] - columns)
        totals.append(jnp.broadcast_to(running_rows(decay_ref[b])[:, size - 1 : size], (heads, width)))
        for h in range(heads):
            part = slice(h * width, (h + 1) * width)
            value = v_ref[b, :, part]
            high, low = halves(k_ref[b, :, part].astype(F32) * tail[:, h : h + 1])
            at = (b * heads + h) * width
            out_ref[at : at + width, :] = (mm(high, value, TN) + mm(low, value, TN)).astype(BF)
    total = jnp.concatenate(totals, axis=0)
    pieces = [piece.astype(F32) for piece in thirds(total)]
    pieces.append(jnp.zeros_like(total))
    out_ref[seqs * heads * width :, :] = jnp.concatenate(pieces, axis=0).astype(BF)
    copies[-1].wait()


def inner_kernel(q_hbm, k_hbm, v_hbm, decay_hbm, residual_hbm, after, out_ref, q_ref, rows_ref, *scratch):
    k_ref, v_ref, decay_ref, residual_ref, sems = scratch
    pairs = (
        (decay_hbm, decay_ref),
        (q_hbm, q_ref),
        (k_hbm, k_ref),
        (v_hbm, v_ref),
        (residual_hbm, residual_ref),
    )
    copies = [pltpu.make_async_copy(source, to, sems.at[n]) for n, (source, to) in enumerate(pairs)]
    for copy in copies:
        copy.start()
    for copy in copies:
        copy.wait()
    own, seqs, _ = residual_ref.shape
    for b in range(seqs):
        rows_ref[b * own : (b + 1) * own, :] = residual_ref[:, b, :].astype(F32)
    _, heads, size = decay_ref.shape
    width = k_ref.shape[2] // heads
    causal = lower_triangle(size)
    for b in range(seqs):
        columns = running_columns(decay_ref[b])
        rows = running_rows(decay_ref[b])
        for h in range(heads):
            part = slice(h * width, (h + 1) * width)
            spread = columns[:, h : h + 1] - rows[h : h + 1, :]
            decay = jnp.where(causal, jnp.exp(jnp.where(causal, spread, 0.0)), 0.0)
            scores = mm(q_ref[b, :, part], k_ref[b, :, part], NT) * decay
            high, low = halves(scores)
            value = v_ref[b, :, part]
            out_ref[b, :, part] = mm(high, value) + mm(low, value)


def attend_kernel(count, line, *refs):
    q_ref, inner_ref, decay_ref, gain_ref = refs[:4]
    states = refs[4 : 3 + count]
    own_ref, partner_ref = refs[3 + count :]
    seqs, size, feat = q_ref.shape
    heads = decay_ref.shape[1]
    width = feat // heads
    me = lax.axis_index("seq")
    index = lax.axis_index("exp")
    each = seqs * heads
    base = each * width
    totals = []
    for state in states:
        three = state[base : base + 4 * each, :].astype(F32)
        totals.append(three[:each] + three[each : 2 * each] + three[2 * each : 3 * each])
    factors = []
    for first in range(1, count):
        later = jnp.zeros_like(totals[0])
        for second in range(1, count):
            between = ((me ^ first) < (me ^ second)) & ((me ^ second) < me)
            later = later + jnp.where(between, totals[second - 1], 0.0)
        factors.append(jnp.where((me ^ first) < me, jnp.exp(later), 0.0))
    rows = []
    for b in range(seqs):
        grown = jnp.exp(running_columns(decay_ref[b]))
        parts = []
        for h in range(heads):
            part = slice(h * width, (h + 1) * width)
            n = b * heads + h
            incoming = jnp.zeros((width, width), F32)
            for state, factor in zip(states, factors):
                incoming = incoming + factor[n : n + 1, :] * state[n * width : (n + 1) * width, :].astype(F32)
            high, low = halves(incoming)
            query = q_ref[b, :, part]
            raw = inner_ref[b, :, part] + grown[:, h : h + 1] * (mm(query, high) + mm(query, low))
            meansq = jnp.mean(raw * raw, axis=-1, keepdims=True)
            parts.append((raw * lax.rsqrt(meansq + 1e-06) * gain_ref[:, part]).astype(BF))
        rows.append(jnp.concatenate(parts, axis=1))
    attention = jnp.concatenate(rows, axis=0)
    total = seqs * size
    own = size // (2 * line)
    to = lax.broadcasted_iota(jnp.int32, (total, total), 0)
    source = source_position(to // (total // 2), (to // (seqs * own)) % line, to % own, index, own)
    source = source + size * ((to // own) % seqs)
    pick = (source == lax.broadcasted_iota(jnp.int32, (total, total), 1)).astype(BF)
    attention = mm(pick, attention).astype(BF)
    own_ref[...] = attention[: total // 2, :]
    partner_ref[...] = attention[total // 2 :, :]


def project_kernel(own_ref, partner_ref, proj_ref, partner_proj_ref, keep_ref, *send_refs):
    rows, model = keep_ref.shape
    tile = column_tile(model)
    for n in range(model // tile):
        columns = slice(n * tile, (n + 1) * tile)
        product = mm(own_ref[...], proj_ref[:, columns]) + mm(partner_ref[...], partner_proj_ref[:, columns])
        keep_ref[:, columns] = product[:rows, :]
        for d, send_ref in enumerate(send_refs, start=1):
            send_ref[:, columns] = product[d * rows : (d + 1) * rows, :].astype(BF)


def column_tile(model):
    return max(t for t in range(128, 1025, 128) if model % t == 0)


def source_position(flip, distance, place, index, own):
    return own * (2 * ((index // 2) ^ distance) + ((index % 2) ^ flip)) + place


def mix_kernel(kept_ref, residual_ref, gain_ref, *refs):
    mixed_ref, normed_ref = refs[-2:]
    mixed = residual_ref[...] + kept_ref[...]
    for got_ref in refs[:-2]:
        mixed = mixed + got_ref[...].astype(F32)
    mixed_ref[...] = mixed
    meansq = jnp.mean(mixed * mixed, axis=-1, keepdims=True)
    normed_ref[...] = (mixed * lax.rsqrt(meansq + 1e-06) * gain_ref[...]).astype(BF)


def place_kernel(mixed_ref, out_ref):
    own, seqs, _ = out_ref.shape
    for b in range(seqs):
        out_ref[:, b, :] = mixed_ref[b * own : (b + 1) * own, :]


def load_kernel(gate_hbm, up_hbm, after, gate_ref, up_ref, sems):
    parts = sems.shape[1]
    rows = gate_ref.shape[1] // parts
    copies = []
    for m, (source, to) in enumerate(((gate_hbm, gate_ref), (up_hbm, up_ref))):
        for n in range(parts):
            part = pl.ds(n * rows, rows)
            copies.append(pltpu.make_async_copy(source.at[0, part], to.at[0, part], sems.at[m, n]))
            copies[-1].start()
    for copy in copies:
        copy.wait()


def gather_kernel(first, second, *refs):
    near_ref, rest_ref, corner_ref = refs[-3:]
    for to, sources in ((near_ref, refs[:first]), (rest_ref, refs[first : first + second])):
        at = 0
        for source in sources:
            to[at : at + source.shape[0], :] = source[...]
            at += source.shape[0]
    corner_ref[...] = refs[first - 1][...]


def halves_kernel(one_ref, two_ref, corner_ref, after, low_ref, high_ref):
    half = low_ref.shape[0]
    first = one_ref.shape[0] - 2 * half
    low_ref[...] = one_ref[first : first + half, :]
    high_ref[...] = two_ref[first + half :, :]


def exchanged(block, corner, count, after):
    rows, unit = block.shape[0], corner.shape[0]
    if count != 4 or unit % 16 != 0 or (rows - unit) % 32 != 0 or rows == unit:
        return [[swap(block, "seq", d)] for d in range(1, count)]
    one, two = swap(block, "seq", 1), swap(block, "seq", 2)
    corner = swap(corner, "exp", 2)
    vmem, anywhere = pl.BlockSpec(memory_space=pltpu.VMEM), pl.BlockSpec(memory_space=pl.ANY)
    low, high = pl.pallas_call(
        halves_kernel,
        in_specs=[vmem] * 3 + [anywhere],
        out_specs=[vmem] * 2,
        out_shape=[jax.ShapeDtypeStruct(((rows - unit) // 2, block.shape[1]), block.dtype)] * 2,
        compiler_params=params(VMEM_BYTES // 8),
        cost_estimate=cost(1, 4 * block.size),
        name="halves",
    )(one, two, corner, after)
    one, two, low, high = lax.optimization_barrier((one, two, low, high))
    return [[one], [two], [corner, swap(low, "seq", 2), swap(high, "seq", 1)]]


def route_kernel(capacity, own, routes_ref, weights_ref, slot_ref, weight_ref, a_ref, b_ref):
    seqs, tops, _ = routes_ref.shape
    count, total = slot_ref.shape
    size = total // seqs
    me = lax.axis_index("seq")
    index = lax.axis_index("exp")
    line = size // (2 * own)
    lines, shares = [], []
    for c in range(count):
        part = slice(c * size, (c + 1) * size)
        hit, share = [], []
        for b in range(seqs):
            hits = [routes_ref[b, k : k + 1, part] == index for k in range(tops)]
            hit.append(sum(jnp.where(one, 1.0, 0.0) for one in hits))
            share.append(sum(jnp.where(one, weights_ref[b, k : k + 1, part], 0.0) for k, one in enumerate(hits)))
        lines.append(jnp.concatenate(hit, axis=1))
        shares.append(jnp.concatenate(share, axis=1))
    chosen = jnp.concatenate(lines, axis=0).astype(BF)
    weight = jnp.concatenate(shares, axis=0)
    to = lax.broadcasted_iota(jnp.int32, (total, total), 1)
    row = source_position(to // (total // 2), (to // (seqs * own)) % line, to % own, index, own) * seqs
    row = row + (to // own) % seqs
    origin = lax.broadcasted_iota(jnp.int32, (total, total), 0)
    origin = (origin % size) * seqs + origin // size
    rank = mm(chosen, (origin <= row).astype(BF)) - 1.0
    same = (origin == row).astype(BF)
    picked = mm(chosen, same) > 0.5
    block = lax.broadcasted_iota(jnp.int32, (count, total), 0) % (count // 2)
    a_ref[...] = jnp.where(picked, rank.astype(jnp.int32) + block * capacity, -1)
    high, middle, low = thirds(weight)
    b_ref[...] = mm(high, same) + mm(middle, same) + mm(low, same)
    for d in range(count):
        slot_ref[d : d + 1, :] = a_ref[pl.ds(me ^ d, 1), :]
        weight_ref[d : d + 1, :] = b_ref[pl.ds(me ^ d, 1), :]


def expert_kernel(plan, arrays, later, slot_ref, weight_ref, gate_ref, up_ref, *refs):
    array_refs, (out_hbm, rows_ref, out_ref, sems) = refs[:arrays], refs[-4:]
    count, total = slot_ref.shape
    blocks = count // 2
    first_block = later * blocks
    slots, width = rows_ref.shape
    tile = out_ref.shape[1]
    numbers = lax.broadcasted_iota(jnp.int32, (slots, total), 0)
    lines = range(first_block, first_block + blocks)
    pick = jnp.concatenate([(slot_ref[n : n + 1, :] == numbers).astype(BF) for n in lines], axis=1)
    weight = jnp.concatenate([weight_ref[n : n + 1, :] for n in lines], axis=1)
    parts = [part.astype(F32) for part in thirds(weight)] + [jnp.zeros((5, blocks * total), F32)]
    scale = jnp.sum(mm(jnp.concatenate(parts, axis=0).astype(BF), pick, NT), axis=0, keepdims=True)

    step = column_tile(width)
    for n in range(width // step):
        part = slice(n * step, (n + 1) * step)
        rows = [array_refs[number][first : first + height, part] for number, first, height in plan]
        rows_ref[:, part] = mm(pick, jnp.concatenate(rows, axis=0)).astype(BF)
    side = (lax.axis_index("seq") // blocks) ^ later
    columns = pl.ds(pl.multiple_of(side * slots, slots), slots)
    copies = []
    for step in range(out_ref.shape[0]):
        part = slice(step * tile, (step + 1) * tile)
        gate = mm(gate_ref[0, part, :], rows_ref[...], NT)
        up = mm(up_ref[0, part, :], rows_ref[...], NT)
        out_ref[step] = scale * (gate / (1.0 + jnp.exp(-gate))) * up
        copies.append(pltpu.make_async_copy(out_ref.at[step], out_hbm.at[0, part, columns], sems.at[step]))
        copies[-1].start()
    for copy in copies:
        copy.wait()


def params(vmem=VMEM_BYTES):
    return pltpu.CompilerParams(vmem_limit_bytes=vmem)


def cost(flops, bytes_accessed, transcendentals=0):
    return pl.CostEstimate(flops=int(flops), bytes_accessed=int(bytes_accessed), transcendentals=int(transcendentals))


def whole(shape):
    return pl.BlockSpec(shape, lambda *_: (0,) * len(shape))


def expert_half(later, slot, weight, w_gate, w_up, plan, arrays, previous, slots):
    units, width = w_gate.shape[1:]
    tile = max(size for size in range(16, 385, 16) if units % size == 0)
    steps = units // tile
    carried = [] if previous is None else [previous]
    vmem, hbm = pl.BlockSpec(memory_space=pltpu.VMEM), pl.BlockSpec(memory_space=pltpu.HBM)
    return pl.pallas_call(
        functools.partial(expert_kernel, plan, len(arrays), later),
        in_specs=[vmem] * (4 + len(arrays)) + [hbm] * len(carried),
        out_specs=hbm,
        out_shape=jax.ShapeDtypeStruct((1, units, 2 * slots), F32),
        scratch_shapes=[
            pltpu.VMEM((slots, width), BF),
            pltpu.VMEM((steps, tile, slots), F32),
            pltpu.SemaphoreType.DMA((steps,)),
        ],
        input_output_aliases={4 + len(arrays): 0} if carried else {},
        compiler_params=params(),
        cost_estimate=cost(4 * units * width * slots, 2 * slots * width),
        name="experts",
    )(slot, weight, *in_vmem(w_gate, w_up), *arrays, *carried)


def per_device(
    residual,
    queries,
    key_vecs,
    value_vecs,
    log_decay,
    head_gain,
    out_proj,
    norm_gain,
    routes,
    route_weight,
    w_gate,
    w_up,
):
    count, owners = lax.axis_size("seq"), lax.axis_size("exp")
    line = owners // 2
    me = lax.axis_index("seq")
    seqs, size, feat = queries.shape
    heads = log_decay.shape[1]
    width = feat // heads
    own, _, model = residual.shape
    unit = own * seqs
    total = size * seqs
    capacity = 8 * size // owners

    vmem, hbm, anywhere = (pl.BlockSpec(memory_space=space) for space in (pltpu.VMEM, pltpu.HBM, pl.ANY))

    states, proj = pl.pallas_call(
        state_kernel,
        in_specs=[hbm] * 4,
        out_specs=[vmem] * 2,
        out_shape=[
            pltpu.VMEM((seqs * heads * (width + 4), width), BF),
            pltpu.VMEM(out_proj.shape, BF),
        ],
        scratch_shapes=[
            pltpu.VMEM(key_vecs.shape, BF),
            pltpu.VMEM(value_vecs.shape, BF),
            pltpu.VMEM(log_decay.shape, F32),
            pltpu.SemaphoreType.DMA((4,)),
        ],
        compiler_params=params(),
        cost_estimate=cost(4 * total * feat * width, 6 * total * feat),
        name="states",
    )(*in_hbm(key_vecs, value_vecs, log_decay, out_proj))
    arrived = [swap(states, "seq", d) for d in range(1, count)]

    inner, query, residual_rows = pl.pallas_call(
        inner_kernel,
        in_specs=[hbm] * 5 + [anywhere],
        out_specs=[vmem] * 3,
        out_shape=[
            pltpu.VMEM((seqs, size, feat), F32),
            pltpu.VMEM(queries.shape, BF),
            pltpu.VMEM((unit, model), F32),
        ],
        scratch_shapes=[
            pltpu.VMEM(key_vecs.shape, BF),
            pltpu.VMEM(value_vecs.shape, BF),
            pltpu.VMEM(log_decay.shape, F32),
            pltpu.VMEM(residual.shape, BF),
            pltpu.SemaphoreType.DMA((5,)),
        ],
        compiler_params=params(),
        cost_estimate=cost(6 * total * feat * size, 10 * total * feat),
        name="inner",
    )(*in_hbm(queries, key_vecs, value_vecs, log_decay, residual), *in_vmem(states))

    mine, theirs = pl.pallas_call(
        functools.partial(attend_kernel, count, line),
        in_specs=[vmem] * (4 + count - 1),
        out_specs=[vmem] * 2,
        out_shape=[jax.ShapeDtypeStruct((total // 2, feat), BF)] * 2,
        compiler_params=params(),
        cost_estimate=cost(6 * total * feat * width, 10 * total * feat),
        name="attend",
    )(*in_vmem(query, inner), log_decay, head_gain.reshape(1, feat), *arrived)

    keep, *sends = pl.pallas_call(
        project_kernel,
        in_specs=[vmem] * 4,
        out_specs=[vmem] * line,
        out_shape=[jax.ShapeDtypeStruct((unit, model), F32)]
        + [jax.ShapeDtypeStruct((unit, model), BF)] * (line - 1),
        compiler_params=params(),
        cost_estimate=cost(2 * total * feat * model, 4 * feat * model + 3 * total * model),
        name="project",
    )(mine, swap(theirs, "exp", 1), *in_vmem(proj), swap(proj, "exp", 1))
    got = [swap(send, "exp", 2 * d) for d, send in enumerate(sends, start=1)]

    routes, route_weight, keep = lax.optimization_barrier((routes, route_weight, keep))
    slot, weight = pl.pallas_call(
        functools.partial(route_kernel, capacity, own),
        out_shape=[jax.ShapeDtypeStruct((count, total), jnp.int32), jax.ShapeDtypeStruct((count, total), F32)],
        scratch_shapes=[pltpu.VMEM((count, total), jnp.int32), pltpu.VMEM((count, total), F32)],
        compiler_params=params(),
        cost_estimate=cost(10 * count * total * total, 16 * count * total),
        name="route",
    )(jnp.transpose(routes, (1, 2, 0)), jnp.transpose(route_weight, (1, 2, 0)))

    keep, slot, weight = lax.optimization_barrier((keep, slot, weight))
    mixed, normed = pl.pallas_call(
        mix_kernel,
        out_shape=[jax.ShapeDtypeStruct((unit, model), F32), jax.ShapeDtypeStruct((unit, model), BF)],
        compiler_params=params(),
        cost_estimate=cost(10 * unit * model, 16 * unit * model),
        name="mix",
    )(keep, residual_rows, norm_gain.reshape(1, model), *got)
    attn_out = pl.pallas_call(
        place_kernel,
        out_shape=jax.ShapeDtypeStruct((own, seqs, model), F32),
        compiler_params=params(VMEM_BYTES // 8),
        cost_estimate=cost(1, 8 * unit * model),
        name="place",
    )(mixed)

    along = [swap(normed, "exp", 2 * d) for d in range(1, line)]
    across = [normed] + [swap(normed, "seq", d) for d in range(1, count)]
    rows = [len(arrays) * unit for arrays in (across, along)]
    near, rest, corner = pl.pallas_call(
        functools.partial(gather_kernel, count, line - 1),
        in_specs=[vmem] * (count + line - 1) + [anywhere],
        out_specs=[vmem] * 3,
        out_shape=[jax.ShapeDtypeStruct((n, model), BF) for n in (*rows, unit)],
        compiler_params=params(VMEM_BYTES // 8),
        cost_estimate=cost(1, 4 * sum(rows) * model),
        name="gather",
    )(*across, *along, *in_hbm(attn_out))
    gate, up = pl.pallas_call(
        load_kernel,
        in_specs=[hbm, hbm, anywhere],
        out_specs=[vmem] * 2,
        out_shape=[pltpu.VMEM(w_gate.shape, BF), pltpu.VMEM(w_up.shape, BF)],
        scratch_shapes=[pltpu.SemaphoreType.DMA((2, 4))],
        compiler_params=params(VMEM_BYTES // 8),
        cost_estimate=cost(1, 4 * w_gate.size),
        name="load",
    )(*in_hbm(w_gate, w_up), rest)
    rests = [[rest]] + exchanged(rest, corner, count, *in_vmem(gate))
    half = count // 2
    slots = half * capacity

    def planned(first, parts):
        plan, arrays = [], [near, near_partner]
        for n, pieces in enumerate(parts):
            partners = [swap(piece, "exp", 1) for piece in pieces]
            for k, share in enumerate((pieces, partners)):
                plan.append((k, (first + n) * unit, unit))
                for piece in share:
                    plan.append((len(arrays), 0, piece.shape[0]))
                    arrays.append(piece)
        return plan, arrays

    near_partner = swap(near, "exp", 1)
    plan, arrays = planned(0, rests[:half])
    hidden = expert_half(0, slot, weight, gate, up, plan, arrays, None, slots)
    *rests[-1][-2:], hidden = lax.optimization_barrier((*rests[-1][-2:], hidden))
    plan, arrays = planned(half, rests[half:])
    hidden = expert_half(1, slot, weight, gate, up, plan, arrays, hidden, slots)
    return (attn_out, hidden)


def solution(mesh):
    placed = (
        P(("seq", "exp"), None, None),
        P(None, "seq", "exp"),
        P(None, "seq", "exp"),
        P(None, "seq", "exp"),
        P(None, "exp", "seq"),
        P("exp"),
        P("exp", None),
        P(),
        P(),
        P(),
        P("exp", "seq", None),
        P("exp", "seq", None),
    )
    return jax.shard_map(
        per_device,
        mesh=mesh,
        in_specs=placed,
        out_specs=(P(("seq", "exp"), None, None), P("exp", "seq", None)),
        check_vma=False,
    )
```

```python
import functools

import jax
import jax.numpy as jnp
from jax import lax
from jax.experimental import pallas as pl
from jax.experimental.pallas import tpu as pltpu
from jax.sharding import PartitionSpec as P

BF, F32 = jnp.bfloat16, jnp.float32
PRECISE = lax.Precision.HIGHEST
VMEM_BYTES = 16 * 1024 * 1024
NT = (((1,), (1,)), ((), ()))
TN = (((0,), (0,)), ((), ()))


def in_hbm(*arrays):
    return [pltpu.with_memory_space_constraint(array, pltpu.HBM) for array in arrays]


def in_vmem(*arrays):
    return [pltpu.with_memory_space_constraint(array, pltpu.VMEM) for array in arrays]


def swap(block, axis, distance, forward_only=False):
    devices = range(lax.axis_size(axis))
    route = [(i, i ^ distance) for i in devices if not forward_only or i < i ^ distance]
    return lax.ppermute(block, axis, route)


def mm(a, b, dims=(((1,), (0,)), ((), ()))):
    return lax.dot_general(a, b, dims, preferred_element_type=F32)


def halves(x):
    high = x.astype(BF)
    return high, (x - high.astype(F32)).astype(BF)


def thirds(x):
    high, rest = x.astype(BF), None
    rest = x - high.astype(F32)
    middle = rest.astype(BF)
    return high, middle, (rest - middle.astype(F32)).astype(BF)


def lower_triangle(size):
    return (
        lax.broadcasted_iota(jnp.int32, (size, size), 0) >= lax.broadcasted_iota(jnp.int32, (size, size), 1)
    )


def running_columns(log_decay):
    tri = lower_triangle(log_decay.shape[1]).astype(F32)
    return lax.dot_general(tri, log_decay, NT, precision=PRECISE, preferred_element_type=F32)


def running_rows(log_decay):
    tri = lower_triangle(log_decay.shape[1]).astype(F32)
    return lax.dot_general(log_decay, tri, NT, precision=PRECISE, preferred_element_type=F32)


def state_kernel(k_hbm, v_hbm, decay_hbm, proj_hbm, out_ref, proj_ref, k_ref, v_ref, decay_ref, sems):
    pairs = ((decay_hbm, decay_ref), (k_hbm, k_ref), (v_hbm, v_ref), (proj_hbm, proj_ref))
    copies = [pltpu.make_async_copy(source, to, sems.at[n]) for n, (source, to) in enumerate(pairs)]
    for copy in copies:
        copy.start()
    for copy in copies[:-1]:
        copy.wait()
    seqs, heads, size = decay_ref.shape
    width = k_ref.shape[2] // heads
    totals = []
    for b in range(seqs):
        columns = running_columns(decay_ref[b])
        tail = jnp.exp(columns[size - 1 : size, :] - columns)
        totals.append(jnp.broadcast_to(running_rows(decay_ref[b])[:, size - 1 : size], (heads, width)))
        for h in range(heads):
            part = slice(h * width, (h + 1) * width)
            value = v_ref[b, :, part]
            high, low = halves(k_ref[b, :, part].astype(F32) * tail[:, h : h + 1])
            at = (b * heads + h) * width
            out_ref[at : at + width, :] = (mm(high, value, TN) + mm(low, value, TN)).astype(BF)
    total = jnp.concatenate(totals, axis=0)
    pieces = [piece.astype(F32) for piece in thirds(total)]
    pieces.append(jnp.zeros_like(total))
    out_ref[seqs * heads * width :, :] = jnp.concatenate(pieces, axis=0).astype(BF)
    copies[-1].wait()


def inner_kernel(q_hbm, k_hbm, v_hbm, decay_hbm, residual_hbm, after, out_ref, q_ref, rows_ref, *scratch):
    k_ref, v_ref, decay_ref, residual_ref, sems = scratch
    pairs = (
        (decay_hbm, decay_ref),
        (q_hbm, q_ref),
        (k_hbm, k_ref),
        (v_hbm, v_ref),
        (residual_hbm, residual_ref),
    )
    copies = [pltpu.make_async_copy(source, to, sems.at[n]) for n, (source, to) in enumerate(pairs)]
    for copy in copies:
        copy.start()
    for copy in copies:
        copy.wait()
    own, seqs, _ = residual_ref.shape
    for b in range(seqs):
        rows_ref[b * own : (b + 1) * own, :] = residual_ref[:, b, :].astype(F32)
    _, heads, size = decay_ref.shape
    width = k_ref.shape[2] // heads
    causal = lower_triangle(size)
    for b in range(seqs):
        columns = running_columns(decay_ref[b])
        rows = running_rows(decay_ref[b])
        for h in range(heads):
            part = slice(h * width, (h + 1) * width)
            spread = columns[:, h : h + 1] - rows[h : h + 1, :]
            decay = jnp.where(causal, jnp.exp(jnp.where(causal, spread, 0.0)), 0.0)
            scores = mm(q_ref[b, :, part], k_ref[b, :, part], NT) * decay
            high, low = halves(scores)
            value = v_ref[b, :, part]
            out_ref[b, :, part] = mm(high, value) + mm(low, value)


def attend_kernel(count, line, *refs):
    q_ref, inner_ref, decay_ref, gain_ref = refs[:4]
    states = refs[4 : 3 + count]
    own_ref, partner_ref = refs[3 + count :]
    seqs, size, feat = q_ref.shape
    heads = decay_ref.shape[1]
    width = feat // heads
    me = lax.axis_index("seq")
    index = lax.axis_index("exp")
    each = seqs * heads
    base = each * width
    totals = []
    for state in states:
        three = state[base : base + 4 * each, :].astype(F32)
        totals.append(three[:each] + three[each : 2 * each] + three[2 * each : 3 * each])
    factors = []
    for first in range(1, count):
        later = jnp.zeros_like(totals[0])
        for second in range(1, count):
            between = ((me ^ first) < (me ^ second)) & ((me ^ second) < me)
            later = later + jnp.where(between, totals[second - 1], 0.0)
        factors.append(jnp.where((me ^ first) < me, jnp.exp(later), 0.0))
    rows = []
    for b in range(seqs):
        grown = jnp.exp(running_columns(decay_ref[b]))
        parts = []
        for h in range(heads):
            part = slice(h * width, (h + 1) * width)
            n = b * heads + h
            incoming = jnp.zeros((width, width), F32)
            for state, factor in zip(states, factors):
                incoming = incoming + factor[n : n + 1, :] * state[n * width : (n + 1) * width, :].astype(F32)
            high, low = halves(incoming)
            query = q_ref[b, :, part]
            raw = inner_ref[b, :, part] + grown[:, h : h + 1] * (mm(query, high) + mm(query, low))
            meansq = jnp.mean(raw * raw, axis=-1, keepdims=True)
            parts.append((raw * lax.rsqrt(meansq + 1e-06) * gain_ref[:, part]).astype(BF))
        rows.append(jnp.concatenate(parts, axis=1))
    attention = jnp.concatenate(rows, axis=0)
    total = seqs * size
    own = size // (2 * line)
    to = lax.broadcasted_iota(jnp.int32, (total, total), 0)
    source = source_position(to // (total // 2), (to // (seqs * own)) % line, to % own, index, own)
    source = source + size * ((to // own) % seqs)
    pick = (source == lax.broadcasted_iota(jnp.int32, (total, total), 1)).astype(BF)
    attention = mm(pick, attention).astype(BF)
    own_ref[...] = attention[: total // 2, :]
    partner_ref[...] = attention[total // 2 :, :]


def project_kernel(own_ref, partner_ref, proj_ref, partner_proj_ref, keep_ref, *send_refs):
    rows, model = keep_ref.shape
    tile = column_tile(model)
    for n in range(model // tile):
        columns = slice(n * tile, (n + 1) * tile)
        product = mm(own_ref[...], proj_ref[:, columns]) + mm(partner_ref[...], partner_proj_ref[:, columns])
        keep_ref[:, columns] = product[:rows, :]
        for d, send_ref in enumerate(send_refs, start=1):
            send_ref[:, columns] = product[d * rows : (d + 1) * rows, :].astype(BF)


def column_tile(model):
    return max(t for t in range(128, 1025, 128) if model % t == 0)


def source_position(flip, distance, place, index, own):
    return own * (2 * ((index // 2) ^ distance) + ((index % 2) ^ flip)) + place


def mix_kernel(kept_ref, residual_ref, gain_ref, *refs):
    mixed_ref, normed_ref = refs[-2:]
    mixed = residual_ref[...] + kept_ref[...]
    for got_ref in refs[:-2]:
        mixed = mixed + got_ref[...].astype(F32)
    mixed_ref[...] = mixed
    meansq = jnp.mean(mixed * mixed, axis=-1, keepdims=True)
    normed_ref[...] = (mixed * lax.rsqrt(meansq + 1e-06) * gain_ref[...]).astype(BF)


def place_kernel(mixed_ref, out_ref):
    own, seqs, _ = out_ref.shape
    for b in range(seqs):
        out_ref[:, b, :] = mixed_ref[b * own : (b + 1) * own, :]


def load_kernel(gate_hbm, up_hbm, after, gate_ref, up_ref, sems):
    parts = sems.shape[1]
    rows = gate_ref.shape[1] // parts
    copies = []
    for m, (source, to) in enumerate(((gate_hbm, gate_ref), (up_hbm, up_ref))):
        for n in range(parts):
            part = pl.ds(n * rows, rows)
            copies.append(pltpu.make_async_copy(source.at[0, part], to.at[0, part], sems.at[m, n]))
            copies[-1].start()
    for copy in copies:
        copy.wait()


def gather_kernel(first, second, *refs):
    near_ref, rest_ref, corner_ref = refs[-3:]
    for to, sources in ((near_ref, refs[:first]), (rest_ref, refs[first : first + second])):
        at = 0
        for source in sources:
            to[at : at + source.shape[0], :] = source[...]
            at += source.shape[0]
    corner_ref[...] = refs[first - 1][...]


def halves_kernel(one_ref, two_ref, corner_ref, after, low_ref, high_ref):
    half = low_ref.shape[0]
    first = one_ref.shape[0] - 2 * half
    low_ref[...] = one_ref[first : first + half, :]
    high_ref[...] = two_ref[first + half :, :]


def exchanged(block, corner, count, after):
    rows, unit = block.shape[0], corner.shape[0]
    if count != 4 or unit % 16 != 0 or (rows - unit) % 32 != 0 or rows == unit:
        return [[swap(block, "seq", d)] for d in range(1, count)]
    one, two = swap(block, "seq", 1), swap(block, "seq", 2)
    corner = swap(corner, "exp", 2)
    vmem, anywhere = pl.BlockSpec(memory_space=pltpu.VMEM), pl.BlockSpec(memory_space=pl.ANY)
    low, high = pl.pallas_call(
        halves_kernel,
        in_specs=[vmem] * 3 + [anywhere],
        out_specs=[vmem] * 2,
        out_shape=[jax.ShapeDtypeStruct(((rows - unit) // 2, block.shape[1]), block.dtype)] * 2,
        compiler_params=params(VMEM_BYTES // 8),
        cost_estimate=cost(1, 4 * block.size),
        name="halves",
    )(one, two, corner, after)
    one, two, low, high = lax.optimization_barrier((one, two, low, high))
    return [[one], [two], [corner, swap(low, "seq", 2), swap(high, "seq", 1)]]


def route_kernel(own, routes_ref, weights_ref, slot_ref, weight_ref, a_ref, b_ref):
    seqs, tops, _ = routes_ref.shape
    count, total = slot_ref.shape
    size = total // seqs
    me = lax.axis_index("seq")
    index = lax.axis_index("exp")
    line = size // (2 * own)
    lines, shares = [], []
    for c in range(count):
        part = slice(c * size, (c + 1) * size)
        hit, share = [], []
        for b in range(seqs):
            hits = [routes_ref[b, k : k + 1, part] == index for k in range(tops)]
            hit.append(sum(jnp.where(one, 1.0, 0.0) for one in hits))
            share.append(sum(jnp.where(one, weights_ref[b, k : k + 1, part], 0.0) for k, one in enumerate(hits)))
        lines.append(jnp.concatenate(hit, axis=1))
        shares.append(jnp.concatenate(share, axis=1))
    chosen = jnp.concatenate(lines, axis=0).astype(BF)
    weight = jnp.concatenate(shares, axis=0)
    to = lax.broadcasted_iota(jnp.int32, (total, total), 1)
    row = source_position(to // (total // 2), (to // (seqs * own)) % line, to % own, index, own) * seqs
    row = row + (to // own) % seqs
    origin = lax.broadcasted_iota(jnp.int32, (total, total), 0)
    origin = (origin % size) * seqs + origin // size
    rank = mm(chosen, (origin <= row).astype(BF)) - 1.0
    same = (origin == row).astype(BF)
    picked = mm(chosen, same) > 0.5
    a_ref[...] = jnp.where(picked, rank.astype(jnp.int32), -1)
    high, middle, low = thirds(weight)
    b_ref[...] = mm(high, same) + mm(middle, same) + mm(low, same)
    for d in range(count):
        slot_ref[d : d + 1, :] = a_ref[pl.ds(me ^ d, 1), :]
        weight_ref[d : d + 1, :] = b_ref[pl.ds(me ^ d, 1), :]


def expert_kernel(plan, arrays, lines, slot_ref, weight_ref, gate_ref, up_ref, *refs):
    array_refs, (out_hbm, rows_ref, out_ref, sems) = refs[:arrays], refs[-4:]
    total = slot_ref.shape[1]
    blocks = len(lines)
    slots, width = rows_ref.shape
    me = lax.axis_index("seq")
    tile = out_ref.shape[1]
    capacity = slots // blocks
    apart = capacity % 128 == 0
    numbers = lax.broadcasted_iota(jnp.int32, (slots, total), 0)
    picks = []
    for n, line in enumerate(lines):
        place = n if apart else (me ^ line) % blocks
        slot = slot_ref[line : line + 1, :]
        picks.append((jnp.where(slot < 0, slot, slot + place * capacity) == numbers).astype(BF))
    weight = jnp.concatenate([weight_ref[line : line + 1, :] for line in lines], axis=1)
    parts = [part.astype(F32) for part in thirds(weight)] + [jnp.zeros((5, blocks * total), F32)]
    parts = jnp.concatenate(parts, axis=0).astype(BF)
    scale = jnp.sum(mm(parts, jnp.concatenate(picks, axis=1), NT), axis=0, keepdims=True)

    step = column_tile(width)
    for at in range(0, width, step):
        part = slice(at, at + step)
        rows = []
        for pieces in plan:
            rows.append([array_refs[m][first : first + height, part] for m, first, height in pieces])
        if apart:
            for n, pick in enumerate(picks):
                own = slice(n * capacity, (n + 1) * capacity)
                rows_ref[own, part] = mm(pick[own], jnp.concatenate(rows[n], axis=0)).astype(BF)
        else:
            rows = jnp.concatenate([piece for pieces in rows for piece in pieces], axis=0)
            rows_ref[:, part] = mm(jnp.concatenate(picks, axis=1), rows).astype(BF)

    targets = [(slice(0, slots), (me ^ lines[0]) // blocks)]
    if apart:
        targets = [(slice(n * capacity, (n + 1) * capacity), me ^ line) for n, line in enumerate(lines)]
    copies = []
    for step in range(out_ref.shape[0]):
        part = slice(step * tile, (step + 1) * tile)
        gate = mm(gate_ref[0, part, :], rows_ref[...], NT)
        up = mm(up_ref[0, part, :], rows_ref[...], NT)
        out_ref[step] = scale * (gate / (1.0 + jnp.exp(-gate))) * up
        for columns, place in targets:
            size = columns.stop - columns.start
            to = out_hbm.at[0, part, pl.ds(pl.multiple_of(place * size, size), size)]
            copies.append(pltpu.make_async_copy(out_ref.at[step, :, columns], to, sems.at[len(copies)]))
            copies[-1].start()
    for copy in copies:
        copy.wait()


def params(vmem=VMEM_BYTES):
    return pltpu.CompilerParams(vmem_limit_bytes=vmem)


def cost(flops, bytes_accessed, transcendentals=0):
    return pl.CostEstimate(flops=int(flops), bytes_accessed=int(bytes_accessed), transcendentals=int(transcendentals))


def whole(shape):
    return pl.BlockSpec(shape, lambda *_: (0,) * len(shape))


def experts(lines, capacity, slot, weight, w_gate, w_up, plan, arrays, previous):
    units, width = w_gate.shape[1:]
    tile = max(size for size in range(16, 385, 16) if units % size == 0)
    steps = units // tile
    slots = len(lines) * capacity
    carried = [] if previous is None else [previous]
    vmem, hbm = pl.BlockSpec(memory_space=pltpu.VMEM), pl.BlockSpec(memory_space=pltpu.HBM)
    return pl.pallas_call(
        functools.partial(expert_kernel, plan, len(arrays), lines),
        in_specs=[vmem] * (4 + len(arrays)) + [hbm] * len(carried),
        out_specs=hbm,
        out_shape=jax.ShapeDtypeStruct((1, units, slot.shape[0] * capacity), F32),
        scratch_shapes=[
            pltpu.VMEM((slots, width), BF),
            pltpu.VMEM((steps, tile, slots), F32),
            pltpu.SemaphoreType.DMA((steps * len(lines),)),
        ],
        input_output_aliases={4 + len(arrays): 0} if carried else {},
        compiler_params=params(),
        cost_estimate=cost(4 * units * width * slots, 2 * slots * width),
        name="experts",
    )(slot, weight, *in_vmem(w_gate, w_up), *arrays, *carried)


def per_device(
    residual,
    queries,
    key_vecs,
    value_vecs,
    log_decay,
    head_gain,
    out_proj,
    norm_gain,
    routes,
    route_weight,
    w_gate,
    w_up,
):
    count, owners = lax.axis_size("seq"), lax.axis_size("exp")
    line = owners // 2
    me = lax.axis_index("seq")
    seqs, size, feat = queries.shape
    heads = log_decay.shape[1]
    width = feat // heads
    own, _, model = residual.shape
    unit = own * seqs
    total = size * seqs
    capacity = 8 * size // owners

    vmem, hbm, anywhere = (pl.BlockSpec(memory_space=space) for space in (pltpu.VMEM, pltpu.HBM, pl.ANY))

    states, proj = pl.pallas_call(
        state_kernel,
        in_specs=[hbm] * 4,
        out_specs=[vmem] * 2,
        out_shape=[
            pltpu.VMEM((seqs * heads * (width + 4), width), BF),
            pltpu.VMEM(out_proj.shape, BF),
        ],
        scratch_shapes=[
            pltpu.VMEM(key_vecs.shape, BF),
            pltpu.VMEM(value_vecs.shape, BF),
            pltpu.VMEM(log_decay.shape, F32),
            pltpu.SemaphoreType.DMA((4,)),
        ],
        compiler_params=params(),
        cost_estimate=cost(4 * total * feat * width, 6 * total * feat),
        name="states",
    )(*in_hbm(key_vecs, value_vecs, log_decay, out_proj))
    arrived = [swap(states, "seq", d) for d in range(1, count)]

    inner, query, residual_rows = pl.pallas_call(
        inner_kernel,
        in_specs=[hbm] * 5 + [anywhere],
        out_specs=[vmem] * 3,
        out_shape=[
            pltpu.VMEM((seqs, size, feat), F32),
            pltpu.VMEM(queries.shape, BF),
            pltpu.VMEM((unit, model), F32),
        ],
        scratch_shapes=[
            pltpu.VMEM(key_vecs.shape, BF),
            pltpu.VMEM(value_vecs.shape, BF),
            pltpu.VMEM(log_decay.shape, F32),
            pltpu.VMEM(residual.shape, BF),
            pltpu.SemaphoreType.DMA((5,)),
        ],
        compiler_params=params(),
        cost_estimate=cost(6 * total * feat * size, 10 * total * feat),
        name="inner",
    )(*in_hbm(queries, key_vecs, value_vecs, log_decay, residual), *in_vmem(states))

    mine, theirs = pl.pallas_call(
        functools.partial(attend_kernel, count, line),
        in_specs=[vmem] * (4 + count - 1),
        out_specs=[vmem] * 2,
        out_shape=[jax.ShapeDtypeStruct((total // 2, feat), BF)] * 2,
        compiler_params=params(),
        cost_estimate=cost(6 * total * feat * width, 10 * total * feat),
        name="attend",
    )(*in_vmem(query, inner), log_decay, head_gain.reshape(1, feat), *arrived)

    keep, *sends = pl.pallas_call(
        project_kernel,
        in_specs=[vmem] * 4,
        out_specs=[vmem] * line,
        out_shape=[jax.ShapeDtypeStruct((unit, model), F32)]
        + [jax.ShapeDtypeStruct((unit, model), BF)] * (line - 1),
        compiler_params=params(),
        cost_estimate=cost(2 * total * feat * model, 4 * feat * model + 3 * total * model),
        name="project",
    )(mine, swap(theirs, "exp", 1), *in_vmem(proj), swap(proj, "exp", 1))
    got = [swap(send, "exp", 2 * d) for d, send in enumerate(sends, start=1)]

    routes, route_weight, keep = lax.optimization_barrier((routes, route_weight, keep))
    slot, weight = pl.pallas_call(
        functools.partial(route_kernel, own),
        out_shape=[jax.ShapeDtypeStruct((count, total), jnp.int32), jax.ShapeDtypeStruct((count, total), F32)],
        scratch_shapes=[pltpu.VMEM((count, total), jnp.int32), pltpu.VMEM((count, total), F32)],
        compiler_params=params(),
        cost_estimate=cost(10 * count * total * total, 16 * count * total),
        name="route",
    )(jnp.transpose(routes, (1, 2, 0)), jnp.transpose(route_weight, (1, 2, 0)))

    keep, slot, weight = lax.optimization_barrier((keep, slot, weight))
    mixed, normed = pl.pallas_call(
        mix_kernel,
        out_shape=[jax.ShapeDtypeStruct((unit, model), F32), jax.ShapeDtypeStruct((unit, model), BF)],
        compiler_params=params(),
        cost_estimate=cost(10 * unit * model, 16 * unit * model),
        name="mix",
    )(keep, residual_rows, norm_gain.reshape(1, model), *reversed(got))
    attn_out = pl.pallas_call(
        place_kernel,
        out_shape=jax.ShapeDtypeStruct((own, seqs, model), F32),
        compiler_params=params(VMEM_BYTES // 8),
        cost_estimate=cost(1, 8 * unit * model),
        name="place",
    )(mixed)

    along = [swap(normed, "exp", 2 * d) for d in range(1, line)]
    across = [normed] + [swap(normed, "seq", d) for d in range(1, count)]
    rows = [len(arrays) * unit for arrays in (across, along)]
    near, rest, corner = pl.pallas_call(
        functools.partial(gather_kernel, count, line - 1),
        in_specs=[vmem] * (count + line - 1) + [anywhere],
        out_specs=[vmem] * 3,
        out_shape=[jax.ShapeDtypeStruct((n, model), BF) for n in (*rows, unit)],
        compiler_params=params(VMEM_BYTES // 8),
        cost_estimate=cost(1, 4 * sum(rows) * model),
        name="gather",
    )(*across, *along, *in_hbm(attn_out))
    gate, up = pl.pallas_call(
        load_kernel,
        in_specs=[hbm, hbm, anywhere],
        out_specs=[vmem] * 2,
        out_shape=[pltpu.VMEM(w_gate.shape, BF), pltpu.VMEM(w_up.shape, BF)],
        scratch_shapes=[pltpu.SemaphoreType.DMA((2, 4))],
        compiler_params=params(VMEM_BYTES // 8),
        cost_estimate=cost(1, 4 * w_gate.size),
        name="load",
    )(*in_hbm(w_gate, w_up), rest)
    near_partner = swap(near, "exp", 1)

    def computed(lines, parts, previous):
        plan, arrays = [], [near, near_partner]
        for n, pieces in zip(lines, parts):
            partners = [swap(piece, "exp", 1) for piece in pieces]
            plan.append([])
            for k, share in enumerate((pieces, partners)):
                plan[-1].append((k, n * unit, unit))
                for piece in share:
                    plan[-1].append((len(arrays), 0, piece.shape[0]))
                    arrays.append(piece)
        return experts(lines, capacity, slot, weight, gate, up, plan, arrays, previous)

    half = count // 2
    rests = [[rest]] + exchanged(rest, corner, count, *in_vmem(gate))
    hidden = computed(range(half), rests[:half], None)
    *rests[-1][-2:], hidden = lax.optimization_barrier((*rests[-1][-2:], hidden))
    hidden = computed(range(half, count), rests[half:], hidden)
    return (attn_out, hidden)


def solution(mesh):
    placed = (
        P(("seq", "exp"), None, None),
        P(None, "seq", "exp"),
        P(None, "seq", "exp"),
        P(None, "seq", "exp"),
        P(None, "exp", "seq"),
        P("exp"),
        P("exp", None),
        P(),
        P(),
        P(),
        P("exp", "seq", None),
        P("exp", "seq", None),
    )
    return jax.shard_map(
        per_device,
        mesh=mesh,
        in_specs=placed,
        out_specs=(P(("seq", "exp"), None, None), P("exp", "seq", None)),
        check_vma=False,
    )
```

```python
import functools

import jax
import jax.numpy as jnp
from jax import lax
from jax.experimental import pallas as pl
from jax.experimental.pallas import tpu as pltpu
from jax.sharding import PartitionSpec as P

BF, F32 = jnp.bfloat16, jnp.float32
PRECISE = lax.Precision.HIGHEST
VMEM_BYTES = 16 * 1024 * 1024
NT = (((1,), (1,)), ((), ()))
TN = (((0,), (0,)), ((), ()))


def in_hbm(*arrays):
    return [pltpu.with_memory_space_constraint(array, pltpu.HBM) for array in arrays]


def in_vmem(*arrays):
    return [pltpu.with_memory_space_constraint(array, pltpu.VMEM) for array in arrays]


def swap(block, axis, distance, forward_only=False):
    devices = range(lax.axis_size(axis))
    route = [(i, i ^ distance) for i in devices if not forward_only or i < i ^ distance]
    return lax.ppermute(block, axis, route)


def mm(a, b, dims=(((1,), (0,)), ((), ()))):
    return lax.dot_general(a, b, dims, preferred_element_type=F32)


def halves(x):
    high = x.astype(BF)
    return high, (x - high.astype(F32)).astype(BF)


def thirds(x):
    high, rest = x.astype(BF), None
    rest = x - high.astype(F32)
    middle = rest.astype(BF)
    return high, middle, (rest - middle.astype(F32)).astype(BF)


def lower_triangle(size):
    return (
        lax.broadcasted_iota(jnp.int32, (size, size), 0) >= lax.broadcasted_iota(jnp.int32, (size, size), 1)
    )


def running_columns(log_decay):
    tri = lower_triangle(log_decay.shape[1]).astype(F32)
    return lax.dot_general(tri, log_decay, NT, precision=PRECISE, preferred_element_type=F32)


def running_rows(log_decay):
    tri = lower_triangle(log_decay.shape[1]).astype(F32)
    return lax.dot_general(log_decay, tri, NT, precision=PRECISE, preferred_element_type=F32)


def state_kernel(k_hbm, v_hbm, decay_hbm, proj_hbm, out_ref, proj_ref, k_ref, v_ref, decay_ref, sems):
    pairs = ((decay_hbm, decay_ref), (k_hbm, k_ref), (v_hbm, v_ref), (proj_hbm, proj_ref))
    copies = [pltpu.make_async_copy(source, to, sems.at[n]) for n, (source, to) in enumerate(pairs)]
    for copy in copies:
        copy.start()
    for copy in copies[:-1]:
        copy.wait()
    seqs, heads, size = decay_ref.shape
    width = k_ref.shape[2] // heads
    totals = []
    for b in range(seqs):
        columns = running_columns(decay_ref[b])
        tail = jnp.exp(columns[size - 1 : size, :] - columns)
        totals.append(jnp.broadcast_to(running_rows(decay_ref[b])[:, size - 1 : size], (heads, width)))
        for h in range(heads):
            part = slice(h * width, (h + 1) * width)
            value = v_ref[b, :, part]
            high, low = halves(k_ref[b, :, part].astype(F32) * tail[:, h : h + 1])
            at = (b * heads + h) * width
            out_ref[at : at + width, :] = (mm(high, value, TN) + mm(low, value, TN)).astype(BF)
    total = jnp.concatenate(totals, axis=0)
    pieces = [piece.astype(F32) for piece in thirds(total)]
    pieces.append(jnp.zeros_like(total))
    out_ref[seqs * heads * width :, :] = jnp.concatenate(pieces, axis=0).astype(BF)
    copies[-1].wait()


def inner_kernel(q_hbm, k_hbm, v_hbm, decay_hbm, residual_hbm, after, out_ref, q_ref, rows_ref, *scratch):
    k_ref, v_ref, decay_ref, residual_ref, sems = scratch
    pairs = (
        (decay_hbm, decay_ref),
        (q_hbm, q_ref),
        (k_hbm, k_ref),
        (v_hbm, v_ref),
        (residual_hbm, residual_ref),
    )
    copies = [pltpu.make_async_copy(source, to, sems.at[n]) for n, (source, to) in enumerate(pairs)]
    for copy in copies:
        copy.start()
    for copy in copies:
        copy.wait()
    own, seqs, _ = residual_ref.shape
    for b in range(seqs):
        rows_ref[b * own : (b + 1) * own, :] = residual_ref[:, b, :].astype(F32)
    _, heads, size = decay_ref.shape
    width = k_ref.shape[2] // heads
    causal = lower_triangle(size)
    for b in range(seqs):
        columns = running_columns(decay_ref[b])
        rows = running_rows(decay_ref[b])
        for h in range(heads):
            part = slice(h * width, (h + 1) * width)
            spread = columns[:, h : h + 1] - rows[h : h + 1, :]
            decay = jnp.where(causal, jnp.exp(jnp.where(causal, spread, 0.0)), 0.0)
            scores = mm(q_ref[b, :, part], k_ref[b, :, part], NT) * decay
            high, low = halves(scores)
            value = v_ref[b, :, part]
            out_ref[b, :, part] = mm(high, value) + mm(low, value)


def attend_kernel(count, line, *refs):
    q_ref, inner_ref, decay_ref, gain_ref = refs[:4]
    states = refs[4 : 3 + count]
    own_ref, partner_ref = refs[3 + count :]
    seqs, size, feat = q_ref.shape
    heads = decay_ref.shape[1]
    width = feat // heads
    me = lax.axis_index("seq")
    index = lax.axis_index("exp")
    each = seqs * heads
    base = each * width
    totals = []
    for state in states:
        three = state[base : base + 4 * each, :].astype(F32)
        totals.append(three[:each] + three[each : 2 * each] + three[2 * each : 3 * each])
    factors = []
    for first in range(1, count):
        later = jnp.zeros_like(totals[0])
        for second in range(1, count):
            between = ((me ^ first) < (me ^ second)) & ((me ^ second) < me)
            later = later + jnp.where(between, totals[second - 1], 0.0)
        factors.append(jnp.where((me ^ first) < me, jnp.exp(later), 0.0))
    rows = []
    for b in range(seqs):
        grown = jnp.exp(running_columns(decay_ref[b]))
        parts = []
        for h in range(heads):
            part = slice(h * width, (h + 1) * width)
            n = b * heads + h
            incoming = jnp.zeros((width, width), F32)
            for state, factor in zip(states, factors):
                incoming = incoming + factor[n : n + 1, :] * state[n * width : (n + 1) * width, :].astype(F32)
            high, low = halves(incoming)
            query = q_ref[b, :, part]
            raw = inner_ref[b, :, part] + grown[:, h : h + 1] * (mm(query, high) + mm(query, low))
            meansq = jnp.mean(raw * raw, axis=-1, keepdims=True)
            parts.append((raw * lax.rsqrt(meansq + 1e-06) * gain_ref[:, part]).astype(BF))
        rows.append(jnp.concatenate(parts, axis=1))
    attention = jnp.concatenate(rows, axis=0)
    total = seqs * size
    own = size // (2 * line)
    to = lax.broadcasted_iota(jnp.int32, (total, total), 0)
    source = source_position(to // (total // 2), (to // (seqs * own)) % line, to % own, index, own)
    source = source + size * ((to // own) % seqs)
    pick = (source == lax.broadcasted_iota(jnp.int32, (total, total), 1)).astype(BF)
    attention = mm(pick, attention).astype(BF)
    own_ref[...] = attention[: total // 2, :]
    partner_ref[...] = attention[total // 2 :, :]


def project_kernel(own_ref, partner_ref, proj_ref, partner_proj_ref, keep_ref, *send_refs):
    rows, model = keep_ref.shape
    tile = column_tile(model)
    for n in range(model // tile):
        columns = slice(n * tile, (n + 1) * tile)
        product = mm(own_ref[...], proj_ref[:, columns]) + mm(partner_ref[...], partner_proj_ref[:, columns])
        keep_ref[:, columns] = product[:rows, :]
        for d, send_ref in enumerate(send_refs, start=1):
            send_ref[:, columns] = product[d * rows : (d + 1) * rows, :].astype(BF)


def column_tile(model):
    return max(t for t in range(128, 1025, 128) if model % t == 0)


def source_position(flip, distance, place, index, own):
    return own * (2 * ((index // 2) ^ distance) + ((index % 2) ^ flip)) + place


def mix_kernel(kept_ref, residual_ref, gain_ref, after, *refs):
    mixed_ref, normed_ref = refs[-2:]
    mixed = residual_ref[...] + kept_ref[...]
    for got_ref in refs[:-2]:
        mixed = mixed + got_ref[...].astype(F32)
    mixed_ref[...] = mixed
    meansq = jnp.mean(mixed * mixed, axis=-1, keepdims=True)
    normed_ref[...] = (mixed * lax.rsqrt(meansq + 1e-06) * gain_ref[...]).astype(BF)


def place_kernel(mixed_ref, out_ref):
    own, seqs, _ = out_ref.shape
    for b in range(seqs):
        out_ref[:, b, :] = mixed_ref[b * own : (b + 1) * own, :]


def load_kernel(gate_hbm, up_hbm, after, gate_ref, up_ref, sems):
    parts = sems.shape[1]
    rows = gate_ref.shape[1] // parts
    copies = []
    for m, (source, to) in enumerate(((gate_hbm, gate_ref), (up_hbm, up_ref))):
        for n in range(parts):
            part = pl.ds(n * rows, rows)
            copies.append(pltpu.make_async_copy(source.at[0, part], to.at[0, part], sems.at[m, n]))
            copies[-1].start()
    for copy in copies:
        copy.wait()


def gather_kernel(plans, *refs):
    for to, plan in zip(refs[-len(plans) :], plans):
        at = 0
        for number, first, height in plan:
            to[at : at + height, :] = refs[number][first : first + height, :]
            at += height


def halves_kernel(one_ref, two_ref, corner_ref, after, low_ref, high_ref):
    half = low_ref.shape[0]
    first = one_ref.shape[0] - 2 * half
    low_ref[...] = one_ref[first : first + half, :]
    high_ref[...] = two_ref[first + half :, :]


def exchanged(block, corner, unit, after):
    rows, head = block.shape[0], unit // 2
    half = (rows - head) // 2
    one, two = swap(block, "seq", 1), swap(block, "seq", 2)
    corner = swap(corner, "exp", 2)
    vmem, anywhere = pl.BlockSpec(memory_space=pltpu.VMEM), pl.BlockSpec(memory_space=pl.ANY)
    low, high = pl.pallas_call(
        halves_kernel,
        in_specs=[vmem] * 3 + [anywhere],
        out_specs=[vmem] * 2,
        out_shape=[jax.ShapeDtypeStruct((half, block.shape[1]), block.dtype)] * 2,
        compiler_params=params(VMEM_BYTES // 8),
        cost_estimate=cost(1, 4 * block.size),
        name="halves",
    )(one, two, corner, after)
    one, two, low, high = lax.optimization_barrier((one, two, low, high))
    far = [(swap(low, "seq", 2), 0, half), (swap(high, "seq", 1), 0, half)]
    return [
        [(corner, 0, head), (one, 0, rows)],
        [(corner, head, head), (two, 0, rows)],
        [(corner, 2 * head, unit)] + far,
    ]


def route_kernel(own, routes_ref, weights_ref, slot_ref, weight_ref, a_ref, b_ref):
    seqs, tops, _ = routes_ref.shape
    count, total = slot_ref.shape
    size = total // seqs
    me = lax.axis_index("seq")
    index = lax.axis_index("exp")
    line = size // (2 * own)
    lines, shares = [], []
    for c in range(count):
        part = slice(c * size, (c + 1) * size)
        hit, share = [], []
        for b in range(seqs):
            hits = [routes_ref[b, k : k + 1, part] == index for k in range(tops)]
            hit.append(sum(jnp.where(one, 1.0, 0.0) for one in hits))
            share.append(sum(jnp.where(one, weights_ref[b, k : k + 1, part], 0.0) for k, one in enumerate(hits)))
        lines.append(jnp.concatenate(hit, axis=1))
        shares.append(jnp.concatenate(share, axis=1))
    chosen = jnp.concatenate(lines, axis=0).astype(BF)
    weight = jnp.concatenate(shares, axis=0)
    to = lax.broadcasted_iota(jnp.int32, (total, total), 1)
    row = source_position(to // (total // 2), (to // (seqs * own)) % line, to % own, index, own) * seqs
    row = row + (to // own) % seqs
    origin = lax.broadcasted_iota(jnp.int32, (total, total), 0)
    origin = (origin % size) * seqs + origin // size
    rank = mm(chosen, (origin <= row).astype(BF)) - 1.0
    same = (origin == row).astype(BF)
    picked = mm(chosen, same) > 0.5
    a_ref[...] = jnp.where(picked, rank.astype(jnp.int32), -1)
    high, middle, low = thirds(weight)
    b_ref[...] = mm(high, same) + mm(middle, same) + mm(low, same)
    for d in range(count):
        slot_ref[d : d + 1, :] = a_ref[pl.ds(me ^ d, 1), :]
        weight_ref[d : d + 1, :] = b_ref[pl.ds(me ^ d, 1), :]


def expert_kernel(plan, arrays, lines, slot_ref, weight_ref, gate_ref, up_ref, *refs):
    array_refs, (out_hbm, rows_ref, out_ref, sems) = refs[:arrays], refs[-4:]
    total = slot_ref.shape[1]
    blocks = len(lines)
    slots, width = rows_ref.shape
    me = lax.axis_index("seq")
    tile = out_ref.shape[1]
    capacity = slots // blocks
    apart = capacity % 128 == 0
    numbers = lax.broadcasted_iota(jnp.int32, (slots, total), 0)
    picks = []
    for n, line in enumerate(lines):
        place = n if apart else (me ^ line) % blocks
        slot = slot_ref[line : line + 1, :]
        picks.append((jnp.where(slot < 0, slot, slot + place * capacity) == numbers).astype(BF))
    weight = jnp.concatenate([weight_ref[line : line + 1, :] for line in lines], axis=1)
    parts = [part.astype(F32) for part in thirds(weight)] + [jnp.zeros((5, blocks * total), F32)]
    parts = jnp.concatenate(parts, axis=0).astype(BF)
    scale = jnp.sum(mm(parts, jnp.concatenate(picks, axis=1), NT), axis=0, keepdims=True)

    step = column_tile(width)
    for at in range(0, width, step):
        part = slice(at, at + step)
        rows = []
        for pieces in plan:
            rows.append([array_refs[m][first : first + height, part] for m, first, height in pieces])
        if apart:
            for n, pick in enumerate(picks):
                own = slice(n * capacity, (n + 1) * capacity)
                rows_ref[own, part] = mm(pick[own], jnp.concatenate(rows[n], axis=0)).astype(BF)
        else:
            rows = jnp.concatenate([piece for pieces in rows for piece in pieces], axis=0)
            rows_ref[:, part] = mm(jnp.concatenate(picks, axis=1), rows).astype(BF)

    targets = [(slice(0, slots), (me ^ lines[0]) // blocks)]
    if apart:
        targets = [(slice(n * capacity, (n + 1) * capacity), me ^ line) for n, line in enumerate(lines)]
    copies = []
    for step in range(out_ref.shape[0]):
        part = slice(step * tile, (step + 1) * tile)
        gate = mm(gate_ref[0, part, :], rows_ref[...], NT)
        up = mm(up_ref[0, part, :], rows_ref[...], NT)
        out_ref[step] = scale * (gate / (1.0 + jnp.exp(-gate))) * up
        for columns, place in targets:
            size = columns.stop - columns.start
            to = out_hbm.at[0, part, pl.ds(pl.multiple_of(place * size, size), size)]
            copies.append(pltpu.make_async_copy(out_ref.at[step, :, columns], to, sems.at[len(copies)]))
            copies[-1].start()
    for copy in copies:
        copy.wait()


def params(vmem=VMEM_BYTES):
    return pltpu.CompilerParams(vmem_limit_bytes=vmem)


def cost(flops, bytes_accessed, transcendentals=0):
    return pl.CostEstimate(flops=int(flops), bytes_accessed=int(bytes_accessed), transcendentals=int(transcendentals))


def whole(shape):
    return pl.BlockSpec(shape, lambda *_: (0,) * len(shape))


def experts(lines, capacity, slot, weight, w_gate, w_up, plan, arrays, previous):
    units, width = w_gate.shape[1:]
    tile = max(size for size in range(16, 385, 16) if units % size == 0)
    steps = units // tile
    slots = len(lines) * capacity
    carried = [] if previous is None else [previous]
    vmem, hbm = pl.BlockSpec(memory_space=pltpu.VMEM), pl.BlockSpec(memory_space=pltpu.HBM)
    return pl.pallas_call(
        functools.partial(expert_kernel, plan, len(arrays), lines),
        in_specs=[vmem] * (4 + len(arrays)) + [hbm] * len(carried),
        out_specs=hbm,
        out_shape=jax.ShapeDtypeStruct((1, units, slot.shape[0] * capacity), F32),
        scratch_shapes=[
            pltpu.VMEM((slots, width), BF),
            pltpu.VMEM((steps, tile, slots), F32),
            pltpu.SemaphoreType.DMA((steps * len(lines),)),
        ],
        input_output_aliases={4 + len(arrays): 0} if carried else {},
        compiler_params=params(),
        cost_estimate=cost(4 * units * width * slots, 2 * slots * width),
        name="experts",
    )(slot, weight, *in_vmem(w_gate, w_up), *arrays, *carried)


def per_device(
    residual,
    queries,
    key_vecs,
    value_vecs,
    log_decay,
    head_gain,
    out_proj,
    norm_gain,
    routes,
    route_weight,
    w_gate,
    w_up,
):
    count, owners = lax.axis_size("seq"), lax.axis_size("exp")
    line = owners // 2
    me = lax.axis_index("seq")
    seqs, size, feat = queries.shape
    heads = log_decay.shape[1]
    width = feat // heads
    own, _, model = residual.shape
    unit = own * seqs
    total = size * seqs
    capacity = 8 * size // owners

    vmem, hbm, anywhere = (pl.BlockSpec(memory_space=space) for space in (pltpu.VMEM, pltpu.HBM, pl.ANY))

    states, proj = pl.pallas_call(
        state_kernel,
        in_specs=[hbm] * 4,
        out_specs=[vmem] * 2,
        out_shape=[
            pltpu.VMEM((seqs * heads * (width + 4), width), BF),
            pltpu.VMEM(out_proj.shape, BF),
        ],
        scratch_shapes=[
            pltpu.VMEM(key_vecs.shape, BF),
            pltpu.VMEM(value_vecs.shape, BF),
            pltpu.VMEM(log_decay.shape, F32),
            pltpu.SemaphoreType.DMA((4,)),
        ],
        compiler_params=params(),
        cost_estimate=cost(4 * total * feat * width, 6 * total * feat),
        name="states",
    )(*in_hbm(key_vecs, value_vecs, log_decay, out_proj))
    arrived = [swap(states, "seq", d) for d in range(1, count)]

    inner, query, residual_rows = pl.pallas_call(
        inner_kernel,
        in_specs=[hbm] * 5 + [anywhere],
        out_specs=[vmem] * 3,
        out_shape=[
            pltpu.VMEM((seqs, size, feat), F32),
            pltpu.VMEM(queries.shape, BF),
            pltpu.VMEM((unit, model), F32),
        ],
        scratch_shapes=[
            pltpu.VMEM(key_vecs.shape, BF),
            pltpu.VMEM(value_vecs.shape, BF),
            pltpu.VMEM(log_decay.shape, F32),
            pltpu.VMEM(residual.shape, BF),
            pltpu.SemaphoreType.DMA((5,)),
        ],
        compiler_params=params(),
        cost_estimate=cost(6 * total * feat * size, 10 * total * feat),
        name="inner",
    )(*in_hbm(queries, key_vecs, value_vecs, log_decay, residual), *in_vmem(states))

    mine, theirs = pl.pallas_call(
        functools.partial(attend_kernel, count, line),
        in_specs=[vmem] * (4 + count - 1),
        out_specs=[vmem] * 2,
        out_shape=[jax.ShapeDtypeStruct((total // 2, feat), BF)] * 2,
        compiler_params=params(),
        cost_estimate=cost(6 * total * feat * width, 10 * total * feat),
        name="attend",
    )(*in_vmem(query, inner), log_decay, head_gain.reshape(1, feat), *arrived)

    keep, *sends = pl.pallas_call(
        project_kernel,
        in_specs=[vmem] * 4,
        out_specs=[vmem] * line,
        out_shape=[jax.ShapeDtypeStruct((unit, model), F32)]
        + [jax.ShapeDtypeStruct((unit, model), BF)] * (line - 1),
        compiler_params=params(),
        cost_estimate=cost(2 * total * feat * model, 4 * feat * model + 3 * total * model),
        name="project",
    )(mine, swap(theirs, "exp", 1), *in_vmem(proj), swap(proj, "exp", 1))
    got = [swap(send, "exp", 2 * d) for d, send in enumerate(sends, start=1)]

    routes, route_weight, keep = lax.optimization_barrier((routes, route_weight, keep))
    slot, weight = pl.pallas_call(
        functools.partial(route_kernel, own),
        out_shape=[jax.ShapeDtypeStruct((count, total), jnp.int32), jax.ShapeDtypeStruct((count, total), F32)],
        scratch_shapes=[pltpu.VMEM((count, total), jnp.int32), pltpu.VMEM((count, total), F32)],
        compiler_params=params(),
        cost_estimate=cost(10 * count * total * total, 16 * count * total),
        name="route",
    )(jnp.transpose(routes, (1, 2, 0)), jnp.transpose(route_weight, (1, 2, 0)))

    keep, slot, weight = lax.optimization_barrier((keep, slot, weight))
    gate, up = pl.pallas_call(
        load_kernel,
        in_specs=[hbm, hbm, anywhere],
        out_specs=[vmem] * 2,
        out_shape=[pltpu.VMEM(w_gate.shape, BF), pltpu.VMEM(w_up.shape, BF)],
        scratch_shapes=[pltpu.SemaphoreType.DMA((2, 4))],
        compiler_params=params(VMEM_BYTES // 8),
        cost_estimate=cost(1, 4 * w_gate.size),
        name="load",
    )(*in_hbm(w_gate, w_up), keep)
    mixed, normed = pl.pallas_call(
        mix_kernel,
        in_specs=[vmem] * 3 + [anywhere] + [vmem] * (line - 1),
        out_shape=[jax.ShapeDtypeStruct((unit, model), F32), jax.ShapeDtypeStruct((unit, model), BF)],
        compiler_params=params(),
        cost_estimate=cost(10 * unit * model, 16 * unit * model),
        name="mix",
    )(keep, residual_rows, norm_gain.reshape(1, model), *in_vmem(gate), *reversed(got))
    attn_out = pl.pallas_call(
        place_kernel,
        out_shape=jax.ShapeDtypeStruct((own, seqs, model), F32),
        compiler_params=params(VMEM_BYTES // 8),
        cost_estimate=cost(1, 8 * unit * model),
        name="place",
    )(mixed)

    along = [swap(normed, "exp", 2 * d) for d in range(1, line)]
    across = [normed] + [swap(normed, "seq", d) for d in range(1, count)]
    arrays = along[:1] + across[1:] + along[1:] + [normed]

    def parts_of(some, first=0):
        return [(next(n for n, a in enumerate(arrays) if a is one), first, unit - first) for one in some]

    plans = [parts_of(across), parts_of(along)]
    head = unit // 2
    square = count == 4 and unit % 32 == 0 and line > 2
    if square:
        plans.append(parts_of(along[:1], head) + parts_of(along[1:]))
        plans.append([(n, 0, head) for n, *_ in parts_of(across[1:3])] + parts_of(across[3:]))
    rows = [sum(height for _, _, height in plan) for plan in plans]
    near, rest, *going = pl.pallas_call(
        functools.partial(gather_kernel, plans),
        in_specs=[vmem] * len(arrays) + [anywhere],
        out_specs=[vmem] * len(plans),
        out_shape=[jax.ShapeDtypeStruct((n, model), BF) for n in rows],
        compiler_params=params(VMEM_BYTES // 8),
        cost_estimate=cost(1, 4 * sum(rows) * model),
        name="gather",
    )(*arrays, *in_hbm(attn_out))
    def computed(lines, blocks, previous):
        plan, arrays = [], []
        for n, pieces in zip(lines, blocks):
            plan.append([])
            for partner in (False, True):
                for piece, first, height in [(near, n * unit, unit)] + pieces:
                    number = next((m for m, one in enumerate(arrays) if one is piece), len(arrays))
                    if number == len(arrays):
                        arrays.append(piece)
                    plan[-1].append((2 * number + partner, first, height))
        for piece in arrays:
            if not any(one is piece for one, _ in swapped):
                swapped.append((piece, swap(piece, "exp", 1)))
        both = [pair for piece in arrays for pair in next(pair for pair in swapped if pair[0] is piece)]
        return experts(lines, capacity, slot, weight, gate, up, plan, both, previous)

    half = count // 2
    swapped = []
    blocks = [[(rest, 0, rest.shape[0])]]
    if square:
        blocks += exchanged(*going, unit, *in_vmem(gate))
    else:
        blocks += [[(swap(rest, "seq", d), 0, rest.shape[0])] for d in range(1, count)]
    hidden = computed(range(half), blocks[:half], None)
    *last, hidden = lax.optimization_barrier((*(piece for piece, *_ in blocks[-1][-2:]), hidden))
    blocks[-1][-2:] = [(piece, *place) for piece, (_, *place) in zip(last, blocks[-1][-2:])]
    hidden = computed(range(half, count), blocks[half:], hidden)
    return (attn_out, hidden)


def solution(mesh):
    placed = (
        P(("seq", "exp"), None, None),
        P(None, "seq", "exp"),
        P(None, "seq", "exp"),
        P(None, "seq", "exp"),
        P(None, "exp", "seq"),
        P("exp"),
        P("exp", None),
        P(),
        P(),
        P(),
        P("exp", "seq", None),
        P("exp", "seq", None),
    )
    return jax.shard_map(
        per_device,
        mesh=mesh,
        in_specs=placed,
        out_specs=(P(("seq", "exp"), None, None), P("exp", "seq", None)),
        check_vma=False,
    )
```

```python
import functools

import jax
import jax.numpy as jnp
from jax import lax
from jax.experimental import pallas as pl
from jax.experimental.pallas import tpu as pltpu
from jax.sharding import PartitionSpec as P

BF, F32 = jnp.bfloat16, jnp.float32
PRECISE = lax.Precision.HIGHEST
VMEM_BYTES = 16 * 1024 * 1024
NT = (((1,), (1,)), ((), ()))
TN = (((0,), (0,)), ((), ()))


def in_hbm(*arrays):
    return [pltpu.with_memory_space_constraint(array, pltpu.HBM) for array in arrays]


def in_vmem(*arrays):
    return [pltpu.with_memory_space_constraint(array, pltpu.VMEM) for array in arrays]


def swap(block, axis, distance, forward_only=False):
    devices = range(lax.axis_size(axis))
    route = [(i, i ^ distance) for i in devices if not forward_only or i < i ^ distance]
    return lax.ppermute(block, axis, route)


def mm(a, b, dims=(((1,), (0,)), ((), ()))):
    return lax.dot_general(a, b, dims, preferred_element_type=F32)


def halves(x):
    high = x.astype(BF)
    return high, (x - high.astype(F32)).astype(BF)


def thirds(x):
    high, rest = x.astype(BF), None
    rest = x - high.astype(F32)
    middle = rest.astype(BF)
    return high, middle, (rest - middle.astype(F32)).astype(BF)


def lower_triangle(size):
    return (
        lax.broadcasted_iota(jnp.int32, (size, size), 0) >= lax.broadcasted_iota(jnp.int32, (size, size), 1)
    )


def running_columns(log_decay):
    tri = lower_triangle(log_decay.shape[1]).astype(F32)
    return lax.dot_general(tri, log_decay, NT, precision=PRECISE, preferred_element_type=F32)


def running_rows(log_decay):
    tri = lower_triangle(log_decay.shape[1]).astype(F32)
    return lax.dot_general(log_decay, tri, NT, precision=PRECISE, preferred_element_type=F32)


def state_kernel(k_hbm, v_hbm, decay_hbm, proj_hbm, out_ref, proj_ref, k_ref, v_ref, decay_ref, sems):
    seqs, heads, size = decay_ref.shape
    width = k_ref.shape[2] // heads
    pairs = [(decay_hbm, decay_ref)]
    for b in range(seqs):
        pairs += [(k_hbm.at[b], k_ref.at[b]), (v_hbm.at[b], v_ref.at[b])]
    pairs.append((proj_hbm, proj_ref))
    copies = [pltpu.make_async_copy(source, to, sems.at[n]) for n, (source, to) in enumerate(pairs)]
    for copy in copies:
        copy.start()
    copies[0].wait()
    totals, tails = [], []
    for b in range(seqs):
        columns = running_columns(decay_ref[b])
        tails.append(jnp.exp(columns[size - 1 : size, :] - columns))
        totals.append(jnp.broadcast_to(jnp.sum(decay_ref[b], axis=1, keepdims=True), (heads, width)))
    for b, tail in enumerate(tails):
        copies[1 + 2 * b].wait()
        copies[2 + 2 * b].wait()
        for h in range(heads):
            part = slice(h * width, (h + 1) * width)
            value = v_ref[b, :, part]
            high, low = halves(k_ref[b, :, part].astype(F32) * tail[:, h : h + 1])
            at = (b * heads + h) * width
            out_ref[at : at + width, :] = (mm(high, value, TN) + mm(low, value, TN)).astype(BF)
    total = jnp.concatenate(totals, axis=0)
    pieces = [piece.astype(F32) for piece in thirds(total)]
    pieces.append(jnp.zeros_like(total))
    out_ref[seqs * heads * width :, :] = jnp.concatenate(pieces, axis=0).astype(BF)
    copies[-1].wait()


def inner_kernel(line, q_hbm, k_hbm, v_hbm, decay_hbm, residual_hbm, after, *refs):
    out_ref, q_ref, rows_ref, grown_ref, order_ref = refs[:5]
    scratch = refs[5:]
    k_ref, v_ref, decay_ref, residual_ref, sems = scratch
    pairs = (
        (decay_hbm, decay_ref),
        (q_hbm, q_ref),
        (k_hbm, k_ref),
        (v_hbm, v_ref),
        (residual_hbm, residual_ref),
    )
    copies = [pltpu.make_async_copy(source, to, sems.at[n]) for n, (source, to) in enumerate(pairs)]
    for copy in copies:
        copy.start()
    own, seqs, _ = residual_ref.shape
    index = lax.axis_index("exp")
    total = order_ref.shape[0]
    to = lax.broadcasted_iota(jnp.int32, (total, total), 0)
    source = source_position(to // (total // 2), (to // (seqs * own)) % line, to % own, index, own)
    source = source + (total // seqs) * ((to // own) % seqs)
    order_ref[...] = (source == lax.broadcasted_iota(jnp.int32, (total, total), 1)).astype(BF)
    for copy in copies:
        copy.wait()
    for b in range(seqs):
        rows_ref[b * own : (b + 1) * own, :] = residual_ref[:, b, :].astype(F32)
    _, heads, size = decay_ref.shape
    width = k_ref.shape[2] // heads
    causal = lower_triangle(size)
    for b in range(seqs):
        columns = running_columns(decay_ref[b])
        rows = running_rows(decay_ref[b])
        grown_ref[b] = jnp.exp(columns)
        for h in range(heads):
            part = slice(h * width, (h + 1) * width)
            spread = columns[:, h : h + 1] - rows[h : h + 1, :]
            decay = jnp.where(causal, jnp.exp(jnp.where(causal, spread, 0.0)), 0.0)
            scores = mm(q_ref[b, :, part], k_ref[b, :, part], NT) * decay
            high, low = halves(scores)
            value = v_ref[b, :, part]
            out_ref[b, :, part] = mm(high, value) + mm(low, value)


def attend_kernel(count, *refs):
    q_ref, inner_ref, grown_ref, order_ref, gain_ref = refs[:5]
    states = refs[5 : 4 + count]
    own_ref, partner_ref = refs[4 + count :]
    seqs, size, feat = q_ref.shape
    heads = grown_ref.shape[2]
    width = feat // heads
    me = lax.axis_index("seq")
    each = seqs * heads
    base = each * width
    totals = []
    for state in states:
        three = state[base : base + 4 * each, :].astype(F32)
        totals.append(three[:each] + three[each : 2 * each] + three[2 * each : 3 * each])
    factors = []
    for first in range(1, count):
        later = jnp.zeros_like(totals[0])
        for second in range(1, count):
            between = ((me ^ first) < (me ^ second)) & ((me ^ second) < me)
            later = later + jnp.where(between, totals[second - 1], 0.0)
        factors.append(jnp.where((me ^ first) < me, jnp.exp(later), 0.0))
    rows = []
    for b in range(seqs):
        grown = grown_ref[b]
        parts = []
        for h in range(heads):
            part = slice(h * width, (h + 1) * width)
            n = b * heads + h
            incoming = jnp.zeros((width, width), F32)
            for state, factor in zip(states, factors):
                incoming = incoming + factor[n : n + 1, :] * state[n * width : (n + 1) * width, :].astype(F32)
            high, low = halves(incoming)
            query = q_ref[b, :, part]
            raw = inner_ref[b, :, part] + grown[:, h : h + 1] * (mm(query, high) + mm(query, low))
            meansq = jnp.mean(raw * raw, axis=-1, keepdims=True)
            parts.append((raw * lax.rsqrt(meansq + 1e-06) * gain_ref[:, part]).astype(BF))
        rows.append(jnp.concatenate(parts, axis=1))
    attention = jnp.concatenate(rows, axis=0)
    total = seqs * size
    attention = mm(order_ref[...], attention).astype(BF)
    own_ref[...] = attention[: total // 2, :]
    partner_ref[...] = attention[total // 2 :, :]


def project_kernel(own_ref, partner_ref, proj_ref, partner_proj_ref, keep_ref, *send_refs):
    rows, model = keep_ref.shape
    tile = column_tile(model)
    for n in range(model // tile):
        columns = slice(n * tile, (n + 1) * tile)
        product = mm(own_ref[...], proj_ref[:, columns]) + mm(partner_ref[...], partner_proj_ref[:, columns])
        keep_ref[:, columns] = product[:rows, :]
        for d, send_ref in enumerate(send_refs, start=1):
            send_ref[:, columns] = product[d * rows : (d + 1) * rows, :].astype(BF)


def column_tile(model):
    return max(t for t in range(128, 1025, 128) if model % t == 0)


def source_position(flip, distance, place, index, own):
    return own * (2 * ((index // 2) ^ distance) + ((index % 2) ^ flip)) + place


def mix_kernel(kept_ref, residual_ref, gain_ref, after, *refs):
    mixed_ref, normed_ref = refs[-2:]
    mixed = residual_ref[...] + kept_ref[...]
    for got_ref in refs[:-2]:
        mixed = mixed + got_ref[...].astype(F32)
    mixed_ref[...] = mixed
    meansq = jnp.mean(mixed * mixed, axis=-1, keepdims=True)
    normed_ref[...] = (mixed * lax.rsqrt(meansq + 1e-06) * gain_ref[...]).astype(BF)


def place_kernel(mixed_ref, out_ref):
    own, seqs, _ = out_ref.shape
    for b in range(seqs):
        out_ref[:, b, :] = mixed_ref[b * own : (b + 1) * own, :]


def load_kernel(gate_hbm, up_hbm, after, gate_ref, up_ref, sems):
    parts = sems.shape[1]
    rows = gate_ref.shape[1] // parts
    copies = []
    for m, (source, to) in enumerate(((gate_hbm, gate_ref), (up_hbm, up_ref))):
        for n in range(parts):
            part = pl.ds(n * rows, rows)
            copies.append(pltpu.make_async_copy(source.at[0, part], to.at[0, part], sems.at[m, n]))
            copies[-1].start()
    for copy in copies:
        copy.wait()


def gather_kernel(plans, *refs):
    for to, plan in zip(refs[-len(plans) :], plans):
        at = 0
        for number, first, height in plan:
            to[at : at + height, :] = refs[number][first : first + height, :]
            at += height


def halves_kernel(one_ref, two_ref, corner_ref, after, low_ref, high_ref):
    half = low_ref.shape[0]
    first = one_ref.shape[0] - 2 * half
    low_ref[...] = one_ref[first : first + half, :]
    high_ref[...] = two_ref[first + half :, :]


def exchanged(block, corner, unit, after):
    rows, head = block.shape[0], unit // 2
    half = (rows - head) // 2
    one, two = swap(block, "seq", 1), swap(block, "seq", 2)
    corner = swap(corner, "exp", 2)
    vmem, anywhere = pl.BlockSpec(memory_space=pltpu.VMEM), pl.BlockSpec(memory_space=pl.ANY)
    low, high = pl.pallas_call(
        halves_kernel,
        in_specs=[vmem] * 3 + [anywhere],
        out_specs=[vmem] * 2,
        out_shape=[jax.ShapeDtypeStruct((half, block.shape[1]), block.dtype)] * 2,
        compiler_params=params(VMEM_BYTES // 8),
        cost_estimate=cost(1, 4 * block.size),
        name="halves",
    )(one, two, corner, after)
    one, two, low, high = lax.optimization_barrier((one, two, low, high))
    far = [(swap(low, "seq", 2), 0, half), (swap(high, "seq", 1), 0, half)]
    return [
        [(corner, 0, head), (one, 0, rows)],
        [(corner, head, head), (two, 0, rows)],
        [(corner, 2 * head, unit)] + far,
    ]


def route_kernel(own, routes_ref, weights_ref, slot_ref, weight_ref, a_ref, b_ref):
    seqs, tops, _ = routes_ref.shape
    count, total = slot_ref.shape
    size = total // seqs
    me = lax.axis_index("seq")
    index = lax.axis_index("exp")
    line = size // (2 * own)
    lines, shares = [], []
    for c in range(count):
        part = slice(c * size, (c + 1) * size)
        hit, share = [], []
        for b in range(seqs):
            hits = [routes_ref[b, k : k + 1, part] == index for k in range(tops)]
            hit.append(sum(jnp.where(one, 1.0, 0.0) for one in hits))
            share.append(sum(jnp.where(one, weights_ref[b, k : k + 1, part], 0.0) for k, one in enumerate(hits)))
        lines.append(jnp.concatenate(hit, axis=1))
        shares.append(jnp.concatenate(share, axis=1))
    chosen = jnp.concatenate(lines, axis=0).astype(BF)
    weight = jnp.concatenate(shares, axis=0)
    to = lax.broadcasted_iota(jnp.int32, (total, total), 1)
    row = source_position(to // (total // 2), (to // (seqs * own)) % line, to % own, index, own) * seqs
    row = row + (to // own) % seqs
    origin = lax.broadcasted_iota(jnp.int32, (total, total), 0)
    origin = (origin % size) * seqs + origin // size
    rank = mm(chosen, (origin <= row).astype(BF)) - 1.0
    same = (origin == row).astype(BF)
    picked = mm(chosen, same) > 0.5
    a_ref[...] = jnp.where(picked, rank.astype(jnp.int32), -1)
    high, middle, low = thirds(weight)
    b_ref[...] = mm(high, same) + mm(middle, same) + mm(low, same)
    for d in range(count):
        slot_ref[d : d + 1, :] = a_ref[pl.ds(me ^ d, 1), :]
        weight_ref[d : d + 1, :] = b_ref[pl.ds(me ^ d, 1), :]


def expert_kernel(plan, arrays, lines, slot_ref, weight_ref, gate_ref, up_ref, *refs):
    array_refs, (out_hbm, rows_ref, out_ref, sems) = refs[:arrays], refs[-4:]
    total = slot_ref.shape[1]
    blocks = len(lines)
    slots, width = rows_ref.shape
    me = lax.axis_index("seq")
    tile = out_ref.shape[1]
    capacity = slots // blocks
    apart = capacity % 128 == 0
    numbers = lax.broadcasted_iota(jnp.int32, (slots, total), 0)
    picks = []
    for n, line in enumerate(lines):
        place = n if apart else (me ^ line) % blocks
        slot = slot_ref[line : line + 1, :]
        picks.append((jnp.where(slot < 0, slot, slot + place * capacity) == numbers).astype(BF))
    weight = jnp.concatenate([weight_ref[line : line + 1, :] for line in lines], axis=1)
    parts = [part.astype(F32) for part in thirds(weight)] + [jnp.zeros((5, blocks * total), F32)]
    parts = jnp.concatenate(parts, axis=0).astype(BF)
    scale = jnp.sum(mm(parts, jnp.concatenate(picks, axis=1), NT), axis=0, keepdims=True)

    step = column_tile(width)
    for at in range(0, width, step):
        part = slice(at, at + step)
        rows = []
        for pieces in plan:
            rows.append([array_refs[m][first : first + height, part] for m, first, height in pieces])
        if apart:
            for n, pick in enumerate(picks):
                own = slice(n * capacity, (n + 1) * capacity)
                rows_ref[own, part] = mm(pick[own], jnp.concatenate(rows[n], axis=0)).astype(BF)
        else:
            rows = jnp.concatenate([piece for pieces in rows for piece in pieces], axis=0)
            rows_ref[:, part] = mm(jnp.concatenate(picks, axis=1), rows).astype(BF)

    targets = [(slice(0, slots), (me ^ lines[0]) // blocks)]
    if apart:
        targets = [(slice(n * capacity, (n + 1) * capacity), me ^ line) for n, line in enumerate(lines)]
    copies = []
    for step in range(out_ref.shape[0]):
        part = slice(step * tile, (step + 1) * tile)
        gate = mm(gate_ref[0, part, :], rows_ref[...], NT)
        up = mm(up_ref[0, part, :], rows_ref[...], NT)
        out_ref[step] = scale * (gate / (1.0 + jnp.exp(-gate))) * up
        for columns, place in targets:
            size = columns.stop - columns.start
            to = out_hbm.at[0, part, pl.ds(pl.multiple_of(place * size, size), size)]
            copies.append(pltpu.make_async_copy(out_ref.at[step, :, columns], to, sems.at[len(copies)]))
            copies[-1].start()
    for copy in copies:
        copy.wait()


def params(vmem=VMEM_BYTES):
    return pltpu.CompilerParams(vmem_limit_bytes=vmem)


def cost(flops, bytes_accessed, transcendentals=0):
    return pl.CostEstimate(flops=int(flops), bytes_accessed=int(bytes_accessed), transcendentals=int(transcendentals))


def whole(shape):
    return pl.BlockSpec(shape, lambda *_: (0,) * len(shape))


def experts(lines, capacity, slot, weight, w_gate, w_up, plan, arrays, previous):
    units, width = w_gate.shape[1:]
    tile = max(size for size in range(16, 385, 16) if units % size == 0)
    steps = units // tile
    slots = len(lines) * capacity
    carried = [] if previous is None else [previous]
    vmem, hbm = pl.BlockSpec(memory_space=pltpu.VMEM), pl.BlockSpec(memory_space=pltpu.HBM)
    return pl.pallas_call(
        functools.partial(expert_kernel, plan, len(arrays), lines),
        in_specs=[vmem] * (4 + len(arrays)) + [hbm] * len(carried),
        out_specs=hbm,
        out_shape=jax.ShapeDtypeStruct((1, units, slot.shape[0] * capacity), F32),
        scratch_shapes=[
            pltpu.VMEM((slots, width), BF),
            pltpu.VMEM((steps, tile, slots), F32),
            pltpu.SemaphoreType.DMA((steps * len(lines),)),
        ],
        input_output_aliases={4 + len(arrays): 0} if carried else {},
        compiler_params=params(),
        cost_estimate=cost(4 * units * width * slots, 2 * slots * width),
        name="experts",
    )(slot, weight, *in_vmem(w_gate, w_up), *arrays, *carried)


def per_device(
    residual,
    queries,
    key_vecs,
    value_vecs,
    log_decay,
    head_gain,
    out_proj,
    norm_gain,
    routes,
    route_weight,
    w_gate,
    w_up,
):
    count, owners = lax.axis_size("seq"), lax.axis_size("exp")
    line = owners // 2
    me = lax.axis_index("seq")
    seqs, size, feat = queries.shape
    heads = log_decay.shape[1]
    width = feat // heads
    own, _, model = residual.shape
    unit = own * seqs
    total = size * seqs
    capacity = 8 * size // owners

    vmem, hbm, anywhere = (pl.BlockSpec(memory_space=space) for space in (pltpu.VMEM, pltpu.HBM, pl.ANY))

    states, proj = pl.pallas_call(
        state_kernel,
        in_specs=[hbm] * 4,
        out_specs=[vmem] * 2,
        out_shape=[
            pltpu.VMEM((seqs * heads * (width + 4), width), BF),
            pltpu.VMEM(out_proj.shape, BF),
        ],
        scratch_shapes=[
            pltpu.VMEM(key_vecs.shape, BF),
            pltpu.VMEM(value_vecs.shape, BF),
            pltpu.VMEM(log_decay.shape, F32),
            pltpu.SemaphoreType.DMA((2 + 2 * seqs,)),
        ],
        compiler_params=params(),
        cost_estimate=cost(4 * total * feat * width, 6 * total * feat),
        name="states",
    )(*in_hbm(key_vecs, value_vecs, log_decay, out_proj))
    arrived = [swap(states, "seq", d) for d in range(1, count)]

    inner, query, residual_rows, grown, order = pl.pallas_call(
        functools.partial(inner_kernel, line),
        in_specs=[hbm] * 5 + [anywhere],
        out_specs=[vmem] * 5,
        out_shape=[
            pltpu.VMEM((seqs, size, feat), F32),
            pltpu.VMEM(queries.shape, BF),
            pltpu.VMEM((unit, model), F32),
            pltpu.VMEM((seqs, size, heads), F32),
            pltpu.VMEM((total, total), BF),
        ],
        scratch_shapes=[
            pltpu.VMEM(key_vecs.shape, BF),
            pltpu.VMEM(value_vecs.shape, BF),
            pltpu.VMEM(log_decay.shape, F32),
            pltpu.VMEM(residual.shape, BF),
            pltpu.SemaphoreType.DMA((5,)),
        ],
        compiler_params=params(),
        cost_estimate=cost(6 * total * feat * size, 10 * total * feat),
        name="inner",
    )(*in_hbm(queries, key_vecs, value_vecs, log_decay, residual), *in_vmem(states))

    mine, theirs = pl.pallas_call(
        functools.partial(attend_kernel, count),
        in_specs=[vmem] * (5 + count - 1),
        out_specs=[vmem] * 2,
        out_shape=[jax.ShapeDtypeStruct((total // 2, feat), BF)] * 2,
        compiler_params=params(),
        cost_estimate=cost(6 * total * feat * width, 10 * total * feat),
        name="attend",
    )(*in_vmem(query, inner, grown, order), head_gain.reshape(1, feat), *arrived)

    keep, *sends = pl.pallas_call(
        project_kernel,
        in_specs=[vmem] * 4,
        out_specs=[vmem] * line,
        out_shape=[jax.ShapeDtypeStruct((unit, model), F32)]
        + [jax.ShapeDtypeStruct((unit, model), BF)] * (line - 1),
        compiler_params=params(),
        cost_estimate=cost(2 * total * feat * model, 4 * feat * model + 3 * total * model),
        name="project",
    )(mine, swap(theirs, "exp", 1), *in_vmem(proj), swap(proj, "exp", 1))
    got = [swap(send, "exp", 2 * d) for d, send in enumerate(sends, start=1)]

    routes, route_weight, keep = lax.optimization_barrier((routes, route_weight, keep))
    slot, weight = pl.pallas_call(
        functools.partial(route_kernel, own),
        out_shape=[jax.ShapeDtypeStruct((count, total), jnp.int32), jax.ShapeDtypeStruct((count, total), F32)],
        scratch_shapes=[pltpu.VMEM((count, total), jnp.int32), pltpu.VMEM((count, total), F32)],
        compiler_params=params(),
        cost_estimate=cost(10 * count * total * total, 16 * count * total),
        name="route",
    )(jnp.transpose(routes, (1, 2, 0)), jnp.transpose(route_weight, (1, 2, 0)))

    keep, slot, weight = lax.optimization_barrier((keep, slot, weight))
    gate, up = pl.pallas_call(
        load_kernel,
        in_specs=[hbm, hbm, anywhere],
        out_specs=[vmem] * 2,
        out_shape=[pltpu.VMEM(w_gate.shape, BF), pltpu.VMEM(w_up.shape, BF)],
        scratch_shapes=[pltpu.SemaphoreType.DMA((2, 4))],
        compiler_params=params(VMEM_BYTES // 8),
        cost_estimate=cost(1, 4 * w_gate.size),
        name="load",
    )(*in_hbm(w_gate, w_up), keep)
    mixed, normed = pl.pallas_call(
        mix_kernel,
        in_specs=[vmem] * 3 + [anywhere] + [vmem] * (line - 1),
        out_shape=[jax.ShapeDtypeStruct((unit, model), F32), jax.ShapeDtypeStruct((unit, model), BF)],
        compiler_params=params(),
        cost_estimate=cost(10 * unit * model, 16 * unit * model),
        name="mix",
    )(keep, residual_rows, norm_gain.reshape(1, model), *in_vmem(gate), *got[1:2], *got[:1], *got[2:])
    attn_out = pl.pallas_call(
        place_kernel,
        out_shape=jax.ShapeDtypeStruct((own, seqs, model), F32),
        compiler_params=params(VMEM_BYTES // 8),
        cost_estimate=cost(1, 8 * unit * model),
        name="place",
    )(mixed)

    along = [swap(normed, "exp", 2 * d) for d in range(1, line)]
    across = [normed] + [swap(normed, "seq", d) for d in range(1, count)]
    arrays = along[:1] + across[1:] + along[1:] + [normed]

    def parts_of(some, first=0):
        return [(next(n for n, a in enumerate(arrays) if a is one), first, unit - first) for one in some]

    plans = [parts_of(across), parts_of(along)]
    head = unit // 2
    square = count == 4 and unit % 32 == 0 and line > 2
    if square:
        plans.append(parts_of(along[:1], head) + parts_of(along[1:]))
        plans.append([(n, 0, head) for n, *_ in parts_of(across[1:3])] + parts_of(across[3:]))
    rows = [sum(height for _, _, height in plan) for plan in plans]
    near, rest, *going = pl.pallas_call(
        functools.partial(gather_kernel, plans),
        in_specs=[vmem] * len(arrays) + [anywhere],
        out_specs=[vmem] * len(plans),
        out_shape=[jax.ShapeDtypeStruct((n, model), BF) for n in rows],
        compiler_params=params(VMEM_BYTES // 8),
        cost_estimate=cost(1, 4 * sum(rows) * model),
        name="gather",
    )(*arrays, *in_hbm(attn_out))
    def computed(lines, blocks, previous):
        plan, arrays = [], []
        for n, pieces in zip(lines, blocks):
            plan.append([])
            for partner in (False, True):
                for piece, first, height in [(near, n * unit, unit)] + pieces:
                    number = next((m for m, one in enumerate(arrays) if one is piece), len(arrays))
                    if number == len(arrays):
                        arrays.append(piece)
                    plan[-1].append((2 * number + partner, first, height))
        for piece in arrays:
            if not any(one is piece for one, _ in swapped):
                swapped.append((piece, swap(piece, "exp", 1)))
        both = [pair for piece in arrays for pair in next(pair for pair in swapped if pair[0] is piece)]
        return experts(lines, capacity, slot, weight, gate, up, plan, both, previous)

    half = count // 2
    swapped = []
    blocks = [[(rest, 0, rest.shape[0])]]
    if square:
        blocks += exchanged(*going, unit, *in_vmem(gate))
    else:
        blocks += [[(swap(rest, "seq", d), 0, rest.shape[0])] for d in range(1, count)]
    hidden = computed(range(half), blocks[:half], None)
    *last, hidden = lax.optimization_barrier((*(piece for piece, *_ in blocks[-1][-2:]), hidden))
    blocks[-1][-2:] = [(piece, *place) for piece, (_, *place) in zip(last, blocks[-1][-2:])]
    hidden = computed(range(half, count), blocks[half:], hidden)
    return (attn_out, hidden)


def solution(mesh):
    placed = (
        P(("seq", "exp"), None, None),
        P(None, "seq", "exp"),
        P(None, "seq", "exp"),
        P(None, "seq", "exp"),
        P(None, "exp", "seq"),
        P("exp"),
        P("exp", None),
        P(),
        P(),
        P(),
        P("exp", "seq", None),
        P("exp", "seq", None),
    )
    return jax.shard_map(
        per_device,
        mesh=mesh,
        in_specs=placed,
        out_specs=(P(("seq", "exp"), None, None), P("exp", "seq", None)),
        check_vma=False,
    )
```

```python
import functools

import jax
import jax.numpy as jnp
from jax import lax
from jax.experimental import pallas as pl
from jax.experimental.pallas import tpu as pltpu
from jax.sharding import PartitionSpec as P

BF, F32 = jnp.bfloat16, jnp.float32
PRECISE = lax.Precision.HIGHEST
VMEM_BYTES = 16 * 1024 * 1024
NT = (((1,), (1,)), ((), ()))
TN = (((0,), (0,)), ((), ()))


def in_hbm(*arrays):
    return [pltpu.with_memory_space_constraint(array, pltpu.HBM) for array in arrays]


def in_vmem(*arrays):
    return [pltpu.with_memory_space_constraint(array, pltpu.VMEM) for array in arrays]


def swap(block, axis, distance, forward_only=False):
    devices = range(lax.axis_size(axis))
    route = [(i, i ^ distance) for i in devices if not forward_only or i < i ^ distance]
    return lax.ppermute(block, axis, route)


def mm(a, b, dims=(((1,), (0,)), ((), ()))):
    return lax.dot_general(a, b, dims, preferred_element_type=F32)


def halves(x):
    high = x.astype(BF)
    return high, (x - high.astype(F32)).astype(BF)


def thirds(x):
    high, rest = x.astype(BF), None
    rest = x - high.astype(F32)
    middle = rest.astype(BF)
    return high, middle, (rest - middle.astype(F32)).astype(BF)


def lower_triangle(size):
    return (
        lax.broadcasted_iota(jnp.int32, (size, size), 0) >= lax.broadcasted_iota(jnp.int32, (size, size), 1)
    )


def running_columns(log_decay):
    tri = lower_triangle(log_decay.shape[1]).astype(F32)
    return lax.dot_general(tri, log_decay, NT, precision=PRECISE, preferred_element_type=F32)


def running_rows(log_decay):
    tri = lower_triangle(log_decay.shape[1]).astype(F32)
    return lax.dot_general(log_decay, tri, NT, precision=PRECISE, preferred_element_type=F32)


def state_kernel(k_hbm, v_hbm, decay_hbm, proj_hbm, out_ref, proj_ref, k_ref, v_ref, decay_ref, sems):
    seqs, heads, size = decay_ref.shape
    width = k_ref.shape[2] // heads
    pairs = [(decay_hbm, decay_ref)]
    for b in range(seqs):
        pairs += [(k_hbm.at[b], k_ref.at[b]), (v_hbm.at[b], v_ref.at[b])]
    pairs.append((proj_hbm, proj_ref))
    copies = [pltpu.make_async_copy(source, to, sems.at[n]) for n, (source, to) in enumerate(pairs)]
    for copy in copies:
        copy.start()
    copies[0].wait()
    totals, tails = [], []
    for b in range(seqs):
        columns = running_columns(decay_ref[b])
        tails.append(jnp.exp(columns[size - 1 : size, :] - columns))
        totals.append(jnp.broadcast_to(jnp.sum(decay_ref[b], axis=1, keepdims=True), (heads, width)))
    for b, tail in enumerate(tails):
        copies[1 + 2 * b].wait()
        copies[2 + 2 * b].wait()
        for h in range(heads):
            part = slice(h * width, (h + 1) * width)
            value = v_ref[b, :, part]
            high, low = halves(k_ref[b, :, part].astype(F32) * tail[:, h : h + 1])
            at = (b * heads + h) * width
            out_ref[at : at + width, :] = (mm(high, value, TN) + mm(low, value, TN)).astype(BF)
    total = jnp.concatenate(totals, axis=0)
    pieces = [piece.astype(F32) for piece in thirds(total)]
    pieces.append(jnp.zeros_like(total))
    out_ref[seqs * heads * width :, :] = jnp.concatenate(pieces, axis=0).astype(BF)
    copies[-1].wait()


def inner_kernel(line, q_hbm, k_hbm, v_hbm, decay_hbm, residual_hbm, after, *refs):
    out_ref, q_ref, rows_ref, grown_ref, order_ref = refs[:5]
    scratch = refs[5:]
    k_ref, v_ref, decay_ref, residual_ref, sems = scratch
    pairs = (
        (decay_hbm, decay_ref),
        (q_hbm, q_ref),
        (k_hbm, k_ref),
        (v_hbm, v_ref),
        (residual_hbm, residual_ref),
    )
    copies = [pltpu.make_async_copy(source, to, sems.at[n]) for n, (source, to) in enumerate(pairs)]
    for copy in copies:
        copy.start()
    own, seqs, _ = residual_ref.shape
    index = lax.axis_index("exp")
    total = order_ref.shape[0]
    to = lax.broadcasted_iota(jnp.int32, (total, total), 0)
    source = source_position(to // (total // 2), (to // (seqs * own)) % line, to % own, index, own)
    source = source + (total // seqs) * ((to // own) % seqs)
    order_ref[...] = (source == lax.broadcasted_iota(jnp.int32, (total, total), 1)).astype(BF)
    for copy in copies:
        copy.wait()
    for b in range(seqs):
        rows_ref[b * own : (b + 1) * own, :] = residual_ref[:, b, :].astype(F32)
    _, heads, size = decay_ref.shape
    width = k_ref.shape[2] // heads
    causal = lower_triangle(size)
    for b in range(seqs):
        columns = running_columns(decay_ref[b])
        rows = running_rows(decay_ref[b])
        grown_ref[b] = jnp.exp(columns)
        for h in range(heads):
            part = slice(h * width, (h + 1) * width)
            spread = columns[:, h : h + 1] - rows[h : h + 1, :]
            decay = jnp.where(causal, jnp.exp(jnp.where(causal, spread, 0.0)), 0.0)
            scores = mm(q_ref[b, :, part], k_ref[b, :, part], NT) * decay
            high, low = halves(scores)
            value = v_ref[b, :, part]
            out_ref[b, :, part] = mm(high, value) + mm(low, value)


def attend_kernel(count, *refs):
    q_ref, inner_ref, grown_ref, order_ref, gain_ref = refs[:5]
    states = refs[5 : 4 + count]
    own_ref, partner_ref = refs[4 + count :]
    seqs, size, feat = q_ref.shape
    heads = grown_ref.shape[2]
    width = feat // heads
    me = lax.axis_index("seq")
    each = seqs * heads
    base = each * width
    totals = []
    for state in states:
        three = state[base : base + 4 * each, :].astype(F32)
        totals.append(three[:each] + three[each : 2 * each] + three[2 * each : 3 * each])
    factors = []
    for first in range(1, count):
        later = jnp.zeros_like(totals[0])
        for second in range(1, count):
            between = ((me ^ first) < (me ^ second)) & ((me ^ second) < me)
            later = later + jnp.where(between, totals[second - 1], 0.0)
        factors.append(jnp.where((me ^ first) < me, jnp.exp(later), 0.0))
    rows = []
    for b in range(seqs):
        grown = grown_ref[b]
        parts = []
        for h in range(heads):
            part = slice(h * width, (h + 1) * width)
            n = b * heads + h
            incoming = jnp.zeros((width, width), F32)
            for state, factor in zip(states, factors):
                incoming = incoming + factor[n : n + 1, :] * state[n * width : (n + 1) * width, :].astype(F32)
            high, low = halves(incoming)
            query = q_ref[b, :, part]
            raw = inner_ref[b, :, part] + grown[:, h : h + 1] * (mm(query, high) + mm(query, low))
            meansq = jnp.mean(raw * raw, axis=-1, keepdims=True)
            parts.append((raw * lax.rsqrt(meansq + 1e-06) * gain_ref[:, part]).astype(BF))
        rows.append(jnp.concatenate(parts, axis=1))
    attention = jnp.concatenate(rows, axis=0)
    total = seqs * size
    attention = mm(order_ref[...], attention).astype(BF)
    own_ref[...] = attention[: total // 2, :]
    partner_ref[...] = attention[total // 2 :, :]


def project_kernel(own_ref, partner_ref, proj_ref, partner_proj_ref, keep_ref, *send_refs):
    rows, model = keep_ref.shape
    tile = column_tile(model)
    for n in range(model // tile):
        columns = slice(n * tile, (n + 1) * tile)
        product = mm(own_ref[...], proj_ref[:, columns]) + mm(partner_ref[...], partner_proj_ref[:, columns])
        keep_ref[:, columns] = product[:rows, :]
        for d, send_ref in enumerate(send_refs, start=1):
            send_ref[:, columns] = product[d * rows : (d + 1) * rows, :].astype(BF)


def column_tile(model):
    return max(t for t in range(128, 1025, 128) if model % t == 0)


def source_position(flip, distance, place, index, own):
    return own * (2 * ((index // 2) ^ distance) + ((index % 2) ^ flip)) + place


def mix_kernel(kept_ref, residual_ref, gain_ref, after, *refs):
    mixed_ref, normed_ref = refs[-2:]
    mixed = residual_ref[...] + kept_ref[...]
    for got_ref in refs[:-2]:
        mixed = mixed + got_ref[...].astype(F32)
    mixed_ref[...] = mixed
    meansq = jnp.mean(mixed * mixed, axis=-1, keepdims=True)
    normed_ref[...] = (mixed * lax.rsqrt(meansq + 1e-06) * gain_ref[...]).astype(BF)


def place_kernel(mixed_ref, out_ref):
    own, seqs, _ = out_ref.shape
    for b in range(seqs):
        out_ref[:, b, :] = mixed_ref[b * own : (b + 1) * own, :]


def load_kernel(gate_hbm, up_hbm, after, gate_ref, up_ref, sems):
    parts = sems.shape[1]
    rows = gate_ref.shape[1] // parts
    copies = []
    for m, (source, to) in enumerate(((gate_hbm, gate_ref), (up_hbm, up_ref))):
        for n in range(parts):
            part = pl.ds(n * rows, rows)
            copies.append(pltpu.make_async_copy(source.at[0, part], to.at[0, part], sems.at[m, n]))
            copies[-1].start()
    for copy in copies:
        copy.wait()


def gather_kernel(plans, *refs):
    for to, plan in zip(refs[-len(plans) :], plans):
        at = 0
        for number, first, height in plan:
            to[at : at + height, :] = refs[number][first : first + height, :]
            at += height


def halves_kernel(one_ref, two_ref, corner_ref, after, low_ref, high_ref):
    half = low_ref.shape[0]
    first = one_ref.shape[0] - 2 * half
    low_ref[...] = one_ref[first : first + half, :]
    high_ref[...] = two_ref[first + half :, :]


def exchanged(block, corner, unit, after):
    rows, head = block.shape[0], unit // 2
    half = (rows - head) // 2
    one, two = swap(block, "seq", 1), swap(block, "seq", 2)
    corner = swap(corner, "exp", 2)
    vmem, anywhere = pl.BlockSpec(memory_space=pltpu.VMEM), pl.BlockSpec(memory_space=pl.ANY)
    low, high = pl.pallas_call(
        halves_kernel,
        in_specs=[vmem] * 3 + [anywhere],
        out_specs=[vmem] * 2,
        out_shape=[jax.ShapeDtypeStruct((half, block.shape[1]), block.dtype)] * 2,
        compiler_params=params(VMEM_BYTES // 8),
        cost_estimate=cost(1, 4 * block.size),
        name="halves",
    )(one, two, corner, after)
    one, two, low, high = lax.optimization_barrier((one, two, low, high))
    far = [(swap(low, "seq", 2), 0, half), (swap(high, "seq", 1), 0, half)]
    return [
        [(corner, 0, head), (one, 0, rows)],
        [(corner, head, head), (two, 0, rows)],
        [(corner, 2 * head, unit)] + far,
    ]


def route_kernel(own, routes_ref, weights_ref, slot_ref, weight_ref, a_ref, b_ref):
    seqs, tops, _ = routes_ref.shape
    count, total = a_ref.shape
    size = total // seqs
    me = lax.axis_index("seq")
    index = lax.axis_index("exp")
    line = size // (2 * own)
    lines, shares = [], []
    for c in range(count):
        part = slice(c * size, (c + 1) * size)
        hit, share = [], []
        for b in range(seqs):
            hits = [routes_ref[b, k : k + 1, part] == index for k in range(tops)]
            hit.append(sum(jnp.where(one, 1.0, 0.0) for one in hits))
            share.append(sum(jnp.where(one, weights_ref[b, k : k + 1, part], 0.0) for k, one in enumerate(hits)))
        lines.append(jnp.concatenate(hit, axis=1))
        shares.append(jnp.concatenate(share, axis=1))
    chosen = jnp.concatenate(lines, axis=0).astype(BF)
    weight = jnp.concatenate(shares, axis=0)
    to = lax.broadcasted_iota(jnp.int32, (total, total), 1)
    row = source_position(to // (total // 2), (to // (seqs * own)) % line, to % own, index, own) * seqs
    row = row + (to // own) % seqs
    origin = lax.broadcasted_iota(jnp.int32, (total, total), 0)
    origin = (origin % size) * seqs + origin // size
    rank = mm(chosen, (origin <= row).astype(BF)) - 1.0
    same = (origin == row).astype(BF)
    picked = mm(chosen, same) > 0.5
    a_ref[...] = jnp.where(picked, rank.astype(jnp.int32), -1)
    high, middle, low = thirds(weight)
    b_ref[...] = mm(high, same) + mm(middle, same) + mm(low, same)
    capacity = weight_ref.shape[1]
    numbers = lax.broadcasted_iota(jnp.int32, (capacity, total), 0)
    for d in range(count):
        slot, weight = a_ref[pl.ds(me ^ d, 1), :], b_ref[pl.ds(me ^ d, 1), :]
        if slot_ref.shape[0] == count:
            slot_ref[d : d + 1, :] = slot
            weight_ref[d : d + 1, :] = weight
            continue
        pick = (slot == numbers).astype(BF)
        slot_ref[d * capacity : (d + 1) * capacity, :] = pick
        weight_ref[d : d + 1, :] = weighed([weight], pick)


def weighed(weights, pick):
    weight = jnp.concatenate(weights, axis=1)
    parts = [part.astype(F32) for part in thirds(weight)] + [jnp.zeros((5, weight.shape[1]), F32)]
    return jnp.sum(mm(jnp.concatenate(parts, axis=0).astype(BF), pick, NT), axis=0, keepdims=True)


def expert_kernel(plan, arrays, lines, slot_ref, weight_ref, gate_ref, up_ref, *refs):
    array_refs, (out_hbm, rows_ref, out_ref, sems) = refs[:arrays], refs[-4:]
    total = slot_ref.shape[1]
    blocks = len(lines)
    slots, width = rows_ref.shape
    me = lax.axis_index("seq")
    tile = out_ref.shape[1]
    capacity = slots // blocks
    apart = capacity % 128 == 0
    picks = []
    if apart:
        picks = [slot_ref[line * capacity : (line + 1) * capacity, :] for line in lines]
        scale = jnp.concatenate([weight_ref[line : line + 1, :] for line in lines], axis=1)
    else:
        numbers = lax.broadcasted_iota(jnp.int32, (slots, total), 0)
        for line in lines:
            slot = slot_ref[line : line + 1, :]
            place = (me ^ line) % blocks
            picks.append((jnp.where(slot < 0, slot, slot + place * capacity) == numbers).astype(BF))
        scale = weighed([weight_ref[line : line + 1, :] for line in lines], jnp.concatenate(picks, axis=1))

    step = column_tile(width)
    for at in range(0, width, step):
        part = slice(at, at + step)
        rows = []
        for pieces in plan:
            rows.append([array_refs[m][first : first + height, part] for m, first, height in pieces])
        if apart:
            for n, pick in enumerate(picks):
                own = slice(n * capacity, (n + 1) * capacity)
                rows_ref[own, part] = mm(pick, jnp.concatenate(rows[n], axis=0)).astype(BF)
        else:
            rows = jnp.concatenate([piece for pieces in rows for piece in pieces], axis=0)
            rows_ref[:, part] = mm(jnp.concatenate(picks, axis=1), rows).astype(BF)

    targets = [(slice(0, slots), (me ^ lines[0]) // blocks)]
    if apart:
        targets = [(slice(n * capacity, (n + 1) * capacity), me ^ line) for n, line in enumerate(lines)]
    copies = []
    for step in range(out_ref.shape[0]):
        part = slice(step * tile, (step + 1) * tile)
        gate = mm(gate_ref[0, part, :], rows_ref[...], NT)
        up = mm(up_ref[0, part, :], rows_ref[...], NT)
        out_ref[step] = scale * (gate / (1.0 + jnp.exp(-gate))) * up
        for columns, place in targets:
            size = columns.stop - columns.start
            to = out_hbm.at[0, part, pl.ds(pl.multiple_of(place * size, size), size)]
            copies.append(pltpu.make_async_copy(out_ref.at[step, :, columns], to, sems.at[len(copies)]))
            copies[-1].start()
    for copy in copies:
        copy.wait()


def params(vmem=VMEM_BYTES):
    return pltpu.CompilerParams(vmem_limit_bytes=vmem)


def cost(flops, bytes_accessed, transcendentals=0):
    return pl.CostEstimate(flops=int(flops), bytes_accessed=int(bytes_accessed), transcendentals=int(transcendentals))


def whole(shape):
    return pl.BlockSpec(shape, lambda *_: (0,) * len(shape))


def experts(lines, capacity, slot, weight, w_gate, w_up, plan, arrays, previous):
    units, width = w_gate.shape[1:]
    tile = max(size for size in range(16, 385, 16) if units % size == 0)
    steps = units // tile
    slots = len(lines) * capacity
    carried = [] if previous is None else [previous]
    vmem, hbm = pl.BlockSpec(memory_space=pltpu.VMEM), pl.BlockSpec(memory_space=pltpu.HBM)
    return pl.pallas_call(
        functools.partial(expert_kernel, plan, len(arrays), lines),
        in_specs=[vmem] * (4 + len(arrays)) + [hbm] * len(carried),
        out_specs=hbm,
        out_shape=jax.ShapeDtypeStruct((1, units, weight.shape[0] * capacity), F32),
        scratch_shapes=[
            pltpu.VMEM((slots, width), BF),
            pltpu.VMEM((steps, tile, slots), F32),
            pltpu.SemaphoreType.DMA((steps * len(lines),)),
        ],
        input_output_aliases={4 + len(arrays): 0} if carried else {},
        compiler_params=params(),
        cost_estimate=cost(4 * units * width * slots, 2 * slots * width),
        name="experts",
    )(slot, weight, *in_vmem(w_gate, w_up), *arrays, *carried)


def per_device(
    residual,
    queries,
    key_vecs,
    value_vecs,
    log_decay,
    head_gain,
    out_proj,
    norm_gain,
    routes,
    route_weight,
    w_gate,
    w_up,
):
    count, owners = lax.axis_size("seq"), lax.axis_size("exp")
    line = owners // 2
    me = lax.axis_index("seq")
    seqs, size, feat = queries.shape
    heads = log_decay.shape[1]
    width = feat // heads
    own, _, model = residual.shape
    unit = own * seqs
    total = size * seqs
    capacity = 8 * size // owners

    vmem, hbm, anywhere = (pl.BlockSpec(memory_space=space) for space in (pltpu.VMEM, pltpu.HBM, pl.ANY))

    states, proj = pl.pallas_call(
        state_kernel,
        in_specs=[hbm] * 4,
        out_specs=[vmem] * 2,
        out_shape=[
            pltpu.VMEM((seqs * heads * (width + 4), width), BF),
            pltpu.VMEM(out_proj.shape, BF),
        ],
        scratch_shapes=[
            pltpu.VMEM(key_vecs.shape, BF),
            pltpu.VMEM(value_vecs.shape, BF),
            pltpu.VMEM(log_decay.shape, F32),
            pltpu.SemaphoreType.DMA((2 + 2 * seqs,)),
        ],
        compiler_params=params(),
        cost_estimate=cost(4 * total * feat * width, 6 * total * feat),
        name="states",
    )(*in_hbm(key_vecs, value_vecs, log_decay, out_proj))
    arrived = [swap(states, "seq", d) for d in range(1, count)]

    inner, query, residual_rows, grown, order = pl.pallas_call(
        functools.partial(inner_kernel, line),
        in_specs=[hbm] * 5 + [anywhere],
        out_specs=[vmem] * 5,
        out_shape=[
            pltpu.VMEM((seqs, size, feat), F32),
            pltpu.VMEM(queries.shape, BF),
            pltpu.VMEM((unit, model), F32),
            pltpu.VMEM((seqs, size, heads), F32),
            pltpu.VMEM((total, total), BF),
        ],
        scratch_shapes=[
            pltpu.VMEM(key_vecs.shape, BF),
            pltpu.VMEM(value_vecs.shape, BF),
            pltpu.VMEM(log_decay.shape, F32),
            pltpu.VMEM(residual.shape, BF),
            pltpu.SemaphoreType.DMA((5,)),
        ],
        compiler_params=params(),
        cost_estimate=cost(6 * total * feat * size, 10 * total * feat),
        name="inner",
    )(*in_hbm(queries, key_vecs, value_vecs, log_decay, residual), *in_vmem(states))

    mine, theirs = pl.pallas_call(
        functools.partial(attend_kernel, count),
        in_specs=[vmem] * (5 + count - 1),
        out_specs=[vmem] * 2,
        out_shape=[jax.ShapeDtypeStruct((total // 2, feat), BF)] * 2,
        compiler_params=params(),
        cost_estimate=cost(6 * total * feat * width, 10 * total * feat),
        name="attend",
    )(*in_vmem(query, inner, grown, order), head_gain.reshape(1, feat), *arrived)

    keep, *sends = pl.pallas_call(
        project_kernel,
        in_specs=[vmem] * 4,
        out_specs=[vmem] * line,
        out_shape=[jax.ShapeDtypeStruct((unit, model), F32)]
        + [jax.ShapeDtypeStruct((unit, model), BF)] * (line - 1),
        compiler_params=params(),
        cost_estimate=cost(2 * total * feat * model, 4 * feat * model + 3 * total * model),
        name="project",
    )(mine, swap(theirs, "exp", 1), *in_vmem(proj), swap(proj, "exp", 1))
    got = [swap(send, "exp", 2 * d) for d, send in enumerate(sends, start=1)]

    routes, route_weight, keep = lax.optimization_barrier((routes, route_weight, keep))
    tables = [jax.ShapeDtypeStruct((count, total), jnp.int32), jax.ShapeDtypeStruct((count, total), F32)]
    if capacity % 128 == 0:
        tables = [
            jax.ShapeDtypeStruct((count * capacity, total), BF),
            jax.ShapeDtypeStruct((count, capacity), F32),
        ]
    slot, weight = pl.pallas_call(
        functools.partial(route_kernel, own),
        out_shape=tables,
        scratch_shapes=[pltpu.VMEM((count, total), jnp.int32), pltpu.VMEM((count, total), F32)],
        compiler_params=params(),
        cost_estimate=cost(10 * count * total * total, 16 * count * total),
        name="route",
    )(jnp.transpose(routes, (1, 2, 0)), jnp.transpose(route_weight, (1, 2, 0)))

    keep, slot, weight = lax.optimization_barrier((keep, slot, weight))
    gate, up = pl.pallas_call(
        load_kernel,
        in_specs=[hbm, hbm, anywhere],
        out_specs=[vmem] * 2,
        out_shape=[pltpu.VMEM(w_gate.shape, BF), pltpu.VMEM(w_up.shape, BF)],
        scratch_shapes=[pltpu.SemaphoreType.DMA((2, max(n for n in (4, 2, 1) if w_gate.shape[1] % (16 * n) == 0)))],
        compiler_params=params(VMEM_BYTES // 8),
        cost_estimate=cost(1, 4 * w_gate.size),
        name="load",
    )(*in_hbm(w_gate, w_up), keep)
    mixed, normed = pl.pallas_call(
        mix_kernel,
        in_specs=[vmem] * 3 + [anywhere] + [vmem] * (line - 1),
        out_shape=[jax.ShapeDtypeStruct((unit, model), F32), jax.ShapeDtypeStruct((unit, model), BF)],
        compiler_params=params(),
        cost_estimate=cost(10 * unit * model, 16 * unit * model),
        name="mix",
    )(keep, residual_rows, norm_gain.reshape(1, model), *in_vmem(gate), *got[1:2], *got[:1], *got[2:])
    attn_out = pl.pallas_call(
        place_kernel,
        out_shape=jax.ShapeDtypeStruct((own, seqs, model), F32),
        compiler_params=params(VMEM_BYTES // 8),
        cost_estimate=cost(1, 8 * unit * model),
        name="place",
    )(mixed)

    along = [swap(normed, "exp", 2 * d) for d in range(1, line)]
    across = [normed] + [swap(normed, "seq", d) for d in range(1, count)]
    arrays = along[:1] + across[1:] + along[1:] + [normed]

    def parts_of(some, first=0):
        return [(next(n for n, a in enumerate(arrays) if a is one), first, unit - first) for one in some]

    plans = [parts_of(across), parts_of(along)]
    head = unit // 2
    square = count == 4 and unit % 32 == 0 and line > 2
    if square:
        plans.append(parts_of(along[:1], head) + parts_of(along[1:]))
        plans.append([(n, 0, head) for n, *_ in parts_of(across[1:3])] + parts_of(across[3:]))
    rows = [sum(height for _, _, height in plan) for plan in plans]
    near, rest, *going = pl.pallas_call(
        functools.partial(gather_kernel, plans),
        in_specs=[vmem] * len(arrays) + [anywhere],
        out_specs=[vmem] * len(plans),
        out_shape=[jax.ShapeDtypeStruct((n, model), BF) for n in rows],
        compiler_params=params(VMEM_BYTES // 8),
        cost_estimate=cost(1, 4 * sum(rows) * model),
        name="gather",
    )(*arrays, *in_hbm(attn_out))
    def computed(lines, blocks, previous):
        plan, arrays = [], []
        for n, pieces in zip(lines, blocks):
            plan.append([])
            for partner in (False, True):
                for piece, first, height in [(near, n * unit, unit)] + pieces:
                    number = next((m for m, one in enumerate(arrays) if one is piece), len(arrays))
                    if number == len(arrays):
                        arrays.append(piece)
                    plan[-1].append((2 * number + partner, first, height))
        for piece in arrays:
            if not any(one is piece for one, _ in swapped):
                swapped.append((piece, swap(piece, "exp", 1)))
        both = [pair for piece in arrays for pair in next(pair for pair in swapped if pair[0] is piece)]
        return experts(lines, capacity, slot, weight, gate, up, plan, both, previous)

    half = count // 2
    swapped = []
    blocks = [[(rest, 0, rest.shape[0])]]
    if square:
        blocks += exchanged(*going, unit, *in_vmem(gate))
    else:
        blocks += [[(swap(rest, "seq", d), 0, rest.shape[0])] for d in range(1, count)]
    hidden = computed(range(half), blocks[:half], None)
    *last, hidden = lax.optimization_barrier((*(piece for piece, *_ in blocks[-1][-2:]), hidden))
    blocks[-1][-2:] = [(piece, *place) for piece, (_, *place) in zip(last, blocks[-1][-2:])]
    hidden = computed(range(half, count), blocks[half:], hidden)
    return (attn_out, hidden)


def solution(mesh):
    placed = (
        P(("seq", "exp"), None, None),
        P(None, "seq", "exp"),
        P(None, "seq", "exp"),
        P(None, "seq", "exp"),
        P(None, "exp", "seq"),
        P("exp"),
        P("exp", None),
        P(),
        P(),
        P(),
        P("exp", "seq", None),
        P("exp", "seq", None),
    )
    return jax.shard_map(
        per_device,
        mesh=mesh,
        in_specs=placed,
        out_specs=(P(("seq", "exp"), None, None), P("exp", "seq", None)),
        check_vma=False,
    )
```

```python
import functools

import jax
import jax.numpy as jnp
from jax import lax
from jax.experimental import pallas as pl
from jax.experimental.pallas import tpu as pltpu
from jax.sharding import PartitionSpec as P

BF, F32 = jnp.bfloat16, jnp.float32
PRECISE = lax.Precision.HIGHEST
VMEM_BYTES = 16 * 1024 * 1024
NT = (((1,), (1,)), ((), ()))
TN = (((0,), (0,)), ((), ()))


def in_hbm(*arrays):
    return [pltpu.with_memory_space_constraint(array, pltpu.HBM) for array in arrays]


def in_vmem(*arrays):
    return [pltpu.with_memory_space_constraint(array, pltpu.VMEM) for array in arrays]


def swap(block, axis, distance, forward_only=False):
    devices = range(lax.axis_size(axis))
    route = [(i, i ^ distance) for i in devices if not forward_only or i < i ^ distance]
    return lax.ppermute(block, axis, route)


def mm(a, b, dims=(((1,), (0,)), ((), ()))):
    return lax.dot_general(a, b, dims, preferred_element_type=F32)


def halves(x):
    high = x.astype(BF)
    return high, (x - high.astype(F32)).astype(BF)


def thirds(x):
    high, rest = x.astype(BF), None
    rest = x - high.astype(F32)
    middle = rest.astype(BF)
    return high, middle, (rest - middle.astype(F32)).astype(BF)


def lower_triangle(size):
    return (
        lax.broadcasted_iota(jnp.int32, (size, size), 0) >= lax.broadcasted_iota(jnp.int32, (size, size), 1)
    )


def running_columns(log_decay):
    tri = lower_triangle(log_decay.shape[1]).astype(F32)
    return lax.dot_general(tri, log_decay, NT, precision=PRECISE, preferred_element_type=F32)


def running_rows(log_decay):
    tri = lower_triangle(log_decay.shape[1]).astype(F32)
    return lax.dot_general(log_decay, tri, NT, precision=PRECISE, preferred_element_type=F32)


def state_kernel(k_hbm, v_hbm, decay_hbm, proj_hbm, out_ref, proj_ref, k_ref, v_ref, decay_ref, sems):
    seqs, heads, size = decay_ref.shape
    width = k_ref.shape[2] // heads
    pairs = [(decay_hbm, decay_ref)]
    for b in range(seqs):
        pairs += [(k_hbm.at[b], k_ref.at[b]), (v_hbm.at[b], v_ref.at[b])]
    pairs.append((proj_hbm, proj_ref))
    copies = [pltpu.make_async_copy(source, to, sems.at[n]) for n, (source, to) in enumerate(pairs)]
    for copy in copies:
        copy.start()
    copies[0].wait()
    totals, tails = [], []
    for b in range(seqs):
        columns = running_columns(decay_ref[b])
        tails.append(jnp.exp(columns[size - 1 : size, :] - columns))
        totals.append(jnp.broadcast_to(jnp.sum(decay_ref[b], axis=1, keepdims=True), (heads, width)))
    for b, tail in enumerate(tails):
        copies[1 + 2 * b].wait()
        copies[2 + 2 * b].wait()
        for h in range(heads):
            part = slice(h * width, (h + 1) * width)
            value = v_ref[b, :, part]
            high, low = halves(k_ref[b, :, part].astype(F32) * tail[:, h : h + 1])
            at = (b * heads + h) * width
            out_ref[at : at + width, :] = (mm(high, value, TN) + mm(low, value, TN)).astype(BF)
    total = jnp.concatenate(totals, axis=0)
    pieces = [piece.astype(F32) for piece in thirds(total)]
    pieces.append(jnp.zeros_like(total))
    out_ref[seqs * heads * width :, :] = jnp.concatenate(pieces, axis=0).astype(BF)
    copies[-1].wait()


def inner_kernel(line, q_hbm, k_hbm, v_hbm, decay_hbm, residual_hbm, after, *refs):
    out_ref, q_ref, rows_ref, grown_ref, order_ref = refs[:5]
    scratch = refs[5:]
    k_ref, v_ref, decay_ref, residual_ref, sems = scratch
    pairs = (
        (decay_hbm, decay_ref),
        (q_hbm, q_ref),
        (k_hbm, k_ref),
        (v_hbm, v_ref),
        (residual_hbm, residual_ref),
    )
    copies = [pltpu.make_async_copy(source, to, sems.at[n]) for n, (source, to) in enumerate(pairs)]
    for copy in copies:
        copy.start()
    own, seqs, _ = residual_ref.shape
    index = lax.axis_index("exp")
    total = order_ref.shape[0]
    to = lax.broadcasted_iota(jnp.int32, (total, total), 0)
    source = source_position(to // (total // 2), (to // (seqs * own)) % line, to % own, index, own)
    source = source + (total // seqs) * ((to // own) % seqs)
    order_ref[...] = (source == lax.broadcasted_iota(jnp.int32, (total, total), 1)).astype(BF)
    for copy in copies:
        copy.wait()
    for b in range(seqs):
        rows_ref[b * own : (b + 1) * own, :] = residual_ref[:, b, :].astype(F32)
    _, heads, size = decay_ref.shape
    width = k_ref.shape[2] // heads
    causal = lower_triangle(size)
    for b in range(seqs):
        columns = running_columns(decay_ref[b])
        rows = running_rows(decay_ref[b])
        grown_ref[b] = jnp.exp(columns)
        for h in range(heads):
            part = slice(h * width, (h + 1) * width)
            spread = columns[:, h : h + 1] - rows[h : h + 1, :]
            decay = jnp.where(causal, jnp.exp(jnp.where(causal, spread, 0.0)), 0.0)
            scores = mm(q_ref[b, :, part], k_ref[b, :, part], NT) * decay
            high, low = halves(scores)
            value = v_ref[b, :, part]
            out_ref[b, :, part] = mm(high, value) + mm(low, value)


def attend_kernel(count, *refs):
    q_ref, inner_ref, grown_ref, order_ref, gain_ref = refs[:5]
    states = refs[5 : 4 + count]
    own_ref, partner_ref = refs[4 + count :]
    seqs, size, feat = q_ref.shape
    heads = grown_ref.shape[2]
    width = feat // heads
    me = lax.axis_index("seq")
    each = seqs * heads
    base = each * width
    totals = []
    for state in states:
        three = state[base : base + 4 * each, :].astype(F32)
        totals.append(three[:each] + three[each : 2 * each] + three[2 * each : 3 * each])
    factors = []
    for first in range(1, count):
        later = jnp.zeros_like(totals[0])
        for second in range(1, count):
            between = ((me ^ first) < (me ^ second)) & ((me ^ second) < me)
            later = later + jnp.where(between, totals[second - 1], 0.0)
        factors.append(jnp.where((me ^ first) < me, jnp.exp(later), 0.0))
    rows = []
    for b in range(seqs):
        grown = grown_ref[b]
        parts = []
        for h in range(heads):
            part = slice(h * width, (h + 1) * width)
            n = b * heads + h
            incoming = jnp.zeros((width, width), F32)
            for state, factor in zip(states, factors):
                incoming = incoming + factor[n : n + 1, :] * state[n * width : (n + 1) * width, :].astype(F32)
            high, low = halves(incoming)
            query = q_ref[b, :, part]
            raw = inner_ref[b, :, part] + grown[:, h : h + 1] * (mm(query, high) + mm(query, low))
            meansq = jnp.mean(raw * raw, axis=-1, keepdims=True)
            parts.append((raw * lax.rsqrt(meansq + 1e-06) * gain_ref[:, part]).astype(BF))
        rows.append(jnp.concatenate(parts, axis=1))
    attention = jnp.concatenate(rows, axis=0)
    total = seqs * size
    attention = mm(order_ref[...], attention).astype(BF)
    own_ref[...] = attention[: total // 2, :]
    partner_ref[...] = attention[total // 2 :, :]


def project_kernel(own_ref, partner_ref, proj_ref, partner_proj_ref, keep_ref, *send_refs):
    rows, model = keep_ref.shape
    tile = column_tile(model)
    for n in range(model // tile):
        columns = slice(n * tile, (n + 1) * tile)
        product = mm(own_ref[...], proj_ref[:, columns]) + mm(partner_ref[...], partner_proj_ref[:, columns])
        keep_ref[:, columns] = product[:rows, :]
        for d, send_ref in enumerate(send_refs, start=1):
            send_ref[:, columns] = product[d * rows : (d + 1) * rows, :].astype(BF)


def column_tile(model):
    return max(t for t in range(128, 1025, 128) if model % t == 0)


def source_position(flip, distance, place, index, own):
    return own * (2 * ((index // 2) ^ distance) + ((index % 2) ^ flip)) + place


def mix_kernel(kept_ref, residual_ref, gain_ref, after, *refs):
    mixed_ref, normed_ref = refs[-2:]
    mixed = residual_ref[...] + kept_ref[...]
    for got_ref in refs[:-2]:
        mixed = mixed + got_ref[...].astype(F32)
    mixed_ref[...] = mixed
    meansq = jnp.mean(mixed * mixed, axis=-1, keepdims=True)
    normed_ref[...] = (mixed * lax.rsqrt(meansq + 1e-06) * gain_ref[...]).astype(BF)


def place_kernel(mixed_ref, out_ref):
    own, seqs, _ = out_ref.shape
    for b in range(seqs):
        out_ref[:, b, :] = mixed_ref[b * own : (b + 1) * own, :]


def load_kernel(gate_hbm, up_hbm, after, gate_ref, up_ref, sems):
    parts = sems.shape[1]
    rows = gate_ref.shape[1] // parts
    copies = []
    for m, (source, to) in enumerate(((gate_hbm, gate_ref), (up_hbm, up_ref))):
        for n in range(parts):
            part = pl.ds(n * rows, rows)
            copies.append(pltpu.make_async_copy(source.at[0, part], to.at[0, part], sems.at[m, n]))
            copies[-1].start()
    for copy in copies:
        copy.wait()


def gather_kernel(plans, *refs):
    for to, plan in zip(refs[-len(plans) :], plans):
        at = 0
        for number, first, height in plan:
            to[at : at + height, :] = refs[number][first : first + height, :]
            at += height


def halves_kernel(one_ref, two_ref, corner_ref, after, low_ref, high_ref):
    half = low_ref.shape[0]
    first = one_ref.shape[0] - 2 * half
    low_ref[...] = one_ref[first : first + half, :]
    high_ref[...] = two_ref[first + half :, :]


def exchanged(block, corner, unit, after):
    rows, head = block.shape[0], unit // 2
    half = (rows - head) // 2
    one, two = swap(block, "seq", 1), swap(block, "seq", 2)
    corner = swap(corner, "exp", 2)
    vmem, anywhere = pl.BlockSpec(memory_space=pltpu.VMEM), pl.BlockSpec(memory_space=pl.ANY)
    low, high = pl.pallas_call(
        halves_kernel,
        in_specs=[vmem] * 3 + [anywhere],
        out_specs=[vmem] * 2,
        out_shape=[jax.ShapeDtypeStruct((half, block.shape[1]), block.dtype)] * 2,
        compiler_params=params(VMEM_BYTES // 8),
        cost_estimate=cost(1, 4 * block.size),
        name="halves",
    )(one, two, corner, after)
    one, two, low, high = lax.optimization_barrier((one, two, low, high))
    far = [(swap(low, "seq", 2), 0, half), (swap(high, "seq", 1), 0, half)]
    return [
        [(corner, 0, head), (one, 0, rows)],
        [(corner, head, head), (two, 0, rows)],
        [(corner, 2 * head, unit)] + far,
    ]


def route_kernel(own, routes_ref, weights_ref, slot_ref, weight_ref, a_ref, b_ref):
    seqs, tops, _ = routes_ref.shape
    count, total = a_ref.shape
    size = total // seqs
    me = lax.axis_index("seq")
    index = lax.axis_index("exp")
    line = size // (2 * own)
    lines, shares = [], []
    for c in range(count):
        part = slice(c * size, (c + 1) * size)
        hit, share = [], []
        for b in range(seqs):
            hits = [routes_ref[b, k : k + 1, part] == index for k in range(tops)]
            hit.append(sum(jnp.where(one, 1.0, 0.0) for one in hits))
            share.append(sum(jnp.where(one, weights_ref[b, k : k + 1, part], 0.0) for k, one in enumerate(hits)))
        lines.append(jnp.concatenate(hit, axis=1))
        shares.append(jnp.concatenate(share, axis=1))
    chosen = jnp.concatenate(lines, axis=0).astype(BF)
    weight = jnp.concatenate(shares, axis=0)
    to = lax.broadcasted_iota(jnp.int32, (total, total), 1)
    row = source_position(to // (total // 2), (to // (seqs * own)) % line, to % own, index, own) * seqs
    row = row + (to // own) % seqs
    origin = lax.broadcasted_iota(jnp.int32, (total, total), 0)
    origin = (origin % size) * seqs + origin // size
    rank = mm(chosen, (origin <= row).astype(BF)) - 1.0
    same = (origin == row).astype(BF)
    picked = mm(chosen, same) > 0.5
    a_ref[...] = jnp.where(picked, rank.astype(jnp.int32), -1)
    high, middle, low = thirds(weight)
    b_ref[...] = mm(high, same) + mm(middle, same) + mm(low, same)
    capacity = weight_ref.shape[1]
    numbers = lax.broadcasted_iota(jnp.int32, (capacity, total), 0)
    for d in range(count):
        slot, weight = a_ref[pl.ds(me ^ d, 1), :], b_ref[pl.ds(me ^ d, 1), :]
        if slot_ref.shape[0] == count:
            slot_ref[d : d + 1, :] = slot
            weight_ref[d : d + 1, :] = weight
            continue
        pick = (slot == numbers).astype(BF)
        slot_ref[d * capacity : (d + 1) * capacity, :] = pick
        weight_ref[d : d + 1, :] = weighed([weight], pick)


def weighed(weights, pick):
    weight = jnp.concatenate(weights, axis=1)
    parts = [part.astype(F32) for part in thirds(weight)] + [jnp.zeros((5, weight.shape[1]), F32)]
    return jnp.sum(mm(jnp.concatenate(parts, axis=0).astype(BF), pick, NT), axis=0, keepdims=True)


def expert_kernel(plan, arrays, lines, slot_ref, weight_ref, gate_ref, up_ref, *refs):
    array_refs, (out_hbm, rows_ref, out_ref, sems) = refs[:arrays], refs[-4:]
    total = slot_ref.shape[1]
    blocks = len(lines)
    slots, width = rows_ref.shape
    me = lax.axis_index("seq")
    tile = out_ref.shape[1]
    capacity = slots // blocks
    apart = capacity % 128 == 0
    picks = []
    if apart:
        picks = [slot_ref[line * capacity : (line + 1) * capacity, :] for line in lines]
        scale = jnp.concatenate([weight_ref[line : line + 1, :] for line in lines], axis=1)
    else:
        numbers = lax.broadcasted_iota(jnp.int32, (slots, total), 0)
        for line in lines:
            slot = slot_ref[line : line + 1, :]
            place = (me ^ line) % blocks
            picks.append((jnp.where(slot < 0, slot, slot + place * capacity) == numbers).astype(BF))
        scale = weighed([weight_ref[line : line + 1, :] for line in lines], jnp.concatenate(picks, axis=1))

    step = column_tile(width)
    for at in range(0, width, step):
        part = slice(at, at + step)
        rows = []
        for pieces in plan:
            rows.append([array_refs[m][first : first + height, part] for m, first, height in pieces])
        if apart:
            for n, pick in enumerate(picks):
                own = slice(n * capacity, (n + 1) * capacity)
                rows_ref[own, part] = mm(pick, jnp.concatenate(rows[n], axis=0)).astype(BF)
        else:
            rows = jnp.concatenate([piece for pieces in rows for piece in pieces], axis=0)
            rows_ref[:, part] = mm(jnp.concatenate(picks, axis=1), rows).astype(BF)

    targets = [(slice(0, slots), (me ^ lines[0]) // blocks)]
    if apart:
        targets = [(slice(n * capacity, (n + 1) * capacity), me ^ line) for n, line in enumerate(lines)]
    copies = []
    for step in range(out_ref.shape[0]):
        part = slice(step * tile, (step + 1) * tile)
        gate = mm(gate_ref[0, part, :], rows_ref[...], NT)
        up = mm(up_ref[0, part, :], rows_ref[...], NT)
        out_ref[step] = scale * (gate / (1.0 + jnp.exp(-gate))) * up
        for columns, place in targets:
            size = columns.stop - columns.start
            to = out_hbm.at[0, part, pl.ds(pl.multiple_of(place * size, size), size)]
            copies.append(pltpu.make_async_copy(out_ref.at[step, :, columns], to, sems.at[len(copies)]))
            copies[-1].start()
    for copy in copies:
        copy.wait()


def params(vmem=VMEM_BYTES):
    return pltpu.CompilerParams(vmem_limit_bytes=vmem)


def cost(flops, bytes_accessed, transcendentals=0):
    return pl.CostEstimate(flops=int(flops), bytes_accessed=int(bytes_accessed), transcendentals=int(transcendentals))


def whole(shape):
    return pl.BlockSpec(shape, lambda *_: (0,) * len(shape))


def experts(lines, capacity, slot, weight, w_gate, w_up, plan, arrays, previous):
    units, width = w_gate.shape[1:]
    tile = max(size for size in range(16, 385, 16) if units % size == 0)
    steps = units // tile
    slots = len(lines) * capacity
    carried = [] if previous is None else [previous]
    vmem, hbm = pl.BlockSpec(memory_space=pltpu.VMEM), pl.BlockSpec(memory_space=pltpu.HBM)
    return pl.pallas_call(
        functools.partial(expert_kernel, plan, len(arrays), lines),
        in_specs=[vmem] * (4 + len(arrays)) + [hbm] * len(carried),
        out_specs=hbm,
        out_shape=jax.ShapeDtypeStruct((1, units, weight.shape[0] * capacity), F32),
        scratch_shapes=[
            pltpu.VMEM((slots, width), BF),
            pltpu.VMEM((steps, tile, slots), F32),
            pltpu.SemaphoreType.DMA((steps * len(lines),)),
        ],
        input_output_aliases={4 + len(arrays): 0} if carried else {},
        compiler_params=params(),
        cost_estimate=cost(4 * units * width * slots, 2 * slots * width),
        name="experts",
    )(slot, weight, *in_vmem(w_gate, w_up), *arrays, *carried)


def per_device(
    residual,
    queries,
    key_vecs,
    value_vecs,
    log_decay,
    head_gain,
    out_proj,
    norm_gain,
    routes,
    route_weight,
    w_gate,
    w_up,
):
    count, owners = lax.axis_size("seq"), lax.axis_size("exp")
    line = owners // 2
    me = lax.axis_index("seq")
    seqs, size, feat = queries.shape
    heads = log_decay.shape[1]
    width = feat // heads
    own, _, model = residual.shape
    unit = own * seqs
    total = size * seqs
    capacity = 8 * size // owners

    vmem, hbm, anywhere = (pl.BlockSpec(memory_space=space) for space in (pltpu.VMEM, pltpu.HBM, pl.ANY))

    states, proj = pl.pallas_call(
        state_kernel,
        in_specs=[hbm] * 4,
        out_specs=[vmem] * 2,
        out_shape=[
            pltpu.VMEM((seqs * heads * (width + 4), width), BF),
            pltpu.VMEM(out_proj.shape, BF),
        ],
        scratch_shapes=[
            pltpu.VMEM(key_vecs.shape, BF),
            pltpu.VMEM(value_vecs.shape, BF),
            pltpu.VMEM(log_decay.shape, F32),
            pltpu.SemaphoreType.DMA((2 + 2 * seqs,)),
        ],
        compiler_params=params(),
        cost_estimate=cost(4 * total * feat * width, 6 * total * feat),
        name="states",
    )(*in_hbm(key_vecs, value_vecs, log_decay, out_proj))
    arrived = [swap(states, "seq", d) for d in range(1, count)]

    inner, query, residual_rows, grown, order = pl.pallas_call(
        functools.partial(inner_kernel, line),
        in_specs=[hbm] * 5 + [anywhere],
        out_specs=[vmem] * 5,
        out_shape=[
            pltpu.VMEM((seqs, size, feat), F32),
            pltpu.VMEM(queries.shape, BF),
            pltpu.VMEM((unit, model), F32),
            pltpu.VMEM((seqs, size, heads), F32),
            pltpu.VMEM((total, total), BF),
        ],
        scratch_shapes=[
            pltpu.VMEM(key_vecs.shape, BF),
            pltpu.VMEM(value_vecs.shape, BF),
            pltpu.VMEM(log_decay.shape, F32),
            pltpu.VMEM(residual.shape, BF),
            pltpu.SemaphoreType.DMA((5,)),
        ],
        compiler_params=params(),
        cost_estimate=cost(6 * total * feat * size, 10 * total * feat),
        name="inner",
    )(*in_hbm(queries, key_vecs, value_vecs, log_decay, residual), *in_vmem(states))

    mine, theirs = pl.pallas_call(
        functools.partial(attend_kernel, count),
        in_specs=[vmem] * (5 + count - 1),
        out_specs=[vmem] * 2,
        out_shape=[jax.ShapeDtypeStruct((total // 2, feat), BF)] * 2,
        compiler_params=params(),
        cost_estimate=cost(6 * total * feat * width, 10 * total * feat),
        name="attend",
    )(*in_vmem(query, inner, grown, order), head_gain.reshape(1, feat), *arrived)

    keep, *sends = pl.pallas_call(
        project_kernel,
        in_specs=[vmem] * 4,
        out_specs=[vmem] * line,
        out_shape=[jax.ShapeDtypeStruct((unit, model), F32)]
        + [jax.ShapeDtypeStruct((unit, model), BF)] * (line - 1),
        compiler_params=params(),
        cost_estimate=cost(2 * total * feat * model, 4 * feat * model + 3 * total * model),
        name="project",
    )(mine, swap(theirs, "exp", 1), *in_vmem(proj), swap(proj, "exp", 1))
    got = [swap(send, "exp", 2 * d) for d, send in enumerate(sends, start=1)]

    routes, route_weight, keep = lax.optimization_barrier((routes, route_weight, keep))
    tables = [jax.ShapeDtypeStruct((count, total), jnp.int32), jax.ShapeDtypeStruct((count, total), F32)]
    if capacity % 128 == 0:
        tables = [
            jax.ShapeDtypeStruct((count * capacity, total), BF),
            jax.ShapeDtypeStruct((count, capacity), F32),
        ]
    slot, weight = pl.pallas_call(
        functools.partial(route_kernel, own),
        out_shape=tables,
        scratch_shapes=[pltpu.VMEM((count, total), jnp.int32), pltpu.VMEM((count, total), F32)],
        compiler_params=params(),
        cost_estimate=cost(10 * count * total * total, 16 * count * total),
        name="route",
    )(jnp.transpose(routes, (1, 2, 0)), jnp.transpose(route_weight, (1, 2, 0)))

    keep, slot, weight = lax.optimization_barrier((keep, slot, weight))
    gate, up = pl.pallas_call(
        load_kernel,
        in_specs=[hbm, hbm, anywhere],
        out_specs=[vmem] * 2,
        out_shape=[pltpu.VMEM(w_gate.shape, BF), pltpu.VMEM(w_up.shape, BF)],
        scratch_shapes=[pltpu.SemaphoreType.DMA((2, max(n for n in (4, 2, 1) if w_gate.shape[1] % (16 * n) == 0)))],
        compiler_params=params(VMEM_BYTES // 8),
        cost_estimate=cost(1, 4 * w_gate.size),
        name="load",
    )(*in_hbm(w_gate, w_up), keep)
    mixed, normed = pl.pallas_call(
        mix_kernel,
        in_specs=[vmem] * 3 + [anywhere] + [vmem] * (line - 1),
        out_shape=[jax.ShapeDtypeStruct((unit, model), F32), jax.ShapeDtypeStruct((unit, model), BF)],
        compiler_params=params(),
        cost_estimate=cost(10 * unit * model, 16 * unit * model),
        name="mix",
    )(keep, residual_rows, norm_gain.reshape(1, model), *in_vmem(gate), *got[1:2], *got[:1], *got[2:])
    attn_out = pl.pallas_call(
        place_kernel,
        out_shape=jax.ShapeDtypeStruct((own, seqs, model), F32),
        compiler_params=params(VMEM_BYTES // 8),
        cost_estimate=cost(1, 8 * unit * model),
        name="place",
    )(mixed)

    along = [swap(normed, "exp", 2 * d) for d in range(1, line)]
    across = [normed] + [swap(normed, "seq", d) for d in range(1, count)]
    arrays = along[:1] + across[1:] + along[1:] + [normed]

    def parts_of(some, first=0):
        return [(next(n for n, a in enumerate(arrays) if a is one), first, unit - first) for one in some]

    plans = [parts_of(across), parts_of(along)]
    head = unit // 2
    square = count == 4 and unit % 32 == 0 and line > 2
    if square:
        plans.append(parts_of(along[:1], head) + parts_of(along[1:]))
        plans.append([(n, 0, head) for n, *_ in parts_of(across[1:3])] + parts_of(across[3:]))
    rows = [sum(height for _, _, height in plan) for plan in plans]
    near, rest, *going = pl.pallas_call(
        functools.partial(gather_kernel, plans),
        in_specs=[vmem] * len(arrays) + [anywhere],
        out_specs=[vmem] * len(plans),
        out_shape=[jax.ShapeDtypeStruct((n, model), BF) for n in rows],
        compiler_params=params(VMEM_BYTES // 8),
        cost_estimate=cost(1, 4 * sum(rows) * model),
        name="gather",
    )(*arrays, *in_hbm(attn_out))
    def computed(lines, blocks, previous):
        plan, arrays = [], []
        for n, pieces in zip(lines, blocks):
            plan.append([])
            for partner in (False, True):
                for piece, first, height in [(near, n * unit, unit)] + pieces:
                    number = next((m for m, one in enumerate(arrays) if one is piece), len(arrays))
                    if number == len(arrays):
                        arrays.append(piece)
                    plan[-1].append((2 * number + partner, first, height))
        for piece in arrays:
            if not any(one is piece for one, _ in swapped):
                swapped.append((piece, swap(piece, "exp", 1)))
        both = [pair for piece in arrays for pair in next(pair for pair in swapped if pair[0] is piece)]
        return experts(lines, capacity, slot, weight, gate, up, plan, both, previous)

    half = count // 2
    swapped = []
    blocks = [[(rest, 0, rest.shape[0])]]
    if square:
        blocks += exchanged(*going, unit, *in_vmem(gate))
    else:
        blocks += [[(swap(rest, "seq", d), 0, rest.shape[0])] for d in range(1, count)]
    hidden = computed(range(half), blocks[:half], None)
    *last, hidden = lax.optimization_barrier((*(piece for piece, *_ in blocks[-1][-2:]), hidden))
    if square:
        height = last[0].shape[0]
        joined = pl.pallas_call(
            functools.partial(gather_kernel, [[(0, 0, height), (1, 0, height)]]),
            in_specs=[vmem] * 2,
            out_specs=vmem,
            out_shape=jax.ShapeDtypeStruct((2 * height, model), BF),
            compiler_params=params(VMEM_BYTES // 8),
            cost_estimate=cost(1, 8 * height * model),
            name="join",
        )(*last)
        blocks[-1][-2:] = [(joined, 0, 2 * height)]
    else:
        blocks[-1][-2:] = [(piece, *place) for piece, (_, *place) in zip(last, blocks[-1][-2:])]
    hidden = computed(range(half, count), blocks[half:], hidden)
    return (attn_out, hidden)


def solution(mesh):
    placed = (
        P(("seq", "exp"), None, None),
        P(None, "seq", "exp"),
        P(None, "seq", "exp"),
        P(None, "seq", "exp"),
        P(None, "exp", "seq"),
        P("exp"),
        P("exp", None),
        P(),
        P(),
        P(),
        P("exp", "seq", None),
        P("exp", "seq", None),
    )
    return jax.shard_map(
        per_device,
        mesh=mesh,
        in_specs=placed,
        out_specs=(P(("seq", "exp"), None, None), P("exp", "seq", None)),
        check_vma=False,
    )
```
